512 devices in a mesh: gz: 64 (over x, z, core), gy: 8 (over y).
Axes of the slice: x: 4, y: 8, z: 8, core: 2. Of those that a mesh axis runs over, the one named last changes fastest.
Arguments:
- volume: bfloat16 [16, 512, 64, 128], P(None, 'gz', 'gy'), may hold values from -6 to 6
- kernel_full: bfloat16 [3, 3, 3, 16, 16], replicated, may hold values from -0.3125 to 0.3125
- kernel_half: bfloat16 [3, 3, 3, 16, 32], replicated, may hold values from -0.3125 to 0.3125
- kernel_quarter: bfloat16 [3, 3, 3, 32, 64], replicated, may hold values from -0.21875 to 0.21875
- kernel_eighth: bfloat16 [3, 3, 3, 64, 128], replicated, may hold values from -0.15625 to 0.15625
- skip_full: bfloat16 [16, 512, 64, 128], P(None, 'gz', 'gy'), may hold values from -0.03125 to 0.03125
- skip_half: bfloat16 [32, 256, 32, 64], P(None, 'gz', 'gy'), may hold values from -0.078125 to 0.078125
- skip_quarter: bfloat16 [64, 128, 16, 32], P(None, 'gz', 'gy'), may hold values from -0.25 to 0.25
- skip_eighth: bfloat16 [128, 64, 8, 16], P(None, 'gz', 'gy'), may hold values from -0.625 to 0.625
Outputs:
- grad_full: float32 [3, 3, 3, 16, 16], replicated
- grad_half: float32 [3, 3, 3, 16, 32], replicated
- grad_quarter: float32 [3, 3, 3, 32, 64], replicated
- grad_eighth: float32 [3, 3, 3, 64, 128], replicated
The draws below stay inside these ranges and needn't reach their ends.
All inputs are finite; a program needn't handle non-finite values.
Results may differ from the reference program's by a relative error of at most 0.0041.
Values may be sent and summed in bfloat16 or wider, within the bound.
No kernel may reach another device: no remote copies, remote signals or barrier semaphores. Data moves between devices by JAX's collectives and lax.ppermute only.
A program may use at most 64 MiB of HBM per device.

```python
import jax
import jax.numpy as jnp
from jax import lax

CH0 = 16
CH1 = 32
CH2 = 64
CH3 = 128
NZ = 512
NY = 64
NX = 128


def block_scale(stream_key, shape, cuts, least, high):
    def one(axis_at, shards_of):
        steps = jax.random.uniform(jax.random.fold_in(jax.random.fold_in(stream_key, 6), axis_at), (shards_of,), jnp.float32, least / len(cuts), high / len(cuts))
        return jnp.repeat(jnp.exp(steps), shape[axis_at] // shards_of).reshape((-1,) + (1,) * (len(shape) - axis_at - 1))

    level = one(*cuts[0])
    for cut in cuts[1:]:
        level = level * one(*cut)
    return level


def scatter_about(own_key, shape, spread, reach, pieces=(), kind=jnp.bfloat16):
    entries = jax.random.normal(own_key, shape, jnp.float32) * spread
    if len(pieces) > 0:
        entries = block_scale(own_key, shape, pieces, -0.22, 0.18) * entries
    return jnp.clip(entries, min=-reach, max=reach).astype(kind)


def setup_inputs(seed: int = 0) -> dict:
    key_list = jax.random.split(jax.random.key(seed), 10)
    volume = scatter_about(key_list[0], (CH0, NZ, NY, NX), 1.0, 6.0, ((1, 64), (2, 8)))
    kernel_full = scatter_about(key_list[1], (3, 3, 3, CH0, CH0), (27 * CH0) ** -0.5, 0.3125)
    kernel_half = scatter_about(key_list[2], (3, 3, 3, CH0, CH1), (27 * CH0) ** -0.5, 0.3125)
    kernel_quarter = scatter_about(key_list[3], (3, 3, 3, CH1, CH2), (27 * CH1) ** -0.5, 0.21875)
    kernel_eighth = scatter_about(key_list[4], (3, 3, 3, CH2, CH3), (27 * CH2) ** -0.5, 0.15625)
    skip_full = scatter_about(key_list[5], (CH0, NZ, NY, NX), (4.0 / (NZ * NY * NX) ** 0.5), 0.03125, ((1, 64), (2, 8)))
    skip_half = scatter_about(key_list[6], (CH1, NZ // 2, NY // 2, NX // 2), (4.0 / (NZ * NY * NX // 8) ** 0.5), 0.078125, ((1, 64), (2, 8)))
    skip_quarter = scatter_about(key_list[7], (CH2, NZ // 4, NY // 4, NX // 4), (4.0 / (NZ * NY * NX // 64) ** 0.5), 0.25, ((1, 64), (2, 8)))
    skip_eighth = scatter_about(key_list[8], (CH3, NZ // 8, NY // 8, NX // 8), (4.0 / (NZ * NY * NX // 512) ** 0.5), 0.625, ((1, 64), (2, 8)))
    return {"volume": volume, "kernel_full": kernel_full, "kernel_half": kernel_half, "kernel_quarter": kernel_quarter, "kernel_eighth": kernel_eighth, "skip_full": skip_full, "skip_half": skip_half, "skip_quarter": skip_quarter, "skip_eighth": skip_eighth}


def convolve(inputs, kernel):
    return lax.conv_general_dilated(inputs[None], kernel, (1, 1, 1), ((1, 1), (1, 1), (1, 1)), dimension_numbers=('NCDHW', 'DHWIO', 'NCDHW'), precision=lax.Precision.HIGHEST)[0]

def shrink(preact):
    chans, depth, height, width = preact.shape
    blocks = jax.nn.silu(preact).reshape(chans, depth // 2, 2, height // 2, 2, width // 2, 2)
    return lax.optimization_barrier(jnp.mean(blocks, axis=(2, 4, 6))).astype(jnp.bfloat16)

def spread_up(carried):
    chans, depth, height, width = carried.shape
    grown = jnp.broadcast_to(carried[:, :, None, :, None, :, None], (chans, depth, 2, height, 2, width, 2))
    return grown.reshape(chans, 2 * depth, 2 * height, 2 * width) * 0.125

def slope(preact):
    sig = jax.nn.sigmoid(preact)
    return sig * (1.0 + preact * (1.0 - sig))

def reference(volume, kernel_full, kernel_half, kernel_quarter, kernel_eighth, skip_full, skip_half, skip_quarter, skip_eighth):
    kernels = [kernel_full.astype(jnp.float32), kernel_half.astype(jnp.float32), kernel_quarter.astype(jnp.float32), kernel_eighth.astype(jnp.float32)]
    skips = [skip_full, skip_half, skip_quarter, skip_eighth]
    inputs = volume.astype(jnp.float32)
    saved = []
    preacts = []
    for level_index in range(4):
        preact = convolve(inputs, kernels[level_index])
        saved.append(inputs)
        preacts.append(preact)
        if level_index < 3:
            inputs = shrink(preact).astype(jnp.float32)
    grads = [None, None, None, None]
    carried = None
    for level_index in (3, 2, 1, 0):
        upstream = skips[level_index].astype(jnp.float32)
        if level_index < 3:
            upstream = upstream + spread_up(carried)
        rounded = lax.optimization_barrier((upstream * slope(preacts[level_index])).astype(jnp.bfloat16))
        gradient = rounded.astype(jnp.float32)
        if level_index > 0:
            outputs, pullback = jax.vjp(convolve, saved[level_index], kernels[level_index])
            carried, grads[level_index] = pullback(gradient)
        else:
            source = saved[0]
            outputs, pullback = jax.vjp(lambda kernel: convolve(source, kernel), kernels[0])
            grads[0] = pullback(gradient)[0]
    return (grads[0], grads[1], grads[2], grads[3])
```

```python
import jax
import jax.numpy as jnp
from jax import lax
from jax.sharding import PartitionSpec as P


def padded_2(array, sides, width):
    for axis, dim in sides:
        devices, length = (lax.axis_size(axis), array.shape[dim])
        up = [(i, (i + 1) % devices) for i in range(devices - 1)]
        down = [(j, i) for i, j in up]
        last = lax.slice_in_dim(array, length - width, length, axis=dim)
        initial = lax.slice_in_dim(array, 0, width, axis=dim)
        before = lax.ppermute(last, axis, up)
        after = lax.ppermute(initial, axis, down)
        array = jnp.concatenate([before, array, after], axis=dim)
    return array


def pad_columns(inputs):
    return jnp.pad(inputs, ((0, 0), (0, 0), (0, 0), (1, 1)))


def act_rims(inputs):
    return padded_2(pad_columns(inputs), ((("x", "z", "c"), 1), ("gy", 2)), 1)


def grad_rims(inputs):
    return padded_2(pad_columns(inputs), ((("x", "z", "c"), 1), ("gy", 2)), 1)


def convolve(padded, kernel):
    return lax.conv_general_dilated(
        padded[None],
        kernel,
        (1, 1, 1),
        "VALID",
        dimension_numbers=("NCDHW", "DHWIO", "NCDHW"),
        preferred_element_type=jnp.float32,
    )[0]


def transposed(padded_grad, kernel):
    return convolve(padded_grad, jnp.swapaxes(jnp.flip(kernel, (0, 1, 2)), 3, 4))


def weight_term(padded, gradient):
    product = lax.conv_general_dilated(
        padded[:, None],
        gradient[None],
        (1, 1, 1),
        "VALID",
        dimension_numbers=("NCDHW", "IODHW", "NCDHW"),
        preferred_element_type=jnp.float32,
    )
    return jnp.transpose(product, (2, 3, 4, 0, 1))


def shrink(preact):
    chans, depth, height, width = preact.shape
    blocks = jax.nn.silu(preact).reshape(chans, depth // 2, 2, height // 2, 2, width // 2, 2)
    return jnp.mean(blocks, axis=(2, 4, 6)).astype(jnp.bfloat16)


def spread_up(carried):
    chans, depth, height, width = carried.shape
    grown = jnp.broadcast_to(
        carried[:, :, None, :, None, :, None], (chans, depth, 2, height, 2, width, 2)
    )
    return grown.reshape(chans, 2 * depth, 2 * height, 2 * width) * 0.125


def slope(preact):
    sig = jax.nn.sigmoid(preact)
    return sig * (1.0 + preact * (1.0 - sig))


def summed(terms):
    rows = [term.reshape(-1, 128) for term in terms]
    total = sum(part.shape[0] for part in rows)
    flat = jnp.concatenate(rows + [jnp.zeros((2560 - total, 128), jnp.float32)], axis=0)
    halves = flat.reshape(2, 1280, 128)
    core = lax.axis_index("c")
    mine = lax.dynamic_index_in_dim(halves, core, 0, False)
    other = lax.dynamic_index_in_dim(halves, 1 - core, 0, False)
    swap = [(0, 1), (1, 0)]
    pair = (mine + lax.ppermute(other, "c", swap)).astype(jnp.bfloat16)
    pieces = lax.all_to_all(pair.reshape(8, 160, 128), "gy", 0, 0)
    column = jnp.sum(pieces.astype(jnp.float32), axis=0)
    pieces = lax.all_to_all(column.reshape(32, 5, 128), ("x", "z"), 0, 0)
    done = jnp.sum(pieces, axis=0).astype(jnp.bfloat16)
    spread = lax.optimization_barrier(jnp.broadcast_to(done[None], (32, 5, 128)))
    column = lax.all_to_all(spread, ("x", "z"), 0, 0).reshape(160, 128)
    spread = lax.optimization_barrier(jnp.broadcast_to(column[None], (8, 160, 128)))
    half = lax.all_to_all(spread, "gy", 0, 0).reshape(1280, 128)
    other = lax.ppermute(half, "c", swap)
    first = jnp.where(core == 0, half, other)
    second = jnp.where(core == 0, other, half)
    whole = jnp.concatenate([first, second], axis=0).astype(jnp.float32)
    outs = []
    at = 0
    for term, part in zip(terms, rows):
        count = part.shape[0]
        outs.append(whole[at : at + count].reshape(term.shape))
        at += count
    return tuple(outs)


def on_device(
    volume,
    kernel_full,
    kernel_half,
    kernel_quarter,
    kernel_eighth,
    skip_full,
    skip_half,
    skip_quarter,
    skip_eighth,
):
    kernels = [kernel_full, kernel_half, kernel_quarter, kernel_eighth]
    skips = [skip_full, skip_half, skip_quarter, skip_eighth]
    inputs = volume
    paddings = []
    preacts = []
    spread_levels = 3
    for level_index in range(spread_levels):
        padded = act_rims(inputs)
        preact = convolve(padded, kernels[level_index])
        paddings.append(padded)
        preacts.append(preact)
        inputs = shrink(preact)
    terms = [None, None, None]
    padded = act_rims(inputs)
    preact = convolve(padded, kernel_eighth)
    gradient = (skip_eighth.astype(jnp.float32) * slope(preact)).astype(jnp.bfloat16)
    deep_term = weight_term(padded, gradient)
    carried = transposed(grad_rims(gradient), kernel_eighth)
    levels_left = (2, 1, 0)
    for level_index in levels_left:
        upstream = skips[level_index].astype(jnp.float32) + spread_up(carried)
        gradient = (upstream * slope(preacts[level_index])).astype(jnp.bfloat16)
        terms[level_index] = weight_term(paddings[level_index], gradient)
        if level_index > 0:
            carried = transposed(grad_rims(gradient), kernels[level_index])
    return summed((terms[0], terms[1], terms[2], deep_term))


def solution(mesh):
    fine = jax.sharding.Mesh(mesh.devices.reshape(4, 8, 2, 8), ("x", "z", "c", "gy"))
    in_specs = (
        P(None, ("x", "z", "c"), "gy", None),
        P(),
        P(),
        P(),
        P(),
        P(None, ("x", "z", "c"), "gy", None),
        P(None, ("x", "z", "c"), "gy", None),
        P(None, ("x", "z", "c"), "gy", None),
        P(None, ("x", "z", "c"), "gy", None),
    )
    out_specs = (P(), P(), P(), P())
    return jax.shard_map(
        on_device, mesh=fine, in_specs=in_specs, out_specs=out_specs, check_vma=False
    )
```

```python
import jax
import jax.numpy as jnp
from jax import lax
from jax.experimental import pallas as pl
from jax.experimental.pallas import tpu as pltpu
from jax.sharding import PartitionSpec as P

F32 = jnp.float32
BF16 = jnp.bfloat16
GZ = ("x", "z", "c")
VMEM_BYTES = 14 * 1024 * 1024
HALF = (256, 640)
NT = (((1,), (1,)), ((), ()))


def call(body, outs, scratch, flops, *args):
    return pl.pallas_call(
        body,
        out_shape=tuple(jax.ShapeDtypeStruct(shape, dtype) for shape, dtype in outs),
        in_specs=[pl.BlockSpec(memory_space=pltpu.VMEM) for _ in args],
        out_specs=tuple(pl.BlockSpec(memory_space=pltpu.VMEM) for _ in outs),
        scratch_shapes=[pltpu.VMEM(shape, dtype) for shape, dtype in scratch],
        compiler_params=pltpu.CompilerParams(vmem_limit_bytes=VMEM_BYTES),
        cost_estimate=pl.CostEstimate(flops=flops, bytes_accessed=1 << 20, transcendentals=0),
    )(*args)


def place_of():
    depth_at, row_at = lax.axis_index(GZ), lax.axis_index("gy")
    return (
        depth_at > 0,
        depth_at < lax.axis_size(GZ) - 1,
        row_at > 0,
        row_at < lax.axis_size("gy") - 1,
        lax.axis_index("c"),
        row_at,
    )


def lanes(shape):
    return lax.broadcasted_iota(jnp.int32, shape, 1)


def at_column(tile, step):
    if step == 0:
        return tile
    moved = pltpu.roll(tile.astype(F32), (-step) % 128, 1)
    edge = 127 if step > 0 else 0
    return jnp.where(lanes(tile.shape) == edge, 0.0, moved).astype(BF16)


def put_shifts(shifts, row, layer, tile):
    for step in range(3):
        shifts[step, row : row + tile.shape[0], layer * 128 : layer * 128 + 128] = at_column(
            tile, step - 1
        )


def convolved(weights, shifts, rows, depth):
    total = None
    for down in range(3):
        for step in range(3):
            window = shifts[step, rows[0] : rows[1], down * 128 : (down + depth) * 128]
            tap = weights[down * 3 + step]
            term = jnp.dot(
                tap[:, : rows[1] - rows[0]], window, preferred_element_type=F32
            )
            total = term if total is None else total + term
    return total


def sigmoid(values):
    return 1.0 / (1.0 + jnp.exp(-values))


def slope(values):
    sig = sigmoid(values)
    return sig * (1.0 + values * (1.0 - sig))


def exact_dot(values, picks):
    high = values.astype(BF16)
    rest = values - high.astype(F32)
    middle = rest.astype(BF16)
    low = (rest - middle.astype(F32)).astype(BF16)
    total = jnp.dot(low, picks, preferred_element_type=F32)
    total = total + jnp.dot(middle, picks, preferred_element_type=F32)
    return total + jnp.dot(high, picks, preferred_element_type=F32)


def pair_columns(down):
    rows = lax.broadcasted_iota(jnp.int32, (128, 128), 0)
    columns = lax.broadcasted_iota(jnp.int32, (128, 128), 1)
    hit = (rows // 2 == columns) if down else (columns // 2 == rows)
    return jnp.where(hit, 0.125, 0.0).astype(BF16)


def pooled(first, second, channels, width):
    both = first + second
    blocks = both.shape[0] // (2 * channels)
    rows = []
    for block in range(blocks):
        start = 2 * block * channels
        rows.append(
            both[start : start + channels] + both[start + channels : start + 2 * channels]
        )
    summed = rows[0] if blocks == 1 else jnp.concatenate(rows, axis=0)
    mean = exact_dot(summed, pair_columns(True))
    return jnp.where(lanes(mean.shape) < width // 2, mean, 0.0)


def silu(values):
    return values * sigmoid(values)


def prepare(kernels, dims):
    def body(*refs):
        ins, outs, wide = refs[:4], refs[4:11], refs[11]
        for level, (rows, chans, feats) in enumerate(dims):
            source, taps = ins[level][...], outs[level]
            picks = (
                lax.broadcasted_iota(jnp.int32, (feats, 128), 0)
                == lax.broadcasted_iota(jnp.int32, (feats, 128), 1) % feats
            )
            spread = jnp.dot(
                source, jnp.where(picks, 1.0, 0.0).astype(BF16), preferred_element_type=F32
            )
            size = taps.shape[2]
            place = lanes((chans, 128)) // feats
            for down in range(3):
                for step in range(3):
                    wide[...] = jnp.zeros_like(wide)
                    for row in range(rows + 2):
                        value = jnp.zeros((chans, 128), F32)
                        for across in range(3):
                            at = ((down * 3 + across) * 3 + step) * chans
                            value = jnp.where(
                                place == row - across, spread[at : at + chans], value
                            )
                        wide[row * chans : (row + 1) * chans, :] = value
                    taps[down * 3 + step] = wide[:size, :].T.astype(BF16)
        for level in range(1, 4):
            rows, chans, feats = dims[level]
            if level == 2:
                rows = 4
            source, taps = ins[level][...], outs[3 + level]
            size = (rows + 2) * feats
            picks = (
                lax.broadcasted_iota(jnp.int32, (feats, size), 0)
                == lax.broadcasted_iota(jnp.int32, (feats, size), 1) % feats
            )
            spread = jnp.dot(
                source, jnp.where(picks, 1.0, 0.0).astype(BF16), preferred_element_type=F32
            )
            place = lanes((chans, size)) // feats
            for down in range(3):
                for step in range(3):
                    for row in range(rows):
                        value = jnp.zeros((chans, size), F32)
                        for across in range(3):
                            at = (((2 - down) * 3 + 2 - across) * 3 + 2 - step) * chans
                            value = jnp.where(
                                place == row + across, spread[at : at + chans], value
                            )
                        taps[down * 3 + step, row * chans : (row + 1) * chans, :] = (
                            value.astype(BF16)
                        )

    shapes = [(9, 128, 256), (9, 128, 128), (9, 128, 128), (9, 128, 256)]
    shapes += [(9, 64, 192), (9, 128, 384), (9, 64, 384)]
    flat = [kernel.reshape(-1, kernel.shape[-1]) for kernel in kernels]
    return call(body, [(s, BF16) for s in shapes], [((256, 128), F32)], 1 << 27, *flat)


def forward_full(volume, halo_z, halo_y, weights):
    def body(own, before, after, above, below, taps, pre, act, shifts):
        for layer in range(10):
            middle = before if layer == 0 else after if layer == 9 else own
            at = 0 if layer in (0, 9) else layer - 1
            put_shifts(shifts, 0, layer, above[layer * 16 : layer * 16 + 16])
            put_shifts(shifts, 16, layer, middle[at, :128])
            put_shifts(shifts, 144, layer, below[layer * 16 : layer * 16 + 16])
        value = convolved(taps, shifts, (0, 160), 8)
        active = silu(value)
        for layer in range(8):
            pre[layer] = value[:, layer * 128 : layer * 128 + 128]
        for layer in range(4):
            at = layer * 256
            act[layer] = pooled(
                active[:, at : at + 128], active[:, at + 128 : at + 256], 16, 128
            ).astype(BF16)

    outs = [((8, 128, 128), F32), ((4, 64, 128), BF16), ((3, 160, 1280), BF16)]
    return call(body, outs, [], 1 << 29, volume, *halo_z, *halo_y, weights)


def forward_half(act, halo_z, halo_y, weights_half, weights_quarter):
    def body(
        own, before, after, above, below, taps, next_taps, pre, act, next_pre, deep, shifts, inner
    ):
        flags = place_of()
        for layer in range(10):
            if layer < 3:
                middle = before[layer]
            elif layer < 7:
                middle = own[layer - 3]
            else:
                middle = after[layer - 7]
            put_shifts(shifts, 0, layer, above[layer])
            put_shifts(shifts, 48, layer, middle)
            put_shifts(shifts, 112, layer, below[layer])
        for part in range(2):
            value = convolved(taps, shifts, (part * 64, part * 64 + 96), 8)
            for layer in range(8):
                pre[layer, part * 128 : part * 128 + 128, :] = value[
                    :, layer * 128 : layer * 128 + 128
                ]
        row = lax.broadcasted_iota(jnp.int32, (128, 128), 0) // 32
        inside = (row > 0) | (flags[2])
        inside = inside & ((row < 3) | (flags[3]))
        for layer in range(4):
            value = pooled(silu(pre[2 * layer]), silu(pre[2 * layer + 1]), 32, 64)
            keep = inside
            if layer == 0:
                keep = keep & (flags[0])
            if layer == 3:
                keep = keep & (flags[1])
            value = jnp.where(keep, value, 0.0).astype(BF16)
            act[layer] = value
            put_shifts(inner, 0, layer, value)
        value = convolved(next_taps, inner, (0, 128), 2)
        next_pre[0] = value[:, :128]
        next_pre[1] = value[:, 128:]
        coarse = pooled(silu(value[:, :128]), silu(value[:, 128:]), 64, 32)
        dense = coarse[:8].astype(BF16).astype(F32)
        for group in range(1, 8):
            part = coarse[group * 8 : group * 8 + 8].astype(BF16).astype(F32)
            dense = dense + pltpu.roll(part, group * 16, 1)
        deep[...] = dense

    outs = [
        ((8, 256, 128), F32),
        ((4, 128, 128), BF16),
        ((2, 128, 128), F32),
        ((8, 128), F32),
        ((3, 160, 1280), BF16),
    ]
    return call(
        body,
        outs,
        [((3, 128, 512), BF16)],
        1 << 29,
        act,
        *halo_z,
        *halo_y,
        weights_half,
        weights_quarter,
    )


def turned(tile, by):
    return tile if by % 128 == 0 else pltpu.roll(tile, by % 128, 1)


def near_cell(tile, layer_step, step):
    moved = turned(tile, -(16 * layer_step + step))
    column = lanes(tile.shape) % 16
    if step > 0:
        moved = jnp.where(column == 15, 0.0, moved)
    if step < 0:
        moved = jnp.where(column == 0, 0.0, moved)
    return moved.astype(BF16)


def columns_last(tile, start):
    width = tile.shape[0]
    column = lax.broadcasted_iota(jnp.int32, (width, 128), 0)
    picks = jnp.where(lanes((width, 128)) == column + start, 1.0, 0.0).astype(BF16)
    return lax.dot_general(tile, picks, (((0,), (0,)), ((), ())), preferred_element_type=F32)


def opened(dense, layer):
    parts = [turned(dense, 16 * layer - 16 * group) for group in range(8)]
    return jnp.concatenate(parts, axis=0)


def deepest(columns, before, acts, after, skip_deep, halo_z, halo_y, skip, pre, weights, weights_back):
    def body(
        before, acts, after, skip_own, skip_before, skip_after, skip_above, skip_below, skip, pre,
        taps, taps_back, dense_out, out, shifts, delta_own, deltas,
    ):
        flags = place_of()
        core, row_at = flags[4], flags[5]
        place = lanes((64, 128)) // 16

        def cells(position, row):
            source = (before, acts, after)[position // 2]
            return source[position % 2 * columns + row]

        for near in range(5):
            row = row_at + near - 2
            valid = (row >= 0) & (row < columns)
            row = jnp.clip(row, 0, columns - 1)
            value = jnp.zeros((64, 128), F32)
            for layer in range(5):
                dense = jnp.where(core == 0, cells(layer, row), cells(layer + 1, row))
                value = jnp.where(place == layer, opened(dense, layer), value)
            value = jnp.where(valid, value, 0.0)
            for down in range(3):
                for step in range(3):
                    shifts[down * 3 + step, near * 64 : near * 64 + 64, :] = near_cell(
                        value, down - 1, step - 1
                    )
        place = lanes((128, 128)) // 16
        for near in range(3):
            value = None
            for tap in range(9):
                window = shifts[tap, near * 64 : near * 64 + 192, :]
                term = jnp.dot(taps[tap][:, :192], window, preferred_element_type=F32)
                value = term if value is None else value + term
            upstream = jnp.zeros((128, 128), F32)
            for layer in range(3):
                if near != 1:
                    at = 352 + layer * 16
                    dense = (skip_above, skip_below)[near // 2][at : at + 16]
                elif layer == 1:
                    dense = skip_own[...]
                else:
                    dense = (skip_before, skip_after)[layer // 2][0, 256:]
                upstream = upstream + columns_last(dense, 16 * layer + 16)
            keep = (place == 2) | ((place == 1) & (flags[0])) | ((place == 3) & (flags[1]))
            if near != 1:
                keep = keep & (flags[2 + near // 2])
            change = jnp.where(keep, upstream * slope(value), 0.0).astype(BF16).astype(F32)
            if near == 1:
                delta_own[...] = jnp.where(place == 2, change, 0.0).astype(BF16)
            deltas[near * 128 : near * 128 + 128, :] = change
        carried = None
        for down in range(3):
            for step in range(3):
                window = near_cell(deltas[...], down - 1, step - 1)
                term = jnp.dot(
                    taps_back[down * 3 + step], window, preferred_element_type=F32
                )
                carried = term if carried is None else carried + term
        carried = exact_dot(turned(carried, -32), pair_columns(False))
        carried = jnp.concatenate([carried, carried], axis=0)
        dense = None
        for layer in range(2):
            wide = [columns_last(skip[layer, row], 0) for row in range(2)]
            change = (jnp.concatenate(wide, axis=0) + carried) * slope(pre[layer])
            change = jnp.where(lanes(change.shape) < 32, change, 0.0).astype(BF16)
            out[layer] = change
            change = change.astype(F32)
            dense = change if dense is None else dense + turned(change, 32)
        dense_out[0] = dense.astype(BF16)

    outs = [
        ((1, 128, 128), BF16),
        ((2, 128, 128), BF16),
        ((9, 320, 128), BF16),
        ((128, 128), BF16),
    ]
    scratch = [((384, 128), F32)]
    return call(
        body, outs, scratch, 1 << 28,
        before, acts, after, skip_deep, *halo_z, *halo_y, skip, pre, weights, weights_back,
    )


def grad_deepest(shifts, delta):
    def body(shifts, delta, grad):
        for tap in range(9):
            grad[tap * 192 : tap * 192 + 192, :] = lax.dot_general(
                shifts[tap, 64:256, :], delta[...], NT, preferred_element_type=F32
            )

    return call(body, [((1728, 128), F32)], [], 1 << 27, shifts, delta)[0]


def diagonal(product, rows, chans, feats):
    place = lanes((3 * chans, 128)) // feats
    value = product[: 3 * chans]
    for row in range(1, rows):
        value = jnp.where(place == row, product[row * chans : (row + 3) * chans], value)
    turn = 64
    while turn >= feats:
        value = value + pltpu.roll(value, turn, 1)
        turn //= 2
    return value


def packed(tall, groups):
    size = tall.shape[0] // groups
    place = lanes((size, 128)) // (128 // groups)
    value = tall[:size, :]
    for group in range(1, groups):
        value = jnp.where(place == group, tall[group * size : (group + 1) * size, :], value)
    return value


def put_grads(tall, shifts, rows, offset, depth, delta, dims):
    count, chans, feats = dims
    for down in range(3):
        for step in range(3):
            at = (offset + down) * 128
            product = lax.dot_general(
                shifts[step, rows[0] : rows[1], at : at + depth * 128],
                delta,
                NT,
                preferred_element_type=F32,
            )
            tap = (down * 3 + step) * 3 * chans
            tall[tap : tap + 3 * chans, :] = diagonal(product, count, chans, feats)


def grad_quarter_of(act, delta):
    def body(act, delta, grad, shifts, tall):
        for layer in range(4):
            put_shifts(shifts, 0, layer, act[layer])
        both = jnp.concatenate([delta[0], delta[1]], axis=1)
        put_grads(tall, shifts, (0, 128), 0, 2, both, (2, 32, 64))
        grad[...] = packed(tall, 2)

    scratch = [((3, 128, 512), BF16), ((864, 128), F32)]
    return call(body, [((432, 128), F32)], scratch, 1 << 28, act, delta)[0]


def back_rest(
    delta, halo_z, halo_y, skip_half, halo_zs, halo_ys, pre_half, skip_full, pre_full,
    weights_quarter, weights_half, shifts_half, shifts_full, deep_grad, quarter_grad,
):
    def body(
        own, before, after, above, below, skip1, before1, after1, above1, below1, pre1, skip0, pre0,
        taps2, taps1, shifts1, shifts0, grad3, grad2, mine, other, moved2, moved1, delta1, delta0, tall, flat,
    ):
        flags = place_of()
        for layer in range(6):
            middle = (before, own, after)[layer // 2][0]
            for part, tile in enumerate((above[layer // 2], middle, below[layer // 2])):
                tile = turned(tile.astype(F32), -32 * (layer % 2))
                tile = jnp.where(lanes(tile.shape) < 32, tile, 0.0).astype(BF16)
                put_shifts(moved2, part * 128, layer, tile)
        value = convolved(taps2, moved2, (0, 384), 4)
        picks = pair_columns(False)
        row = lax.broadcasted_iota(jnp.int32, (192, 128), 0) // 32
        inside = lanes((192, 128)) < 64
        inside = inside & ((row > 0) | (flags[2])) & ((row < 5) | (flags[3]))
        for layer in range(6):
            if layer % 2 == 1 or layer == 0:
                at = (layer + 1) // 2 * 128
                carried = exact_dot(value[:, at : at + 128], picks)
                parts = [carried[part * 32 : part * 32 + 32] for part in (0, 1, 1, 2, 2, 3)]
                carried = jnp.concatenate(parts, axis=0)
            if layer == 0:
                middle = before1[0, 128:256]
            elif layer == 5:
                middle = after1[0, 128:256]
            else:
                middle = skip1[layer - 1]
            edge = 160 + layer * 32
            skip = jnp.concatenate(
                [above1[edge : edge + 32], middle, below1[edge : edge + 32]], axis=0
            ).astype(F32)
            change = (skip + carried) * slope(pre1[layer + 1, 32:224])
            keep = inside
            if layer == 0:
                keep = keep & (flags[0])
            if layer == 5:
                keep = keep & (flags[1])
            change = jnp.where(keep, change, 0.0).astype(BF16)
            put_shifts(moved1, 0, layer, change)
            if 0 < layer < 5:
                delta1[:, (layer - 1) * 128 : layer * 128] = change[32:160]
        value = convolved(taps1, moved1, (0, 192), 4)
        for layer in range(8):
            if layer % 2 == 0:
                at = layer // 2 * 128
                carried = exact_dot(value[:, at : at + 128], picks)
                parts = [carried[part // 2 * 16 : part // 2 * 16 + 16] for part in range(8)]
                carried = jnp.concatenate(parts, axis=0)
            change = (skip0[layer].astype(F32) + carried) * slope(pre0[layer])
            delta0[:, layer * 128 : layer * 128 + 128] = change.astype(BF16)
        flat[:1728, :] = grad3[...]
        flat[1728:2160, :] = grad2[...]
        tall[...] = jnp.zeros_like(tall)
        put_grads(tall, shifts1, (32, 128), 2, 4, delta1[...], (4, 16, 32))
        flat[2160:2272, :] = packed(tall, 4)
        put_grads(tall, shifts0, (0, 160), 0, 8, delta0[...], (8, 16, 16))
        flat[2272:2328, :] = packed(tall, 8)
        flat[2328:, :] = jnp.zeros((2560 - 2328, 128), F32)
        core = flags[4]
        for part in range(5):
            block = slice(part * 128, part * 128 + 128)
            mine[:, block] = flat[pl.ds(pl.multiple_of(part * 512 + core * 256, 256), 256), :]
            other[:, block] = flat[
                pl.ds(pl.multiple_of(part * 512 + (1 - core) * 256, 256), 256), :
            ]

    scratch = [
        ((3, 384, 768), BF16),
        ((3, 192, 768), BF16),
        ((128, 512), BF16),
        ((128, 1024), BF16),
        ((448, 128), F32),
        ((2560, 128), F32),
    ]
    return call(
        body, [(HALF, F32), (HALF, F32)], scratch, 1 << 30,
        delta, *halo_z, *halo_y, skip_half, *halo_zs, *halo_ys, pre_half, skip_full, pre_full,
        weights_quarter, weights_half, shifts_half, shifts_full, deep_grad, quarter_grad,
    )


def unpack(mine, other):
    def body(mine, other, full, half, quarter, eighth, whole, tall):
        core = lax.axis_index("c")
        for part in range(5):
            block = slice(part * 128, part * 128 + 128)
            at = part * 512 + core * 256
            whole[pl.ds(pl.multiple_of(at, 256), 256), :] = mine[:, block].astype(F32)
            at = part * 512 + (1 - core) * 256
            whole[pl.ds(pl.multiple_of(at, 256), 256), :] = other[:, block].astype(F32)

        def spread(out, source, chans):
            for down in range(3):
                for across in range(3):
                    for step in range(3):
                        at = ((down * 3 + across) * 3 + step) * chans
                        start = ((down * 3 + step) * 3 + across) * chans
                        out[at : at + chans, :] = source[
                            start : start + chans, : out.shape[1]
                        ]

        spread(eighth, whole, 64)
        for out, start, size, groups, chans in (
            (quarter, 1728, 432, 2, 32),
            (half, 2160, 112, 4, 16),
            (full, 2272, 56, 8, 16),
        ):
            dense = whole[start : start + size, :]
            for group in range(groups):
                tall[group * size : (group + 1) * size, :] = (
                    dense if group == 0 else pltpu.roll(dense, 128 - group * (128 // groups), 1)
                )
            spread(out, tall, chans)

    outs = [((432, 16), F32), ((432, 32), F32), ((864, 64), F32), ((1728, 128), F32)]
    scratch = [((2560, 128), F32), ((864, 128), F32)]
    return call(body, outs, scratch, 1 << 20, mine, other)


def exchange(first, last, axis):
    size = lax.axis_size(axis)
    up = [(i, i + 1) for i in range(size - 1)]
    down = [(i + 1, i) for i in range(size - 1)]
    return lax.ppermute(last, axis, up), lax.ppermute(first, axis, down)


def rims(block, depth, rows):
    before, after = exchange(block[:depth], block[block.shape[0] - depth :], GZ)
    tall = block.shape[1]

    def edge(start):
        parts = [part[:, start : start + rows] for part in (before, block, after)]
        return jnp.concatenate(parts, axis=0)

    return (before, after), exchange(edge(0), edge(tall - rows), "gy")


def laid_out(array):
    chans, depth, height, width = array.shape
    rows = jnp.transpose(array, (1, 2, 0, 3)).reshape(depth, height * chans, width)
    return jnp.pad(rows, ((0, 0), (0, 0), (0, 128 - width)))


def summed(mine, other):
    swap = [(0, 1), (1, 0)]
    columns, planes = lax.axis_size("gy"), lax.axis_size(("x", "z"))
    rows, width = HALF[0] // columns, HALF[1]
    pair = (mine + lax.ppermute(other, "c", swap)).astype(BF16)
    pieces = lax.all_to_all(pair.reshape(columns, rows, width), "gy", 0, 0)
    column = jnp.sum(pieces.astype(F32), axis=0)
    chunk = rows // planes
    pieces = lax.all_to_all(column, ("x", "z"), 0, 0, tiled=True)
    done = jnp.sum(pieces.reshape(planes, chunk, width), axis=0)
    spread = jnp.broadcast_to(done[None], (planes, chunk, width)).reshape(rows, width)
    column = lax.all_to_all(lax.optimization_barrier(spread), ("x", "z"), 0, 0, tiled=True)
    column = column.astype(BF16)
    spread = lax.optimization_barrier(jnp.broadcast_to(column[None], (columns, rows, width)))
    half = lax.all_to_all(spread, "gy", 0, 0).reshape(HALF)
    return unpack(half, lax.ppermute(half, "c", swap))


def on_device(
    volume,
    kernel_full,
    kernel_half,
    kernel_quarter,
    kernel_eighth,
    skip_full,
    skip_half,
    skip_quarter,
    skip_eighth,
):
    kernels = (kernel_full, kernel_half, kernel_quarter, kernel_eighth)
    volume = laid_out(volume)
    skip1 = laid_out(skip_half)
    skip3 = jnp.transpose(skip_eighth, (1, 2, 3, 0)).reshape(1, 16, 128)
    skip2 = jnp.transpose(skip_quarter, (1, 2, 3, 0))
    first = jnp.concatenate([volume[:1], skip1[:1], skip3], axis=1)
    last = jnp.concatenate([volume[7:], skip1[3:], skip3], axis=1)
    before, after = exchange(first, last, GZ)
    before, after, skip0 = lax.optimization_barrier((before, after, laid_out(skip_full)))

    def edge(start, start1):
        parts = [
            part[:, start : start + 16].reshape(-1, 128)
            for part in (before[:, :128], volume, after[:, :128])
        ]
        parts += [
            part[:, start1 : start1 + 32].reshape(-1, 128)
            for part in (before[:, 128:256], skip1, after[:, 128:256])
        ]
        parts += [before[0, 256:], skip3[0], after[0, 256:]]
        return jnp.concatenate(parts, axis=0)

    above, below = exchange(edge(0, 0), edge(112, 96), "gy")
    halo_z0, halo_y0 = (before, after), (above, below)
    dims = ((8, 16, 16), (4, 16, 32), (2, 32, 64), (1, 64, 128))
    w0, w1, w2, w3, t1, t2, t3 = prepare(kernels, dims)
    pre0, act1, shifts0 = forward_full(volume, halo_z0, halo_y0, w0)
    halo_z, halo_y = rims(act1, 3, 48)
    pre1, act2, pre2, act3, shifts1 = forward_half(act1, halo_z, halo_y, w1, w2)
    columns = lax.axis_size("gy")
    many = (2 * columns,) + act3.shape
    acts = lax.all_to_all(
        lax.optimization_barrier(jnp.broadcast_to(act3[None], many)), ("c", "gy"), 0, 0
    )
    before, after = exchange(acts, acts, ("x", "z"))
    dense2, delta2, shifts3, delta3 = deepest(
        columns, before, acts, after, skip3[0], halo_z0, halo_y0, skip2, pre2, w3, t3
    )
    halo_z, halo_y = rims(dense2, 1, 128)
    grad3 = grad_deepest(shifts3, delta3)
    grad2 = grad_quarter_of(act2, delta2)
    mine, other = back_rest(
        dense2, halo_z, halo_y, skip1, halo_z0, halo_y0, pre1, skip0, pre0,
        t2, t1, shifts1, shifts0, grad3, grad2,
    )
    outs = summed(mine, other)
    return tuple(out.reshape(kernel.shape) for out, kernel in zip(outs, kernels))


def solution(mesh):
    fine = jax.sharding.Mesh(mesh.devices.reshape(4, 8, 2, 8), ("x", "z", "c", "gy"))
    return mapped(fine)


def mapped(fine):
    block = P(None, GZ, "gy", None)
    return jax.shard_map(
        on_device,
        mesh=fine,
        in_specs=(block, P(), P(), P(), P(), block, block, block, block),
        out_specs=(P(), P(), P(), P()),
        check_vma=False,
    )
```

```python
import jax
import jax.numpy as jnp
from jax import lax
from jax.experimental import pallas as pl
from jax.experimental.pallas import tpu as pltpu
from jax.sharding import PartitionSpec as P

F32 = jnp.float32
BF16 = jnp.bfloat16
GZ = ("x", "z", "c")
VMEM_BYTES = 14 * 1024 * 1024
HALF = (256, 640)
NT = (((1,), (1,)), ((), ()))


def call(body, outs, scratch, flops, *args):
    return pl.pallas_call(
        body,
        out_shape=tuple(jax.ShapeDtypeStruct(shape, dtype) for shape, dtype in outs),
        in_specs=[pl.BlockSpec(memory_space=pltpu.VMEM) for _ in args],
        out_specs=tuple(pl.BlockSpec(memory_space=pltpu.VMEM) for _ in outs),
        scratch_shapes=[pltpu.VMEM(shape, dtype) for shape, dtype in scratch],
        compiler_params=pltpu.CompilerParams(vmem_limit_bytes=VMEM_BYTES),
        cost_estimate=pl.CostEstimate(flops=flops, bytes_accessed=1 << 20, transcendentals=0),
    )(*args)


def place_of():
    depth_at, row_at = lax.axis_index(GZ), lax.axis_index("gy")
    return (
        depth_at > 0,
        depth_at < lax.axis_size(GZ) - 1,
        row_at > 0,
        row_at < lax.axis_size("gy") - 1,
        lax.axis_index("c"),
        row_at,
    )


def lanes(shape):
    return lax.broadcasted_iota(jnp.int32, shape, 1)


def at_column(tile, step):
    if step == 0:
        return tile
    moved = pltpu.roll(tile.astype(F32), (-step) % 128, 1)
    edge = 127 if step > 0 else 0
    return jnp.where(lanes(tile.shape) == edge, 0.0, moved).astype(BF16)


def put_shifts(shifts, row, layer, tile):
    for step in range(3):
        shifts[step, row : row + tile.shape[0], layer * 128 : layer * 128 + 128] = at_column(
            tile, step - 1
        )


def convolved(weights, shifts, rows, depth):
    total = None
    for down in range(3):
        for step in range(3):
            window = shifts[step, rows[0] : rows[1], down * 128 : (down + depth) * 128]
            tap = weights[down * 3 + step]
            term = jnp.dot(
                tap[:, : rows[1] - rows[0]], window, preferred_element_type=F32
            )
            total = term if total is None else total + term
    return total


def sigmoid(values):
    return 1.0 / (1.0 + jnp.exp(-values))


def slope(values):
    sig = sigmoid(values)
    return sig * (1.0 + values * (1.0 - sig))


def exact_dot(values, picks):
    high = values.astype(BF16)
    rest = values - high.astype(F32)
    middle = rest.astype(BF16)
    low = (rest - middle.astype(F32)).astype(BF16)
    total = jnp.dot(low, picks, preferred_element_type=F32)
    total = total + jnp.dot(middle, picks, preferred_element_type=F32)
    return total + jnp.dot(high, picks, preferred_element_type=F32)


def pair_columns(down):
    rows = lax.broadcasted_iota(jnp.int32, (128, 128), 0)
    columns = lax.broadcasted_iota(jnp.int32, (128, 128), 1)
    hit = (rows // 2 == columns) if down else (columns // 2 == rows)
    return jnp.where(hit, 0.125, 0.0).astype(BF16)


def pooled(first, second, channels, width):
    both = first + second
    blocks = both.shape[0] // (2 * channels)
    rows = []
    for block in range(blocks):
        start = 2 * block * channels
        rows.append(
            both[start : start + channels] + both[start + channels : start + 2 * channels]
        )
    summed = rows[0] if blocks == 1 else jnp.concatenate(rows, axis=0)
    mean = exact_dot(summed, pair_columns(True))
    return jnp.where(lanes(mean.shape) < width // 2, mean, 0.0)


def silu(values):
    return values * sigmoid(values)


def prepare(kernels, dims):
    def body(*refs):
        ins, outs, wide = refs[:4], refs[4:11], refs[11]
        for level, (rows, chans, feats) in enumerate(dims):
            source, taps = ins[level][...], outs[level]
            picks = (
                lax.broadcasted_iota(jnp.int32, (feats, 128), 0)
                == lax.broadcasted_iota(jnp.int32, (feats, 128), 1) % feats
            )
            spread = jnp.dot(
                source, jnp.where(picks, 1.0, 0.0).astype(BF16), preferred_element_type=F32
            )
            size = taps.shape[2]
            place = lanes((chans, 128)) // feats
            for down in range(3):
                for step in range(3):
                    wide[...] = jnp.zeros_like(wide)
                    for row in range(rows + 2):
                        value = jnp.zeros((chans, 128), F32)
                        for across in range(3):
                            at = ((down * 3 + across) * 3 + step) * chans
                            value = jnp.where(
                                place == row - across, spread[at : at + chans], value
                            )
                        wide[row * chans : (row + 1) * chans, :] = value
                    taps[down * 3 + step] = wide[:size, :].T.astype(BF16)
        for level in range(1, 4):
            rows, chans, feats = dims[level]
            if level == 2:
                rows = 4
            source, taps = ins[level][...], outs[3 + level]
            size = (rows + 2) * feats
            picks = (
                lax.broadcasted_iota(jnp.int32, (feats, size), 0)
                == lax.broadcasted_iota(jnp.int32, (feats, size), 1) % feats
            )
            spread = jnp.dot(
                source, jnp.where(picks, 1.0, 0.0).astype(BF16), preferred_element_type=F32
            )
            place = lanes((chans, size)) // feats
            for down in range(3):
                for step in range(3):
                    for row in range(rows):
                        value = jnp.zeros((chans, size), F32)
                        for across in range(3):
                            at = (((2 - down) * 3 + 2 - across) * 3 + 2 - step) * chans
                            value = jnp.where(
                                place == row + across, spread[at : at + chans], value
                            )
                        taps[down * 3 + step, row * chans : (row + 1) * chans, :] = (
                            value.astype(BF16)
                        )

    shapes = [(9, 128, 256), (9, 128, 128), (9, 128, 128), (9, 128, 256)]
    shapes += [(9, 64, 192), (9, 128, 384), (9, 64, 384)]
    flat = [kernel.reshape(-1, kernel.shape[-1]) for kernel in kernels]
    return call(body, [(s, BF16) for s in shapes], [((256, 128), F32)], 1 << 27, *flat)


def forward_full(volume, halo_z, halo_y, weights, skip_half, skip_deep):
    def body(own, one, two, above, below, taps, skip1, skip3, pre, act, shifts, to_one, to_two):
        even = lax.axis_index("c") == 0
        for layer in range(10):
            if 0 < layer < 9:
                parts = [part[layer * 16 : layer * 16 + 16] for part in (above, below)]
                parts.insert(1, own[layer - 1])
            else:
                near, far = (two, one) if layer == 0 else (one, two)
                at = (144, 0) if layer == 0 else (0, 144)
                parts = [
                    jnp.where(even, part[at[0] : at[0] + 16], part[at[1] : at[1] + 16])
                    for part in (above, below)
                ]
                parts.insert(1, jnp.where(even, near[0], far[0]))
            put_shifts(shifts, 0, layer, parts[0])
            put_shifts(shifts, 16, layer, parts[1])
            put_shifts(shifts, 144, layer, parts[2])
        value = convolved(taps, shifts, (0, 160), 8)
        active = silu(value)
        for layer in range(8):
            pre[layer] = value[:, layer * 128 : layer * 128 + 128]
        for layer in range(4):
            at = layer * 256
            act[layer] = pooled(
                active[:, at : at + 128], active[:, at + 128 : at + 256], 16, 128
            ).astype(BF16)
        for layer in range(3):
            rows = slice(layer * 64, layer * 64 + 64)
            to_one[rows] = jnp.where(even, act[layer + 1], act[layer])
            to_two[rows] = jnp.where(even, act[layer], act[layer + 1])
        to_one[192:320] = jnp.where(even, skip1[3], skip1[0])
        to_two[192:320] = jnp.where(even, skip1[0], skip1[3])
        to_one[320:] = skip3[...]
        to_two[320:] = skip3[...]

    outs = [((8, 128, 128), F32), ((4, 64, 128), BF16), ((3, 160, 1280), BF16)]
    outs += [((336, 128), BF16), ((336, 128), BF16)]
    return call(
        body, outs, [], 1 << 29, volume, *halo_z, *halo_y, weights, skip_half, skip_deep
    )


def forward_half(act, halo_z, halo_y, weights_half, weights_quarter):
    def body(
        own, one, two, above, below, taps, next_taps, pre, act, next_pre, deep, shifts, inner
    ):
        flags = place_of()
        even = flags[4] == 0
        for layer in range(10):
            if 3 <= layer < 7:
                at = layer * 48
                middle = own[layer - 3]
                edges = [part[at : at + 48] for part in (above, below)]
            else:
                near, far = (two, one) if layer < 3 else (one, two)
                at = layer % 7 * 64
                middle = jnp.where(even, near[at : at + 64], far[at : at + 64])
                at = layer % 7 * 48
                at = (336 + at, at) if layer < 3 else (at, 336 + at)
                edges = [
                    jnp.where(even, part[at[0] : at[0] + 48], part[at[1] : at[1] + 48])
                    for part in (above, below)
                ]
            put_shifts(shifts, 0, layer, edges[0])
            put_shifts(shifts, 48, layer, middle)
            put_shifts(shifts, 112, layer, edges[1])
        for part in range(2):
            value = convolved(taps, shifts, (part * 64, part * 64 + 96), 8)
            for layer in range(8):
                pre[layer, part * 128 : part * 128 + 128, :] = value[
                    :, layer * 128 : layer * 128 + 128
                ]
        row = lax.broadcasted_iota(jnp.int32, (128, 128), 0) // 32
        inside = (row > 0) | (flags[2])
        inside = inside & ((row < 3) | (flags[3]))
        for layer in range(4):
            value = pooled(silu(pre[2 * layer]), silu(pre[2 * layer + 1]), 32, 64)
            keep = inside
            if layer == 0:
                keep = keep & (flags[0])
            if layer == 3:
                keep = keep & (flags[1])
            value = jnp.where(keep, value, 0.0).astype(BF16)
            act[layer] = value
            put_shifts(inner, 0, layer, value)
        value = convolved(next_taps, inner, (0, 128), 2)
        next_pre[0] = value[:, :128]
        next_pre[1] = value[:, 128:]
        coarse = pooled(silu(value[:, :128]), silu(value[:, 128:]), 64, 32)
        dense = coarse[:8].astype(BF16).astype(F32)
        for group in range(1, 8):
            part = coarse[group * 8 : group * 8 + 8].astype(BF16).astype(F32)
            dense = dense + pltpu.roll(part, group * 16, 1)
        deep[...] = dense

    outs = [
        ((8, 256, 128), F32),
        ((4, 128, 128), BF16),
        ((2, 128, 128), F32),
        ((8, 128), F32),
        ((3, 160, 1280), BF16),
    ]
    return call(
        body,
        outs,
        [((3, 128, 512), BF16)],
        1 << 29,
        act,
        *halo_z,
        *halo_y,
        weights_half,
        weights_quarter,
    )


def turned(tile, by):
    return tile if by % 128 == 0 else pltpu.roll(tile, by % 128, 1)


def near_cell(tile, layer_step, step):
    moved = turned(tile, -(16 * layer_step + step))
    column = lanes(tile.shape) % 16
    if step > 0:
        moved = jnp.where(column == 15, 0.0, moved)
    if step < 0:
        moved = jnp.where(column == 0, 0.0, moved)
    return moved.astype(BF16)


def columns_last(tile, start):
    width = tile.shape[0]
    column = lax.broadcasted_iota(jnp.int32, (width, 128), 0)
    picks = jnp.where(lanes((width, 128)) == column + start, 1.0, 0.0).astype(BF16)
    return lax.dot_general(tile, picks, (((0,), (0,)), ((), ())), preferred_element_type=F32)


def opened(dense, layer):
    parts = [turned(dense, 16 * layer - 16 * group) for group in range(8)]
    return jnp.concatenate(parts, axis=0)


def deepest(columns, before, acts, after, skip_deep, halo_z, halo_y, skip, pre, weights, weights_back):
    def body(
        before, acts, after, skip_own, skip_one, skip_two, skip_above, skip_below, skip, pre,
        taps, taps_back, dense_out, out, shifts, delta_own, deltas,
    ):
        flags = place_of()
        core, row_at = flags[4], flags[5]
        place = lanes((64, 128)) // 16

        def cells(position, row):
            source = (before, acts, after)[position // 2]
            return source[position % 2 * columns + row]

        for near in range(5):
            row = row_at + near - 2
            valid = (row >= 0) & (row < columns)
            row = jnp.clip(row, 0, columns - 1)
            value = jnp.zeros((64, 128), F32)
            for layer in range(5):
                dense = jnp.where(core == 0, cells(layer, row), cells(layer + 1, row))
                value = jnp.where(place == layer, opened(dense, layer), value)
            value = jnp.where(valid, value, 0.0)
            for down in range(3):
                for step in range(3):
                    shifts[down * 3 + step, near * 64 : near * 64 + 64, :] = near_cell(
                        value, down - 1, step - 1
                    )
        place = lanes((128, 128)) // 16
        for near in range(3):
            value = None
            for tap in range(9):
                window = shifts[tap, near * 64 : near * 64 + 192, :]
                term = jnp.dot(taps[tap][:, :192], window, preferred_element_type=F32)
                value = term if value is None else value + term
            upstream = jnp.zeros((128, 128), F32)
            for layer in range(3):
                if near != 1:
                    edge = (skip_above, skip_below)[near // 2]
                    at = 704 - layer * 16
                    dense = jnp.where(
                        core == 0, edge[at : at + 16], edge[1392 - at - 16 : 1392 - at]
                    )
                elif layer == 1:
                    dense = skip_own[...]
                else:
                    ends = (skip_two, skip_one) if layer == 0 else (skip_one, skip_two)
                    dense = jnp.where(core == 0, ends[0][320:], ends[1][320:])
                upstream = upstream + columns_last(dense, 16 * layer + 16)
            keep = (place == 2) | ((place == 1) & (flags[0])) | ((place == 3) & (flags[1]))
            if near != 1:
                keep = keep & (flags[2 + near // 2])
            change = jnp.where(keep, upstream * slope(value), 0.0).astype(BF16).astype(F32)
            if near == 1:
                delta_own[...] = jnp.where(place == 2, change, 0.0).astype(BF16)
            deltas[near * 128 : near * 128 + 128, :] = change
        carried = None
        for down in range(3):
            for step in range(3):
                window = near_cell(deltas[...], down - 1, step - 1)
                term = jnp.dot(
                    taps_back[down * 3 + step], window, preferred_element_type=F32
                )
                carried = term if carried is None else carried + term
        carried = exact_dot(turned(carried, -32), pair_columns(False))
        carried = jnp.concatenate([carried, carried], axis=0)
        dense = None
        for layer in range(2):
            wide = [columns_last(skip[layer, row], 0) for row in range(2)]
            change = (jnp.concatenate(wide, axis=0) + carried) * slope(pre[layer])
            change = jnp.where(lanes(change.shape) < 32, change, 0.0).astype(BF16)
            out[layer] = change
            change = change.astype(F32)
            dense = change if dense is None else dense + turned(change, 32)
        dense_out[0] = dense.astype(BF16)

    outs = [
        ((1, 128, 128), BF16),
        ((2, 128, 128), BF16),
        ((9, 320, 128), BF16),
        ((128, 128), BF16),
    ]
    scratch = [((384, 128), F32)]
    return call(
        body, outs, scratch, 1 << 28,
        before, acts, after, skip_deep, *halo_z, *halo_y, skip, pre, weights, weights_back,
    )


def grad_deepest(shifts, delta):
    def body(shifts, delta, grad):
        for tap in range(9):
            grad[tap * 192 : tap * 192 + 192, :] = lax.dot_general(
                shifts[tap, 64:256, :], delta[...], NT, preferred_element_type=F32
            )

    return call(body, [((1728, 128), F32)], [], 1 << 27, shifts, delta)[0]


def diagonal(product, rows, chans, feats):
    place = lanes((3 * chans, 128)) // feats
    value = product[: 3 * chans]
    for row in range(1, rows):
        value = jnp.where(place == row, product[row * chans : (row + 3) * chans], value)
    turn = 64
    while turn >= feats:
        value = value + pltpu.roll(value, turn, 1)
        turn //= 2
    return value


def packed(tall, groups):
    size = tall.shape[0] // groups
    place = lanes((size, 128)) // (128 // groups)
    value = tall[:size, :]
    for group in range(1, groups):
        value = jnp.where(place == group, tall[group * size : (group + 1) * size, :], value)
    return value


def put_grads(tall, shifts, rows, offset, depth, delta, dims):
    count, chans, feats = dims
    for down in range(3):
        for step in range(3):
            at = (offset + down) * 128
            product = lax.dot_general(
                shifts[step, rows[0] : rows[1], at : at + depth * 128],
                delta,
                NT,
                preferred_element_type=F32,
            )
            tap = (down * 3 + step) * 3 * chans
            tall[tap : tap + 3 * chans, :] = diagonal(product, count, chans, feats)


def grad_quarter_of(act, delta):
    def body(act, delta, grad, shifts, tall):
        for layer in range(4):
            put_shifts(shifts, 0, layer, act[layer])
        both = jnp.concatenate([delta[0], delta[1]], axis=1)
        put_grads(tall, shifts, (0, 128), 0, 2, both, (2, 32, 64))
        grad[...] = packed(tall, 2)

    scratch = [((3, 128, 512), BF16), ((864, 128), F32)]
    return call(body, [((432, 128), F32)], scratch, 1 << 28, act, delta)[0]


def back_rest(
    delta, halo_z, halo_y, skip_half, halo_zs, halo_ys, pre_half, skip_full, pre_full,
    weights_quarter, weights_half, shifts_half, shifts_full, deep_grad, quarter_grad,
):
    def body(
        own, one, two, above, below, skip1, one1, two1, above1, below1, pre1, skip0, pre0,
        taps2, taps1, shifts1, shifts0, grad3, grad2, mine, other, moved2, moved1, delta1, delta0, tall, flat,
    ):
        flags = place_of()
        even = flags[4] == 0
        for layer in range(6):
            block = layer // 2
            if block == 1:
                tiles = (above[1], own[0], below[1])
            else:
                near, far = (two, one) if block == 0 else (one, two)
                tiles = (
                    jnp.where(even, above[2 - block], above[block]),
                    jnp.where(even, near[0], far[0]),
                    jnp.where(even, below[2 - block], below[block]),
                )
            for part, tile in enumerate(tiles):
                tile = turned(tile.astype(F32), -32 * (layer % 2))
                tile = jnp.where(lanes(tile.shape) < 32, tile, 0.0).astype(BF16)
                put_shifts(moved2, part * 128, layer, tile)
        value = convolved(taps2, moved2, (0, 384), 4)
        picks = pair_columns(False)
        row = lax.broadcasted_iota(jnp.int32, (192, 128), 0) // 32
        inside = lanes((192, 128)) < 64
        inside = inside & ((row > 0) | (flags[2])) & ((row < 5) | (flags[3]))
        for layer in range(6):
            if layer % 2 == 1 or layer == 0:
                at = (layer + 1) // 2 * 128
                carried = exact_dot(value[:, at : at + 128], picks)
                parts = [carried[part * 32 : part * 32 + 32] for part in (0, 1, 1, 2, 2, 3)]
                carried = jnp.concatenate(parts, axis=0)
            if 0 < layer < 5:
                at = 480 + layer * 32
                parts = [above1[at : at + 32], skip1[layer - 1], below1[at : at + 32]]
            else:
                near, far = (two1, one1) if layer == 0 else (one1, two1)
                at = (640, 480) if layer == 0 else (480, 640)
                parts = [
                    jnp.where(even, above1[at[0] : at[0] + 32], above1[at[1] : at[1] + 32]),
                    jnp.where(even, near[192:320], far[192:320]),
                    jnp.where(even, below1[at[0] : at[0] + 32], below1[at[1] : at[1] + 32]),
                ]
            skip = jnp.concatenate(parts, axis=0).astype(F32)
            change = (skip + carried) * slope(pre1[layer + 1, 32:224])
            keep = inside
            if layer == 0:
                keep = keep & (flags[0])
            if layer == 5:
                keep = keep & (flags[1])
            change = jnp.where(keep, change, 0.0).astype(BF16)
            put_shifts(moved1, 0, layer, change)
            if 0 < layer < 5:
                delta1[:, (layer - 1) * 128 : layer * 128] = change[32:160]
        value = convolved(taps1, moved1, (0, 192), 4)
        for layer in range(8):
            if layer % 2 == 0:
                at = layer // 2 * 128
                carried = exact_dot(value[:, at : at + 128], picks)
                parts = [carried[part // 2 * 16 : part // 2 * 16 + 16] for part in range(8)]
                carried = jnp.concatenate(parts, axis=0)
            change = (skip0[layer].astype(F32) + carried) * slope(pre0[layer])
            delta0[:, layer * 128 : layer * 128 + 128] = change.astype(BF16)
        flat[:1728, :] = grad3[...]
        flat[1728:2160, :] = grad2[...]
        tall[...] = jnp.zeros_like(tall)
        put_grads(tall, shifts1, (32, 128), 2, 4, delta1[...], (4, 16, 32))
        flat[2160:2272, :] = packed(tall, 4)
        put_grads(tall, shifts0, (0, 160), 0, 8, delta0[...], (8, 16, 16))
        flat[2272:2328, :] = packed(tall, 8)
        flat[2328:, :] = jnp.zeros((2560 - 2328, 128), F32)
        core = flags[4]
        for part in range(5):
            block = slice(part * 128, part * 128 + 128)
            mine[:, block] = flat[pl.ds(pl.multiple_of(part * 512 + core * 256, 256), 256), :]
            other[:, block] = flat[
                pl.ds(pl.multiple_of(part * 512 + (1 - core) * 256, 256), 256), :
            ]

    scratch = [
        ((3, 384, 768), BF16),
        ((3, 192, 768), BF16),
        ((128, 512), BF16),
        ((128, 1024), BF16),
        ((448, 128), F32),
        ((2560, 128), F32),
    ]
    return call(
        body, [(HALF, F32), (HALF, F32)], scratch, 1 << 30,
        delta, *halo_z, *halo_y, skip_half, *halo_zs, *halo_ys, pre_half, skip_full, pre_full,
        weights_quarter, weights_half, shifts_half, shifts_full, deep_grad, quarter_grad,
    )


def unpack(mine, other):
    def body(mine, other, full, half, quarter, eighth, whole, tall):
        core = lax.axis_index("c")
        for part in range(5):
            block = slice(part * 128, part * 128 + 128)
            at = part * 512 + core * 256
            whole[pl.ds(pl.multiple_of(at, 256), 256), :] = mine[:, block].astype(F32)
            at = part * 512 + (1 - core) * 256
            whole[pl.ds(pl.multiple_of(at, 256), 256), :] = other[:, block].astype(F32)

        def spread(out, source, chans):
            for down in range(3):
                for across in range(3):
                    for step in range(3):
                        at = ((down * 3 + across) * 3 + step) * chans
                        start = ((down * 3 + step) * 3 + across) * chans
                        out[at : at + chans, :] = source[
                            start : start + chans, : out.shape[1]
                        ]

        spread(eighth, whole, 64)
        for out, start, size, groups, chans in (
            (quarter, 1728, 432, 2, 32),
            (half, 2160, 112, 4, 16),
            (full, 2272, 56, 8, 16),
        ):
            dense = whole[start : start + size, :]
            for group in range(groups):
                tall[group * size : (group + 1) * size, :] = (
                    dense if group == 0 else pltpu.roll(dense, 128 - group * (128 // groups), 1)
                )
            spread(out, tall, chans)

    outs = [((432, 16), F32), ((432, 32), F32), ((864, 64), F32), ((1728, 128), F32)]
    scratch = [((2560, 128), F32), ((864, 128), F32)]
    return call(body, outs, scratch, 1 << 20, mine, other)


def exchange(first, last, axis):
    size = lax.axis_size(axis)
    up = [(i, i + 1) for i in range(size - 1)]
    down = [(i + 1, i) for i in range(size - 1)]
    return lax.ppermute(last, axis, up), lax.ppermute(first, axis, down)


def swaps(to_one, to_two):
    size = lax.axis_size(GZ)
    on_chip = [(i, i ^ 1) for i in range(size)]
    between = [(i, i + 1) for i in range(1, size - 1, 2)]
    between += [(j, i) for i, j in between]
    return lax.ppermute(to_one, GZ, on_chip), lax.ppermute(to_two, GZ, between)


def laid_out(array):
    chans, depth, height, width = array.shape
    rows = jnp.transpose(array, (1, 2, 0, 3)).reshape(depth, height * chans, width)
    return jnp.pad(rows, ((0, 0), (0, 0), (0, 128 - width)))


def summed(mine, other):
    swap = [(0, 1), (1, 0)]
    pair = (mine + lax.ppermute(other, "c", swap)).astype(BF16)
    group = ("x", "z", "gy")
    count = lax.axis_size(group)
    chunk, width = HALF[0] // count, HALF[1]
    pieces = lax.all_to_all(pair, group, 0, 0, tiled=True)
    done = jnp.sum(pieces.reshape(count, chunk, width).astype(F32), axis=0).astype(BF16)
    spread = jnp.broadcast_to(done[None], (count, chunk, width)).reshape(HALF)
    half = lax.all_to_all(lax.optimization_barrier(spread), group, 0, 0, tiled=True)
    return unpack(half, lax.ppermute(half, "c", swap))


def on_device(
    volume,
    kernel_full,
    kernel_half,
    kernel_quarter,
    kernel_eighth,
    skip_full,
    skip_half,
    skip_quarter,
    skip_eighth,
):
    kernels = (kernel_full, kernel_half, kernel_quarter, kernel_eighth)
    volume = laid_out(volume)
    even = lax.axis_index("c") == 0
    first, last = volume[:1], volume[7:]
    one, two = swaps(jnp.where(even, last, first), jnp.where(even, first, last))
    skip3 = jnp.transpose(skip_eighth, (1, 2, 3, 0)).reshape(16, 128)
    skip2 = jnp.transpose(skip_quarter, (1, 2, 3, 0))
    one, two, skip0, skip1 = lax.optimization_barrier(
        (one, two, laid_out(skip_full), laid_out(skip_half))
    )

    def flat(parts):
        return jnp.concatenate([part.reshape(-1, 128) for part in parts], axis=0)

    def edge(start):
        return flat([part[:, start : start + 16] for part in (one, volume, two)])

    halo_y = exchange(edge(0), edge(112), "gy")
    dims = ((8, 16, 16), (4, 16, 32), (2, 32, 64), (1, 64, 128))
    w0, w1, w2, w3, t1, t2, t3 = prepare(kernels, dims)
    pre0, act1, shifts0, to_one, to_two = forward_full(
        volume, (one, two), halo_y, w0, skip1, skip3
    )
    halo_z1 = one, two = swaps(to_one, to_two)

    def edge1(start, start1):
        acts = [part[:192].reshape(3, 64, 128) for part in (one, two)]
        acts.insert(1, act1)
        rims = [part[192:320].reshape(1, 128, 128) for part in (one, two)]
        rims.insert(1, skip1)
        parts = [part[:, start : start + 48] for part in acts]
        parts += [part[:, start1 : start1 + 32] for part in rims]
        return flat(parts + [one[320:], skip3, two[320:]])

    halo_y1 = exchange(edge1(0, 0), edge1(16, 96), "gy")
    pre1, act2, pre2, act3, shifts1 = forward_half(act1, halo_z1, halo_y1, w1, w2)
    columns = lax.axis_size("gy")
    many = (2 * columns,) + act3.shape
    acts = lax.all_to_all(
        lax.optimization_barrier(jnp.broadcast_to(act3[None], many)), ("c", "gy"), 0, 0
    )
    before, after = exchange(acts, acts, ("x", "z"))
    dense2, delta2, shifts3, delta3 = deepest(
        columns, before, acts, after, skip3, halo_z1, halo_y1, skip2, pre2, w3, t3
    )
    halo_z = one, two = swaps(dense2, dense2)
    block = jnp.concatenate([one, dense2, two], axis=0)
    halo_y = exchange(block, block, "gy")
    grad3 = grad_deepest(shifts3, delta3)
    grad2 = grad_quarter_of(act2, delta2)
    mine, other = back_rest(
        dense2, halo_z, halo_y, skip1, halo_z1, halo_y1, pre1, skip0, pre0,
        t2, t1, shifts1, shifts0, grad3, grad2,
    )
    outs = summed(mine, other)
    return tuple(out.reshape(kernel.shape) for out, kernel in zip(outs, kernels))


def solution(mesh):
    fine = jax.sharding.Mesh(mesh.devices.reshape(4, 8, 2, 8), ("x", "z", "c", "gy"))
    return mapped(fine)


def mapped(fine):
    block = P(None, GZ, "gy", None)
    return jax.shard_map(
        on_device,
        mesh=fine,
        in_specs=(block, P(), P(), P(), P(), block, block, block, block),
        out_specs=(P(), P(), P(), P()),
        check_vma=False,
    )
```

```python
import jax
import jax.numpy as jnp
from jax import lax
from jax.experimental import pallas as pl
from jax.experimental.pallas import tpu as pltpu
from jax.sharding import PartitionSpec as P

F32 = jnp.float32
BF16 = jnp.bfloat16
GZ = ("x", "z", "c")
VMEM_BYTES = 14 * 1024 * 1024
NT = (((1,), (1,)), ((), ()))


def call(body, outs, scratch, flops, *args):
    return pl.pallas_call(
        body,
        out_shape=tuple(jax.ShapeDtypeStruct(shape, dtype) for shape, dtype in outs),
        in_specs=[pl.BlockSpec(memory_space=pltpu.VMEM) for _ in args],
        out_specs=tuple(pl.BlockSpec(memory_space=pltpu.VMEM) for _ in outs),
        scratch_shapes=[pltpu.VMEM(shape, dtype) for shape, dtype in scratch],
        compiler_params=pltpu.CompilerParams(vmem_limit_bytes=VMEM_BYTES),
        cost_estimate=pl.CostEstimate(flops=flops, bytes_accessed=1 << 20, transcendentals=0),
    )(*args)


def place_of():
    depth_at, row_at = lax.axis_index(GZ), lax.axis_index("gy")
    return (
        depth_at > 0,
        depth_at < lax.axis_size(GZ) - 1,
        row_at > 0,
        row_at < lax.axis_size("gy") - 1,
        lax.axis_index("c"),
        row_at,
    )


def lanes(shape):
    return lax.broadcasted_iota(jnp.int32, shape, 1)


def at_column(tile, step):
    if step == 0:
        return tile
    moved = pltpu.roll(tile.astype(F32), (-step) % 128, 1)
    edge = 127 if step > 0 else 0
    return jnp.where(lanes(tile.shape) == edge, 0.0, moved).astype(BF16)


def put_shifts(shifts, row, layer, tile):
    for step in range(3):
        shifts[step, row : row + tile.shape[0], layer * 128 : layer * 128 + 128] = at_column(
            tile, step - 1
        )


def convolved(weights, shifts, rows, depth):
    total = None
    for down in range(3):
        for step in range(3):
            window = shifts[step, rows[0] : rows[1], down * 128 : (down + depth) * 128]
            tap = weights[down * 3 + step]
            term = jnp.dot(
                tap[:, : rows[1] - rows[0]], window, preferred_element_type=F32
            )
            total = term if total is None else total + term
    return total


def sigmoid(values):
    return 1.0 / (1.0 + jnp.exp(-values))


def slope(values):
    sig = sigmoid(values)
    return sig * (1.0 + values * (1.0 - sig))


def exact_dot(values, picks):
    high = values.astype(BF16)
    rest = values - high.astype(F32)
    middle = rest.astype(BF16)
    low = (rest - middle.astype(F32)).astype(BF16)
    total = jnp.dot(low, picks, preferred_element_type=F32)
    total = total + jnp.dot(middle, picks, preferred_element_type=F32)
    return total + jnp.dot(high, picks, preferred_element_type=F32)


def pair_columns(down):
    rows = lax.broadcasted_iota(jnp.int32, (128, 128), 0)
    columns = lax.broadcasted_iota(jnp.int32, (128, 128), 1)
    hit = (rows // 2 == columns) if down else (columns // 2 == rows)
    return jnp.where(hit, 0.125, 0.0).astype(BF16)


def pooled(first, second, channels, width):
    both = first + second
    blocks = both.shape[0] // (2 * channels)
    rows = []
    for block in range(blocks):
        start = 2 * block * channels
        rows.append(
            both[start : start + channels] + both[start + channels : start + 2 * channels]
        )
    summed = rows[0] if blocks == 1 else jnp.concatenate(rows, axis=0)
    mean = exact_dot(summed, pair_columns(True))
    return jnp.where(lanes(mean.shape) < width // 2, mean, 0.0)


def silu(values):
    return values * sigmoid(values)


def prepare(kernels, dims):
    def body(*refs):
        ins, outs, wide = refs[:4], refs[4:11], refs[11]
        for level, (rows, chans, feats) in enumerate(dims):
            source, taps = ins[level][...], outs[level]
            picks = (
                lax.broadcasted_iota(jnp.int32, (feats, 128), 0)
                == lax.broadcasted_iota(jnp.int32, (feats, 128), 1) % feats
            )
            spread = jnp.dot(
                source, jnp.where(picks, 1.0, 0.0).astype(BF16), preferred_element_type=F32
            )
            size = taps.shape[2]
            place = lanes((chans, 128)) // feats
            for down in range(3):
                for step in range(3):
                    wide[...] = jnp.zeros_like(wide)
                    for row in range(rows + 2):
                        value = jnp.zeros((chans, 128), F32)
                        for across in range(3):
                            at = ((down * 3 + across) * 3 + step) * chans
                            value = jnp.where(
                                place == row - across, spread[at : at + chans], value
                            )
                        wide[row * chans : (row + 1) * chans, :] = value
                    taps[down * 3 + step] = wide[:size, :].T.astype(BF16)
        for level in range(1, 4):
            rows, chans, feats = dims[level]
            if level == 2:
                rows = 4
            source, taps = ins[level][...], outs[3 + level]
            size = (rows + 2) * feats
            picks = (
                lax.broadcasted_iota(jnp.int32, (feats, size), 0)
                == lax.broadcasted_iota(jnp.int32, (feats, size), 1) % feats
            )
            spread = jnp.dot(
                source, jnp.where(picks, 1.0, 0.0).astype(BF16), preferred_element_type=F32
            )
            place = lanes((chans, size)) // feats
            for down in range(3):
                for step in range(3):
                    for row in range(rows):
                        value = jnp.zeros((chans, size), F32)
                        for across in range(3):
                            at = (((2 - down) * 3 + 2 - across) * 3 + 2 - step) * chans
                            value = jnp.where(
                                place == row + across, spread[at : at + chans], value
                            )
                        taps[down * 3 + step, row * chans : (row + 1) * chans, :] = (
                            value.astype(BF16)
                        )

    shapes = [(9, 128, 256), (9, 128, 128), (9, 128, 128), (9, 128, 256)]
    shapes += [(9, 64, 192), (9, 128, 384), (9, 64, 384)]
    flat = [kernel.reshape(-1, kernel.shape[-1]) for kernel in kernels]
    return call(body, [(s, BF16) for s in shapes], [((256, 128), F32)], 1 << 27, *flat)


def forward_full(volume, halo_z, halo_y, weights, skip_half, skip_deep):
    def body(own, one, two, above, below, taps, skip1, skip3, pre, act, shifts, to_one, to_two):
        even = lax.axis_index("c") == 0
        for layer in range(10):
            if 0 < layer < 9:
                parts = [part[layer * 16 : layer * 16 + 16] for part in (above, below)]
                parts.insert(1, own[layer - 1])
            else:
                near, far = (two, one) if layer == 0 else (one, two)
                at = (144, 0) if layer == 0 else (0, 144)
                parts = [
                    jnp.where(even, part[at[0] : at[0] + 16], part[at[1] : at[1] + 16])
                    for part in (above, below)
                ]
                parts.insert(1, jnp.where(even, near[0], far[0]))
            put_shifts(shifts, 0, layer, parts[0])
            put_shifts(shifts, 16, layer, parts[1])
            put_shifts(shifts, 144, layer, parts[2])
        value = convolved(taps, shifts, (0, 160), 8)
        active = silu(value)
        for layer in range(8):
            pre[layer] = value[:, layer * 128 : layer * 128 + 128]
        for layer in range(4):
            at = layer * 256
            act[layer] = pooled(
                active[:, at : at + 128], active[:, at + 128 : at + 256], 16, 128
            ).astype(BF16)
        for layer in range(3):
            rows = slice(layer * 64, layer * 64 + 64)
            to_one[rows] = jnp.where(even, act[layer + 1], act[layer])
            to_two[rows] = jnp.where(even, act[layer], act[layer + 1])
        to_one[192:320] = jnp.where(even, skip1[3], skip1[0])
        to_two[192:320] = jnp.where(even, skip1[0], skip1[3])
        to_one[320:] = skip3[...]
        to_two[320:] = skip3[...]

    outs = [((8, 128, 128), F32), ((4, 64, 128), BF16), ((3, 160, 1280), BF16)]
    outs += [((336, 128), BF16), ((336, 128), BF16)]
    return call(
        body, outs, [], 1 << 29, volume, *halo_z, *halo_y, weights, skip_half, skip_deep
    )


def forward_half(act, halo_z, halo_y, weights_half, weights_quarter):
    def body(
        own, one, two, above, below, taps, next_taps, pre, act, next_pre, deep, shifts, inner
    ):
        flags = place_of()
        even = flags[4] == 0
        for layer in range(10):
            if 3 <= layer < 7:
                at = layer * 48
                middle = own[layer - 3]
                edges = [part[at : at + 48] for part in (above, below)]
            else:
                near, far = (two, one) if layer < 3 else (one, two)
                at = layer % 7 * 64
                middle = jnp.where(even, near[at : at + 64], far[at : at + 64])
                at = layer % 7 * 48
                at = (336 + at, at) if layer < 3 else (at, 336 + at)
                edges = [
                    jnp.where(even, part[at[0] : at[0] + 48], part[at[1] : at[1] + 48])
                    for part in (above, below)
                ]
            put_shifts(shifts, 0, layer, edges[0])
            put_shifts(shifts, 48, layer, middle)
            put_shifts(shifts, 112, layer, edges[1])
        for part in range(2):
            value = convolved(taps, shifts, (part * 64, part * 64 + 96), 8)
            for layer in range(8):
                pre[layer, part * 128 : part * 128 + 128, :] = value[
                    :, layer * 128 : layer * 128 + 128
                ]
        row = lax.broadcasted_iota(jnp.int32, (128, 128), 0) // 32
        inside = (row > 0) | (flags[2])
        inside = inside & ((row < 3) | (flags[3]))
        for layer in range(4):
            value = pooled(silu(pre[2 * layer]), silu(pre[2 * layer + 1]), 32, 64)
            keep = inside
            if layer == 0:
                keep = keep & (flags[0])
            if layer == 3:
                keep = keep & (flags[1])
            value = jnp.where(keep, value, 0.0).astype(BF16)
            act[layer] = value
            put_shifts(inner, 0, layer, value)
        value = convolved(next_taps, inner, (0, 128), 2)
        next_pre[0] = value[:, :128]
        next_pre[1] = value[:, 128:]
        coarse = pooled(silu(value[:, :128]), silu(value[:, 128:]), 64, 32)
        dense = coarse[:8].astype(BF16).astype(F32)
        for group in range(1, 8):
            part = coarse[group * 8 : group * 8 + 8].astype(BF16).astype(F32)
            dense = dense + pltpu.roll(part, group * 16, 1)
        deep[...] = dense

    outs = [
        ((8, 256, 128), F32),
        ((4, 128, 128), BF16),
        ((2, 128, 128), F32),
        ((8, 128), F32),
        ((3, 160, 1280), BF16),
    ]
    return call(
        body,
        outs,
        [((3, 128, 512), BF16)],
        1 << 29,
        act,
        *halo_z,
        *halo_y,
        weights_half,
        weights_quarter,
    )


def turned(tile, by):
    return tile if by % 128 == 0 else pltpu.roll(tile, by % 128, 1)


def near_cell(tile, layer_step, step):
    moved = turned(tile, -(16 * layer_step + step))
    column = lanes(tile.shape) % 16
    if step > 0:
        moved = jnp.where(column == 15, 0.0, moved)
    if step < 0:
        moved = jnp.where(column == 0, 0.0, moved)
    return moved.astype(BF16)


def columns_last(tile, start):
    width = tile.shape[0]
    column = lax.broadcasted_iota(jnp.int32, (width, 128), 0)
    picks = jnp.where(lanes((width, 128)) == column + start, 1.0, 0.0).astype(BF16)
    return lax.dot_general(tile, picks, (((0,), (0,)), ((), ())), preferred_element_type=F32)


def opened(dense, layer):
    parts = [turned(dense, 16 * layer - 16 * group) for group in range(8)]
    return jnp.concatenate(parts, axis=0)


def deepest(columns, acts, skip_deep, halo_z, halo_y, skip, pre, weights, weights_back):
    def body(
        acts, skip_own, skip_one, skip_two, skip_above, skip_below, skip, pre,
        taps, taps_back, dense_out, out, shifts, delta_own, deltas,
    ):
        flags = place_of()
        core, row_at = flags[4], flags[5]
        place = lanes((64, 128)) // 16

        def cells(position, row):
            return acts[position % 2 * columns + row, position // 2]

        for near in range(5):
            row = row_at + near - 2
            valid = (row >= 0) & (row < columns)
            row = jnp.clip(row, 0, columns - 1)
            value = jnp.zeros((64, 128), F32)
            for layer in range(5):
                dense = jnp.where(core == 0, cells(layer, row), cells(layer + 1, row))
                value = jnp.where(place == layer, opened(dense, layer), value)
            value = jnp.where(valid, value, 0.0)
            for down in range(3):
                for step in range(3):
                    shifts[down * 3 + step, near * 64 : near * 64 + 64, :] = near_cell(
                        value, down - 1, step - 1
                    )
        place = lanes((128, 128)) // 16
        for near in range(3):
            value = None
            for tap in range(9):
                window = shifts[tap, near * 64 : near * 64 + 192, :]
                term = jnp.dot(taps[tap][:, :192], window, preferred_element_type=F32)
                value = term if value is None else value + term
            upstream = jnp.zeros((128, 128), F32)
            for layer in range(3):
                if near != 1:
                    edge = (skip_above, skip_below)[near // 2]
                    at = 704 - layer * 16
                    dense = jnp.where(
                        core == 0, edge[at : at + 16], edge[1392 - at - 16 : 1392 - at]
                    )
                elif layer == 1:
                    dense = skip_own[...]
                else:
                    ends = (skip_two, skip_one) if layer == 0 else (skip_one, skip_two)
                    dense = jnp.where(core == 0, ends[0][320:], ends[1][320:])
                upstream = upstream + columns_last(dense, 16 * layer + 16)
            keep = (place == 2) | ((place == 1) & (flags[0])) | ((place == 3) & (flags[1]))
            if near != 1:
                keep = keep & (flags[2 + near // 2])
            change = jnp.where(keep, upstream * slope(value), 0.0).astype(BF16).astype(F32)
            if near == 1:
                delta_own[...] = jnp.where(place == 2, change, 0.0).astype(BF16)
            deltas[near * 128 : near * 128 + 128, :] = change
        carried = None
        for down in range(3):
            for step in range(3):
                window = near_cell(deltas[...], down - 1, step - 1)
                term = jnp.dot(
                    taps_back[down * 3 + step], window, preferred_element_type=F32
                )
                carried = term if carried is None else carried + term
        carried = exact_dot(turned(carried, -32), pair_columns(False))
        carried = jnp.concatenate([carried, carried], axis=0)
        dense = None
        for layer in range(2):
            wide = [columns_last(skip[layer, row], 0) for row in range(2)]
            change = (jnp.concatenate(wide, axis=0) + carried) * slope(pre[layer])
            change = jnp.where(lanes(change.shape) < 32, change, 0.0).astype(BF16)
            out[layer] = change
            change = change.astype(F32)
            dense = change if dense is None else dense + turned(change, 32)
        dense_out[0] = dense.astype(BF16)

    outs = [
        ((1, 128, 128), BF16),
        ((2, 128, 128), BF16),
        ((9, 320, 128), BF16),
        ((128, 128), BF16),
    ]
    scratch = [((384, 128), F32)]
    return call(
        body, outs, scratch, 1 << 28,
        acts, skip_deep, *halo_z, *halo_y, skip, pre, weights, weights_back,
    )


def grad_deepest(shifts, delta):
    def body(shifts, delta, grad):
        for tap in range(9):
            grad[tap * 192 : tap * 192 + 192, :] = lax.dot_general(
                shifts[tap, 64:256, :], delta[...], NT, preferred_element_type=F32
            )

    return call(body, [((1728, 128), F32)], [], 1 << 27, shifts, delta)[0]


def diagonal(product, rows, chans, feats):
    place = lanes((3 * chans, 128)) // feats
    value = product[: 3 * chans]
    for row in range(1, rows):
        value = jnp.where(place == row, product[row * chans : (row + 3) * chans], value)
    turn = 64
    while turn >= feats:
        value = value + pltpu.roll(value, turn, 1)
        turn //= 2
    return value


def packed(tall, groups):
    size = tall.shape[0] // groups
    place = lanes((size, 128)) // (128 // groups)
    value = tall[:size, :]
    for group in range(1, groups):
        value = jnp.where(place == group, tall[group * size : (group + 1) * size, :], value)
    return value


def put_grads(tall, shifts, rows, offset, depth, delta, dims):
    count, chans, feats = dims
    for down in range(3):
        for step in range(3):
            at = (offset + down) * 128
            product = lax.dot_general(
                shifts[step, rows[0] : rows[1], at : at + depth * 128],
                delta,
                NT,
                preferred_element_type=F32,
            )
            tap = (down * 3 + step) * 3 * chans
            tall[tap : tap + 3 * chans, :] = diagonal(product, count, chans, feats)


def grad_quarter_of(act, delta):
    def body(act, delta, grad, shifts, tall):
        for layer in range(4):
            put_shifts(shifts, 0, layer, act[layer])
        both = jnp.concatenate([delta[0], delta[1]], axis=1)
        put_grads(tall, shifts, (0, 128), 0, 2, both, (2, 32, 64))
        grad[...] = packed(tall, 2)

    scratch = [((3, 128, 512), BF16), ((864, 128), F32)]
    return call(body, [((432, 128), F32)], scratch, 1 << 28, act, delta)[0]


def back_rest(
    delta, halo_z, halo_y, skip_half, halo_zs, halo_ys, pre_half, skip_full, pre_full,
    weights_quarter, weights_half, shifts_half, shifts_full, deep_grad, quarter_grad,
):
    def body(
        own, one, two, above, below, skip1, one1, two1, above1, below1, pre1, skip0, pre0,
        taps2, taps1, shifts1, shifts0, grad3, grad2, out, moved2, moved1, delta1, delta0, tall, flat,
    ):
        flags = place_of()
        even = flags[4] == 0
        for layer in range(6):
            block = layer // 2
            if block == 1:
                tiles = (above[1], own[0], below[1])
            else:
                near, far = (two, one) if block == 0 else (one, two)
                tiles = (
                    jnp.where(even, above[2 - block], above[block]),
                    jnp.where(even, near[0], far[0]),
                    jnp.where(even, below[2 - block], below[block]),
                )
            for part, tile in enumerate(tiles):
                tile = turned(tile.astype(F32), -32 * (layer % 2))
                tile = jnp.where(lanes(tile.shape) < 32, tile, 0.0).astype(BF16)
                put_shifts(moved2, part * 128, layer, tile)
        value = convolved(taps2, moved2, (0, 384), 4)
        picks = pair_columns(False)
        row = lax.broadcasted_iota(jnp.int32, (192, 128), 0) // 32
        inside = lanes((192, 128)) < 64
        inside = inside & ((row > 0) | (flags[2])) & ((row < 5) | (flags[3]))
        for layer in range(6):
            if layer % 2 == 1 or layer == 0:
                at = (layer + 1) // 2 * 128
                carried = exact_dot(value[:, at : at + 128], picks)
                parts = [carried[part * 32 : part * 32 + 32] for part in (0, 1, 1, 2, 2, 3)]
                carried = jnp.concatenate(parts, axis=0)
            if 0 < layer < 5:
                at = 480 + layer * 32
                parts = [above1[at : at + 32], skip1[layer - 1], below1[at : at + 32]]
            else:
                near, far = (two1, one1) if layer == 0 else (one1, two1)
                at = (640, 480) if layer == 0 else (480, 640)
                parts = [
                    jnp.where(even, above1[at[0] : at[0] + 32], above1[at[1] : at[1] + 32]),
                    jnp.where(even, near[192:320], far[192:320]),
                    jnp.where(even, below1[at[0] : at[0] + 32], below1[at[1] : at[1] + 32]),
                ]
            skip = jnp.concatenate(parts, axis=0).astype(F32)
            change = (skip + carried) * slope(pre1[layer + 1, 32:224])
            keep = inside
            if layer == 0:
                keep = keep & (flags[0])
            if layer == 5:
                keep = keep & (flags[1])
            change = jnp.where(keep, change, 0.0).astype(BF16)
            put_shifts(moved1, 0, layer, change)
            if 0 < layer < 5:
                delta1[:, (layer - 1) * 128 : layer * 128] = change[32:160]
        value = convolved(taps1, moved1, (0, 192), 4)
        for layer in range(8):
            if layer % 2 == 0:
                at = layer // 2 * 128
                carried = exact_dot(value[:, at : at + 128], picks)
                parts = [carried[part // 2 * 16 : part // 2 * 16 + 16] for part in range(8)]
                carried = jnp.concatenate(parts, axis=0)
            change = (skip0[layer].astype(F32) + carried) * slope(pre0[layer])
            delta0[:, layer * 128 : layer * 128 + 128] = change.astype(BF16)
        flat[:1728, :] = grad3[...]
        flat[1728:2160, :] = grad2[...]
        tall[...] = jnp.zeros_like(tall)
        put_grads(tall, shifts1, (32, 128), 2, 4, delta1[...], (4, 16, 32))
        flat[2160:2272, :] = packed(tall, 4)
        put_grads(tall, shifts0, (0, 160), 0, 8, delta0[...], (8, 16, 16))
        flat[2272:2328, :] = packed(tall, 8)
        flat[2328:, :] = jnp.zeros((2560 - 2328, 128), F32)
        for part in range(5):
            at = part * 512
            out[:, part * 128 : part * 128 + 128] = flat[at : at + 512, :].astype(BF16)

    scratch = [
        ((3, 384, 768), BF16),
        ((3, 192, 768), BF16),
        ((128, 512), BF16),
        ((128, 1024), BF16),
        ((448, 128), F32),
        ((2560, 128), F32),
    ]
    return call(
        body, [((512, 640), BF16)], scratch, 1 << 30,
        delta, *halo_z, *halo_y, skip_half, *halo_zs, *halo_ys, pre_half, skip_full, pre_full,
        weights_quarter, weights_half, shifts_half, shifts_full, deep_grad, quarter_grad,
    )[0]


def unpack(sums):
    def body(sums, full, half, quarter, eighth, whole, tall):
        for part in range(5):
            block = sums[:, part * 128 : part * 128 + 128]
            whole[part * 512 : part * 512 + 512, :] = block.astype(F32)

        def spread(out, source, chans):
            for down in range(3):
                for across in range(3):
                    for step in range(3):
                        at = ((down * 3 + across) * 3 + step) * chans
                        start = ((down * 3 + step) * 3 + across) * chans
                        out[at : at + chans, :] = source[
                            start : start + chans, : out.shape[1]
                        ]

        spread(eighth, whole, 64)
        for out, start, size, groups, chans in (
            (quarter, 1728, 432, 2, 32),
            (half, 2160, 112, 4, 16),
            (full, 2272, 56, 8, 16),
        ):
            dense = whole[start : start + size, :]
            for group in range(groups):
                tall[group * size : (group + 1) * size, :] = (
                    dense if group == 0 else pltpu.roll(dense, 128 - group * (128 // groups), 1)
                )
            spread(out, tall, chans)

    outs = [((432, 16), F32), ((432, 32), F32), ((864, 64), F32), ((1728, 128), F32)]
    scratch = [((2560, 128), F32), ((864, 128), F32)]
    return call(body, outs, scratch, 1 << 20, sums)


def exchange(first, last, axis):
    size = lax.axis_size(axis)
    up = [(i, i + 1) for i in range(size - 1)]
    down = [(i + 1, i) for i in range(size - 1)]
    return lax.ppermute(last, axis, up), lax.ppermute(first, axis, down)


def swaps(to_one, to_two):
    size = lax.axis_size(GZ)
    on_chip = [(i, i ^ 1) for i in range(size)]
    between = [(i, i + 1) for i in range(1, size - 1, 2)]
    between += [(j, i) for i, j in between]
    return lax.ppermute(to_one, GZ, on_chip), lax.ppermute(to_two, GZ, between)


def laid_out(array):
    chans, depth, height, width = array.shape
    rows = jnp.transpose(array, (1, 2, 0, 3)).reshape(depth, height * chans, width)
    return jnp.pad(rows, ((0, 0), (0, 0), (0, 128 - width)))


def copies(part, count):
    def body(part, out):
        value = part[...].astype(BF16)
        for copy in range(count):
            out[copy] = value

    return call(body, [((count,) + part.shape, BF16)], [], 1 << 20, part)[0]


def summed(terms):
    inner, outer = ("x", "c"), ("z", "gy")
    first, second = lax.axis_size(inner), lax.axis_size(outer)
    rows, width = terms.shape[0] // first, terms.shape[1]
    pieces = lax.all_to_all(terms.reshape(first, rows, width), inner, 0, 0)
    part = jnp.sum(pieces.astype(F32), axis=0)
    pieces = lax.all_to_all(part, outer, 0, 0, tiled=True)
    done = jnp.sum(pieces.reshape(second, -1, width), axis=0)
    spread = jnp.broadcast_to(done[None], (second,) + done.shape).reshape(rows, width)
    part = lax.all_to_all(lax.optimization_barrier(spread), outer, 0, 0, tiled=True)
    return lax.all_to_all(copies(part, first), inner, 0, 0).reshape(terms.shape)


def on_device(
    volume,
    kernel_full,
    kernel_half,
    kernel_quarter,
    kernel_eighth,
    skip_full,
    skip_half,
    skip_quarter,
    skip_eighth,
):
    kernels = (kernel_full, kernel_half, kernel_quarter, kernel_eighth)
    volume = laid_out(volume)
    even = lax.axis_index("c") == 0
    first, last = volume[:1], volume[7:]
    one, two = swaps(jnp.where(even, last, first), jnp.where(even, first, last))
    skip3 = jnp.transpose(skip_eighth, (1, 2, 3, 0)).reshape(16, 128)
    skip2 = jnp.transpose(skip_quarter, (1, 2, 3, 0))
    one, two, skip0, skip1, kernels = lax.optimization_barrier(
        (one, two, laid_out(skip_full), laid_out(skip_half), kernels)
    )

    def flat(parts):
        return jnp.concatenate([part.reshape(-1, 128) for part in parts], axis=0)

    def edge(start):
        return flat([part[:, start : start + 16] for part in (one, volume, two)])

    halo_y = exchange(edge(0), edge(112), "gy")
    dims = ((8, 16, 16), (4, 16, 32), (2, 32, 64), (1, 64, 128))
    w0, w1, w2, w3, t1, t2, t3 = prepare(kernels, dims)
    pre0, act1, shifts0, to_one, to_two = forward_full(
        volume, (one, two), halo_y, w0, skip1, skip3
    )
    halo_z1 = one, two = swaps(to_one, to_two)

    def edge1(start, start1):
        acts = [part[:192].reshape(3, 64, 128) for part in (one, two)]
        acts.insert(1, act1)
        rims = [part[192:320].reshape(1, 128, 128) for part in (one, two)]
        rims.insert(1, skip1)
        parts = [part[:, start : start + 48] for part in acts]
        parts += [part[:, start1 : start1 + 32] for part in rims]
        return flat(parts + [one[320:], skip3, two[320:]])

    halo_y1 = exchange(edge1(0, 0), edge1(16, 96), "gy")
    pre1, act2, pre2, act3, shifts1 = forward_half(act1, halo_z1, halo_y1, w1, w2)
    columns = lax.axis_size("gy")
    before, after = exchange(act3, act3, ("x", "z"))
    chips = jnp.stack([before, act3, after])
    many = (2 * columns,) + chips.shape
    acts = lax.all_to_all(
        lax.optimization_barrier(jnp.broadcast_to(chips[None], many)), ("c", "gy"), 0, 0
    )
    dense2, delta2, shifts3, delta3 = deepest(
        columns, acts, skip3, halo_z1, halo_y1, skip2, pre2, w3, t3
    )
    halo_z = one, two = swaps(dense2, dense2)
    block = jnp.concatenate([one, dense2, two], axis=0)
    halo_y = exchange(block, block, "gy")
    grad3 = grad_deepest(shifts3, delta3)
    grad2 = grad_quarter_of(act2, delta2)
    terms = back_rest(
        dense2, halo_z, halo_y, skip1, halo_z1, halo_y1, pre1, skip0, pre0,
        t2, t1, shifts1, shifts0, grad3, grad2,
    )
    outs = unpack(summed(terms))
    return tuple(out.reshape(kernel.shape) for out, kernel in zip(outs, kernels))


def solution(mesh):
    fine = jax.sharding.Mesh(mesh.devices.reshape(4, 8, 2, 8), ("x", "z", "c", "gy"))
    return mapped(fine)


def mapped(fine):
    block = P(None, GZ, "gy", None)
    return jax.shard_map(
        on_device,
        mesh=fine,
        in_specs=(block, P(), P(), P(), P(), block, block, block, block),
        out_specs=(P(), P(), P(), P()),
        check_vma=False,
    )
```

```python
import jax
import jax.numpy as jnp
from jax import lax
from jax.experimental import pallas as pl
from jax.experimental.pallas import tpu as pltpu
from jax.sharding import PartitionSpec as P

F32 = jnp.float32
BF16 = jnp.bfloat16
GZ = ("x", "z", "c")
VMEM_BYTES = 14 * 1024 * 1024
NT = (((1,), (1,)), ((), ()))


def call(body, outs, scratch, flops, *args):
    return pl.pallas_call(
        body,
        out_shape=tuple(jax.ShapeDtypeStruct(shape, dtype) for shape, dtype in outs),
        in_specs=[pl.BlockSpec(memory_space=pltpu.VMEM) for _ in args],
        out_specs=tuple(pl.BlockSpec(memory_space=pltpu.VMEM) for _ in outs),
        scratch_shapes=[pltpu.VMEM(shape, dtype) for shape, dtype in scratch],
        compiler_params=pltpu.CompilerParams(vmem_limit_bytes=VMEM_BYTES),
        cost_estimate=pl.CostEstimate(flops=flops, bytes_accessed=1 << 20, transcendentals=0),
    )(*args)


def place_of():
    depth_at, row_at = lax.axis_index(GZ), lax.axis_index("gy")
    return (
        depth_at > 0,
        depth_at < lax.axis_size(GZ) - 1,
        row_at > 0,
        row_at < lax.axis_size("gy") - 1,
        lax.axis_index("c"),
        row_at,
    )


def row_edges(first, second, start, size):
    rule = lax.axis_index("gy") % 2 == 0
    one, two = (part[start : start + size].astype(F32) for part in (first, second))
    return jnp.where(rule, two, one).astype(BF16), jnp.where(rule, one, two).astype(BF16)


def half_lanes(tile, odd):
    tile = pltpu.roll(tile.astype(F32), 64, 1) if odd else tile.astype(F32)
    return jnp.where(lanes(tile.shape) < 64, tile, 0.0).astype(BF16)


def lanes(shape):
    return lax.broadcasted_iota(jnp.int32, shape, 1)


def at_column(tile, step):
    if step == 0:
        return tile
    moved = pltpu.roll(tile.astype(F32), (-step) % 128, 1)
    edge = 127 if step > 0 else 0
    return jnp.where(lanes(tile.shape) == edge, 0.0, moved).astype(BF16)


def put_shifts(shifts, row, layer, tile):
    for step in range(3):
        shifts[step, row : row + tile.shape[0], layer * 128 : layer * 128 + 128] = at_column(
            tile, step - 1
        )


def convolved(weights, shifts, rows, depth):
    total = None
    for down in range(3):
        for step in range(3):
            window = shifts[step, rows[0] : rows[1], down * 128 : (down + depth) * 128]
            tap = weights[down * 3 + step]
            term = jnp.dot(
                tap[:, : rows[1] - rows[0]], window, preferred_element_type=F32
            )
            total = term if total is None else total + term
    return total


def sigmoid(values):
    return 1.0 / (1.0 + jnp.exp(-values))


def slope(values):
    sig = sigmoid(values)
    return sig * (1.0 + values * (1.0 - sig))


def exact_dot(values, picks):
    high = values.astype(BF16)
    rest = values - high.astype(F32)
    middle = rest.astype(BF16)
    low = (rest - middle.astype(F32)).astype(BF16)
    total = jnp.dot(low, picks, preferred_element_type=F32)
    total = total + jnp.dot(middle, picks, preferred_element_type=F32)
    return total + jnp.dot(high, picks, preferred_element_type=F32)


def pair_columns(down):
    rows = lax.broadcasted_iota(jnp.int32, (128, 128), 0)
    columns = lax.broadcasted_iota(jnp.int32, (128, 128), 1)
    hit = (rows // 2 == columns) if down else (columns // 2 == rows)
    return jnp.where(hit, 0.125, 0.0).astype(BF16)


def pooled(first, second, channels, width):
    both = first + second
    blocks = both.shape[0] // (2 * channels)
    rows = []
    for block in range(blocks):
        start = 2 * block * channels
        rows.append(
            both[start : start + channels] + both[start + channels : start + 2 * channels]
        )
    summed = rows[0] if blocks == 1 else jnp.concatenate(rows, axis=0)
    mean = exact_dot(summed, pair_columns(True))
    return jnp.where(lanes(mean.shape) < width // 2, mean, 0.0)


def silu(values):
    return values * sigmoid(values)


def prepare(kernels, dims):
    def body(*refs):
        ins, outs, wide = refs[:4], refs[4:11], refs[11]
        for level, (rows, chans, feats) in enumerate(dims):
            source, taps = ins[level][...], outs[level]
            picks = (
                lax.broadcasted_iota(jnp.int32, (feats, 128), 0)
                == lax.broadcasted_iota(jnp.int32, (feats, 128), 1) % feats
            )
            spread = jnp.dot(
                source, jnp.where(picks, 1.0, 0.0).astype(BF16), preferred_element_type=F32
            )
            size = taps.shape[2]
            place = lanes((chans, 128)) // feats
            for down in range(3):
                for step in range(3):
                    wide[...] = jnp.zeros_like(wide)
                    for row in range(rows + 2):
                        value = jnp.zeros((chans, 128), F32)
                        for across in range(3):
                            at = ((down * 3 + across) * 3 + step) * chans
                            value = jnp.where(
                                place == row - across, spread[at : at + chans], value
                            )
                        wide[row * chans : (row + 1) * chans, :] = value
                    taps[down * 3 + step] = wide[:size, :].T.astype(BF16)
        for level in range(1, 4):
            rows, chans, feats = dims[level]
            if level == 2:
                rows = 4
            source, taps = ins[level][...], outs[3 + level]
            size = (rows + 2) * feats
            picks = (
                lax.broadcasted_iota(jnp.int32, (feats, size), 0)
                == lax.broadcasted_iota(jnp.int32, (feats, size), 1) % feats
            )
            spread = jnp.dot(
                source, jnp.where(picks, 1.0, 0.0).astype(BF16), preferred_element_type=F32
            )
            place = lanes((chans, size)) // feats
            for down in range(3):
                for step in range(3):
                    for row in range(rows):
                        value = jnp.zeros((chans, size), F32)
                        for across in range(3):
                            at = (((2 - down) * 3 + 2 - across) * 3 + 2 - step) * chans
                            value = jnp.where(
                                place == row + across, spread[at : at + chans], value
                            )
                        taps[down * 3 + step, row * chans : (row + 1) * chans, :] = (
                            value.astype(BF16)
                        )

    shapes = [(9, 128, 256), (9, 128, 128), (9, 128, 128), (9, 128, 256)]
    shapes += [(9, 64, 192), (9, 128, 384), (9, 64, 384)]
    flat = [kernel.reshape(-1, kernel.shape[-1]) for kernel in kernels]
    return call(body, [(s, BF16) for s in shapes], [((256, 128), F32)], 1 << 27, *flat)


def forward_full(volume, halo_z, halo_y, weights, skip_half, skip_deep):
    def body(own, one, two, above, below, taps, skip1, skip3, pre, act, shifts, to_one, to_two):
        even = lax.axis_index("c") == 0
        for layer in range(10):
            if 0 < layer < 9:
                high, low = row_edges(above, below, layer * 16, 16)
                middle = own[layer - 1]
            else:
                near, far = (two, one) if layer == 0 else (one, two)
                at = (144, 0) if layer == 0 else (0, 144)
                yes, no = (row_edges(above, below, start, 16) for start in at)
                high, low = (jnp.where(even, yes[part], no[part]) for part in range(2))
                middle = jnp.where(even, near[0], far[0])
            parts = (high, middle, low)
            put_shifts(shifts, 0, layer, parts[0])
            put_shifts(shifts, 16, layer, parts[1])
            put_shifts(shifts, 144, layer, parts[2])
        value = convolved(taps, shifts, (0, 160), 8)
        active = silu(value)
        for layer in range(8):
            pre[layer] = value[:, layer * 128 : layer * 128 + 128]
        for layer in range(4):
            at = layer * 256
            act[layer] = pooled(
                active[:, at : at + 128], active[:, at + 128 : at + 256], 16, 128
            ).astype(BF16)
        for layer in range(3):
            rows = slice(layer * 64, layer * 64 + 64)
            to_one[rows] = jnp.where(even, act[layer + 1], act[layer])
            to_two[rows] = jnp.where(even, act[layer], act[layer + 1])
        to_one[192:320] = jnp.where(even, skip1[3], skip1[0])
        to_two[192:320] = jnp.where(even, skip1[0], skip1[3])
        to_one[320:] = skip3[...]
        to_two[320:] = skip3[...]

    outs = [((8, 128, 128), F32), ((4, 64, 128), BF16), ((3, 160, 1280), BF16)]
    outs += [((336, 128), BF16), ((336, 128), BF16)]
    return call(
        body, outs, [], 1 << 29, volume, *halo_z, *halo_y, weights, skip_half, skip_deep
    )


def forward_half(act, halo_z, halo_y, weights_half, weights_quarter):
    def body(
        own, one, two, above, below, taps, next_taps, pre, act, next_pre, deep, shifts, inner
    ):
        flags = place_of()
        even = flags[4] == 0
        def edge_at(place):
            found = row_edges(above, below, place // 2 * 48, 48)
            return [half_lanes(part, place % 2) for part in found]

        for layer in range(10):
            if 3 <= layer < 7:
                middle = own[layer - 3]
                edges = edge_at(layer)
            else:
                near, far = (two, one) if layer < 3 else (one, two)
                at = layer % 7 * 64
                middle = jnp.where(even, near[at : at + 64], far[at : at + 64])
                at = layer % 7
                yes, no = (edge_at(place) for place in ((7 + at, at) if layer < 3 else (at, 7 + at)))
                edges = [jnp.where(even, yes[part], no[part]) for part in range(2)]
            put_shifts(shifts, 0, layer, edges[0])
            put_shifts(shifts, 48, layer, middle)
            put_shifts(shifts, 112, layer, edges[1])
        for part in range(2):
            value = convolved(taps, shifts, (part * 64, part * 64 + 96), 8)
            for layer in range(8):
                pre[layer, part * 128 : part * 128 + 128, :] = value[
                    :, layer * 128 : layer * 128 + 128
                ]
        row = lax.broadcasted_iota(jnp.int32, (128, 128), 0) // 32
        inside = (row > 0) | (flags[2])
        inside = inside & ((row < 3) | (flags[3]))
        for layer in range(4):
            value = pooled(silu(pre[2 * layer]), silu(pre[2 * layer + 1]), 32, 64)
            keep = inside
            if layer == 0:
                keep = keep & (flags[0])
            if layer == 3:
                keep = keep & (flags[1])
            value = jnp.where(keep, value, 0.0).astype(BF16)
            act[layer] = value
            put_shifts(inner, 0, layer, value)
        value = convolved(next_taps, inner, (0, 128), 2)
        next_pre[0] = value[:, :128]
        next_pre[1] = value[:, 128:]
        coarse = pooled(silu(value[:, :128]), silu(value[:, 128:]), 64, 32)
        dense = coarse[:8].astype(BF16).astype(F32)
        for group in range(1, 8):
            part = coarse[group * 8 : group * 8 + 8].astype(BF16).astype(F32)
            dense = dense + pltpu.roll(part, group * 16, 1)
        deep[...] = dense

    outs = [
        ((8, 256, 128), F32),
        ((4, 128, 128), BF16),
        ((2, 128, 128), F32),
        ((8, 128), F32),
        ((3, 160, 1280), BF16),
    ]
    return call(
        body,
        outs,
        [((3, 128, 512), BF16)],
        1 << 29,
        act,
        *halo_z,
        *halo_y,
        weights_half,
        weights_quarter,
    )


def turned(tile, by):
    return tile if by % 128 == 0 else pltpu.roll(tile, by % 128, 1)


def near_cell(tile, layer_step, step):
    moved = turned(tile, -(16 * layer_step + step))
    column = lanes(tile.shape) % 16
    if step > 0:
        moved = jnp.where(column == 15, 0.0, moved)
    if step < 0:
        moved = jnp.where(column == 0, 0.0, moved)
    return moved.astype(BF16)


def columns_last(tile, start):
    width = tile.shape[0]
    column = lax.broadcasted_iota(jnp.int32, (width, 128), 0)
    picks = jnp.where(lanes((width, 128)) == column + start, 1.0, 0.0).astype(BF16)
    return lax.dot_general(tile, picks, (((0,), (0,)), ((), ())), preferred_element_type=F32)


def opened(dense, layer):
    parts = [turned(dense, 16 * layer - 16 * group) for group in range(8)]
    return jnp.concatenate(parts, axis=0)


def deepest(columns, acts, chips, skip_deep, halo_z, halo_y, skip, pre, weights, weights_back):
    def body(
        acts, chip_one, chip_two, skip_own, skip_one, skip_two, skip_above, skip_below, skip, pre,
        taps, taps_back, dense_out, out, shifts, delta_own, deltas,
    ):
        flags = place_of()
        core, row_at = flags[4], flags[5]
        place = lanes((64, 128)) // 16

        ahead = lax.axis_index("z") % 2 == 0

        def cells(position, row):
            at = position % 2 * columns + row
            if position // 2 == 1:
                return acts[at]
            if position // 2 == 0:
                return jnp.where(ahead, chip_two[at], chip_one[at])
            return jnp.where(ahead, chip_one[at], chip_two[at])

        for near in range(5):
            row = row_at + near - 2
            valid = (row >= 0) & (row < columns)
            row = jnp.clip(row, 0, columns - 1)
            value = jnp.zeros((64, 128), F32)
            for layer in range(5):
                dense = jnp.where(core == 0, cells(layer, row), cells(layer + 1, row))
                value = jnp.where(place == layer, opened(dense, layer), value)
            value = jnp.where(valid, value, 0.0)
            for down in range(3):
                for step in range(3):
                    shifts[down * 3 + step, near * 64 : near * 64 + 64, :] = near_cell(
                        value, down - 1, step - 1
                    )
        place = lanes((128, 128)) // 16
        for near in range(3):
            value = None
            for tap in range(9):
                window = shifts[tap, near * 64 : near * 64 + 192, :]
                term = jnp.dot(taps[tap][:, :192], window, preferred_element_type=F32)
                value = term if value is None else value + term
            upstream = jnp.zeros((128, 128), F32)
            for layer in range(3):
                if near != 1:
                    yes = row_edges(skip_above, skip_below, 368 - layer * 16, 16)[near // 2]
                    no = row_edges(skip_above, skip_below, 336 + layer * 16, 16)[near // 2]
                    dense = jnp.where(core == 0, yes, no)
                elif layer == 1:
                    dense = skip_own[...]
                else:
                    ends = (skip_two, skip_one) if layer == 0 else (skip_one, skip_two)
                    dense = jnp.where(core == 0, ends[0][320:], ends[1][320:])
                upstream = upstream + columns_last(dense, 16 * layer + 16)
            keep = (place == 2) | ((place == 1) & (flags[0])) | ((place == 3) & (flags[1]))
            if near != 1:
                keep = keep & (flags[2 + near // 2])
            change = jnp.where(keep, upstream * slope(value), 0.0).astype(BF16).astype(F32)
            if near == 1:
                delta_own[...] = jnp.where(place == 2, change, 0.0).astype(BF16)
            deltas[near * 128 : near * 128 + 128, :] = change
        carried = None
        for down in range(3):
            for step in range(3):
                window = near_cell(deltas[...], down - 1, step - 1)
                term = jnp.dot(
                    taps_back[down * 3 + step], window, preferred_element_type=F32
                )
                carried = term if carried is None else carried + term
        carried = exact_dot(turned(carried, -32), pair_columns(False))
        carried = jnp.concatenate([carried, carried], axis=0)
        dense = None
        for layer in range(2):
            wide = [columns_last(skip[layer, row], 0) for row in range(2)]
            change = (jnp.concatenate(wide, axis=0) + carried) * slope(pre[layer])
            change = jnp.where(lanes(change.shape) < 32, change, 0.0).astype(BF16)
            out[layer] = change
            change = change.astype(F32)
            dense = change if dense is None else dense + turned(change, 32)
        dense_out[0] = dense.astype(BF16)

    outs = [
        ((1, 128, 128), BF16),
        ((2, 128, 128), BF16),
        ((9, 320, 128), BF16),
        ((128, 128), BF16),
    ]
    scratch = [((384, 128), F32)]
    return call(
        body, outs, scratch, 1 << 28,
        acts, *chips, skip_deep, *halo_z, *halo_y, skip, pre, weights, weights_back,
    )


def grad_deepest(shifts, delta):
    def body(shifts, delta, grad):
        for tap in range(9):
            grad[tap * 192 : tap * 192 + 192, :] = lax.dot_general(
                shifts[tap, 64:256, :], delta[...], NT, preferred_element_type=F32
            )

    return call(body, [((1728, 128), F32)], [], 1 << 27, shifts, delta)[0]


def diagonal(product, rows, chans, feats):
    place = lanes((3 * chans, 128)) // feats
    value = product[: 3 * chans]
    for row in range(1, rows):
        value = jnp.where(place == row, product[row * chans : (row + 3) * chans], value)
    turn = 64
    while turn >= feats:
        value = value + pltpu.roll(value, turn, 1)
        turn //= 2
    return value


def packed(tall, groups):
    size = tall.shape[0] // groups
    place = lanes((size, 128)) // (128 // groups)
    value = tall[:size, :]
    for group in range(1, groups):
        value = jnp.where(place == group, tall[group * size : (group + 1) * size, :], value)
    return value


def put_grads(tall, shifts, rows, offset, depth, delta, dims):
    count, chans, feats = dims
    for down in range(3):
        for step in range(3):
            at = (offset + down) * 128
            product = lax.dot_general(
                shifts[step, rows[0] : rows[1], at : at + depth * 128],
                delta,
                NT,
                preferred_element_type=F32,
            )
            tap = (down * 3 + step) * 3 * chans
            tall[tap : tap + 3 * chans, :] = diagonal(product, count, chans, feats)


def grad_quarter_of(act, delta):
    def body(act, delta, grad, shifts, tall):
        for layer in range(4):
            put_shifts(shifts, 0, layer, act[layer])
        both = jnp.concatenate([delta[0], delta[1]], axis=1)
        put_grads(tall, shifts, (0, 128), 0, 2, both, (2, 32, 64))
        grad[...] = packed(tall, 2)

    scratch = [((3, 128, 512), BF16), ((864, 128), F32)]
    return call(body, [((432, 128), F32)], scratch, 1 << 28, act, delta)[0]


def back_rest(
    delta, halo_z, halo_y, skip_half, halo_zs, halo_ys, pre_half, skip_full, pre_full,
    weights_quarter, weights_half, shifts_half, shifts_full, deep_grad, quarter_grad,
):
    def body(
        own, one, two, above, below, skip1, one1, two1, above1, below1, pre1, skip0, pre0,
        taps2, taps1, shifts1, shifts0, grad3, grad2, out, moved2, moved1, delta1, delta0, tall, flat,
    ):
        flags = place_of()
        even = flags[4] == 0
        for layer in range(6):
            block = layer // 2
            high, low = row_edges(above, below, block * 128, 128)
            middle = own[0]
            if block != 1:
                near, far = (two, one) if block == 0 else (one, two)
                middle = jnp.where(even, near[0], far[0])
                other = row_edges(above, below, (2 - block) * 128, 128)
                high, low = jnp.where(even, other[0], high), jnp.where(even, other[1], low)
            tiles = (high, middle, low)
            for part, tile in enumerate(tiles):
                tile = turned(tile.astype(F32), -32 * (layer % 2))
                tile = jnp.where(lanes(tile.shape) < 32, tile, 0.0).astype(BF16)
                put_shifts(moved2, part * 128, layer, tile)
        value = convolved(taps2, moved2, (0, 384), 4)

        def edge_at(place):
            found = row_edges(above1, below1, 240 + place // 2 * 32, 32)
            return [half_lanes(part, place % 2) for part in found]

        picks = pair_columns(False)
        row = lax.broadcasted_iota(jnp.int32, (192, 128), 0) // 32
        inside = lanes((192, 128)) < 64
        inside = inside & ((row > 0) | (flags[2])) & ((row < 5) | (flags[3]))
        for layer in range(6):
            if layer % 2 == 1 or layer == 0:
                at = (layer + 1) // 2 * 128
                carried = exact_dot(value[:, at : at + 128], picks)
                parts = [carried[part * 32 : part * 32 + 32] for part in (0, 1, 1, 2, 2, 3)]
                carried = jnp.concatenate(parts, axis=0)
            if 0 < layer < 5:
                high, low = edge_at(layer)
                middle = skip1[layer - 1]
            else:
                near, far = (two1, one1) if layer == 0 else (one1, two1)
                yes, no = edge_at(5 - layer), edge_at(layer)
                high, low = (jnp.where(even, yes[part], no[part]) for part in range(2))
                middle = jnp.where(even, near[192:320], far[192:320])
            parts = (high, middle, low)
            skip = jnp.concatenate(parts, axis=0).astype(F32)
            change = (skip + carried) * slope(pre1[layer + 1, 32:224])
            keep = inside
            if layer == 0:
                keep = keep & (flags[0])
            if layer == 5:
                keep = keep & (flags[1])
            change = jnp.where(keep, change, 0.0).astype(BF16)
            put_shifts(moved1, 0, layer, change)
            if 0 < layer < 5:
                delta1[:, (layer - 1) * 128 : layer * 128] = change[32:160]
        value = convolved(taps1, moved1, (0, 192), 4)
        for layer in range(8):
            if layer % 2 == 0:
                at = layer // 2 * 128
                carried = exact_dot(value[:, at : at + 128], picks)
                parts = [carried[part // 2 * 16 : part // 2 * 16 + 16] for part in range(8)]
                carried = jnp.concatenate(parts, axis=0)
            change = (skip0[layer].astype(F32) + carried) * slope(pre0[layer])
            delta0[:, layer * 128 : layer * 128 + 128] = change.astype(BF16)
        flat[:1728, :] = grad3[...]
        flat[1728:2160, :] = grad2[...]
        tall[...] = jnp.zeros_like(tall)
        put_grads(tall, shifts1, (32, 128), 2, 4, delta1[...], (4, 16, 32))
        flat[2160:2272, :] = packed(tall, 4)
        put_grads(tall, shifts0, (0, 160), 0, 8, delta0[...], (8, 16, 16))
        flat[2272:2328, :] = packed(tall, 8)
        flat[2328:, :] = jnp.zeros((2560 - 2328, 128), F32)
        for part in range(5):
            at = part * 512
            out[:, part * 128 : part * 128 + 128] = flat[at : at + 512, :].astype(BF16)

    scratch = [
        ((3, 384, 768), BF16),
        ((3, 192, 768), BF16),
        ((128, 512), BF16),
        ((128, 1024), BF16),
        ((448, 128), F32),
        ((2560, 128), F32),
    ]
    return call(
        body, [((512, 640), BF16)], scratch, 1 << 30,
        delta, *halo_z, *halo_y, skip_half, *halo_zs, *halo_ys, pre_half, skip_full, pre_full,
        weights_quarter, weights_half, shifts_half, shifts_full, deep_grad, quarter_grad,
    )[0]


def unpack(sums):
    def body(sums, full, half, quarter, eighth, whole, tall):
        for part in range(5):
            block = sums[:, part * 128 : part * 128 + 128]
            whole[part * 512 : part * 512 + 512, :] = block.astype(F32)

        def spread(out, source, chans):
            for down in range(3):
                for across in range(3):
                    for step in range(3):
                        at = ((down * 3 + across) * 3 + step) * chans
                        start = ((down * 3 + step) * 3 + across) * chans
                        out[at : at + chans, :] = source[
                            start : start + chans, : out.shape[1]
                        ]

        spread(eighth, whole, 64)
        for out, start, size, groups, chans in (
            (quarter, 1728, 432, 2, 32),
            (half, 2160, 112, 4, 16),
            (full, 2272, 56, 8, 16),
        ):
            dense = whole[start : start + size, :]
            for group in range(groups):
                tall[group * size : (group + 1) * size, :] = (
                    dense if group == 0 else pltpu.roll(dense, 128 - group * (128 // groups), 1)
                )
            spread(out, tall, chans)

    outs = [((432, 16), F32), ((432, 32), F32), ((864, 64), F32), ((1728, 128), F32)]
    scratch = [((2560, 128), F32), ((864, 128), F32)]
    return call(body, outs, scratch, 1 << 20, sums)


def pairs(axis):
    size = lax.axis_size(axis)
    between = [(i, i + 1) for i in range(1, size - 1, 2)]
    return [(i, i ^ 1) for i in range(size)], between + [(j, i) for i, j in between]


def swaps(to_one, to_two, axis=GZ):
    first, second = pairs(axis)
    return lax.ppermute(to_one, axis, first), lax.ppermute(to_two, axis, second)


def edge_rows(one, two, volume):
    def body(one, two, own, to_one, to_two):
        even = lax.axis_index("gy") % 2 == 0
        for place in range(10):
            block = one[0] if place == 0 else two[0] if place == 9 else own[place - 1]
            at = place * 16
            to_one[at : at + 16] = jnp.where(even, block[112:], block[:16])
            to_two[at : at + 16] = jnp.where(even, block[:16], block[112:])

    return call(body, [((160, 128), BF16)] * 2, [], 1 << 20, one, two, volume)


def edge_rows_half(one, two, act, skip_half, skip_deep):
    def body(one, two, act, skip1, skip3, to_one, to_two):
        even = lax.axis_index("gy") % 2 == 0

        def put(at, size, blocks):
            low, high = blocks
            packed_rows = []
            for rows in (slice(0, size), slice(low.shape[0] - size, low.shape[0])):
                packed_rows.append(
                    low[rows].astype(F32) + pltpu.roll(high[rows].astype(F32), 64, 1)
                )
            top, bottom = packed_rows
            to_one[at : at + size] = jnp.where(even, bottom, top).astype(BF16)
            to_two[at : at + size] = jnp.where(even, top, bottom).astype(BF16)

        def act_at(place):
            if 3 <= place < 7:
                return act[place - 3]
            at = place % 7 * 64
            return (one if place < 3 else two)[at : at + 64]

        def skip_at(place):
            if 0 < place < 5:
                return skip1[place - 1]
            return (one if place == 0 else two)[192:320]

        for pair in range(5):
            put(pair * 48, 48, (act_at(2 * pair), act_at(2 * pair + 1)))
        for pair in range(3):
            put(240 + pair * 32, 32, (skip_at(2 * pair), skip_at(2 * pair + 1)))
        for place, rows in enumerate((one[320:], skip3[...], two[320:])):
            at = 336 + place * 16
            to_one[at : at + 16] = rows
            to_two[at : at + 16] = rows

    return call(
        body, [((384, 128), BF16)] * 2, [], 1 << 20, one, two, act, skip_half, skip_deep
    )


def laid_out(array):
    chans, depth, height, width = array.shape
    rows = jnp.transpose(array, (1, 2, 0, 3)).reshape(depth, height * chans, width)
    return jnp.pad(rows, ((0, 0), (0, 0), (0, 128 - width)))


def copies(part, count):
    def body(part, out):
        value = part[...].astype(BF16)
        for copy in range(count):
            out[copy] = value

    return call(body, [((count,) + part.shape, BF16)], [], 1 << 20, part)[0]


def summed(terms):
    inner, outer = ("x", "c"), ("z", "gy")
    first, second = lax.axis_size(inner), lax.axis_size(outer)
    rows, width = terms.shape[0] // first, terms.shape[1]
    pieces = lax.all_to_all(terms.reshape(first, rows, width), inner, 0, 0)
    part = jnp.sum(pieces.astype(F32), axis=0)
    pieces = lax.all_to_all(part, outer, 0, 0, tiled=True)
    done = jnp.sum(pieces.reshape(second, -1, width), axis=0)
    spread = jnp.broadcast_to(done[None], (second,) + done.shape).reshape(rows, width)
    part = lax.all_to_all(lax.optimization_barrier(spread), outer, 0, 0, tiled=True)
    return lax.all_to_all(copies(part, first), inner, 0, 0).reshape(terms.shape)


def on_device(
    volume,
    kernel_full,
    kernel_half,
    kernel_quarter,
    kernel_eighth,
    skip_full,
    skip_half,
    skip_quarter,
    skip_eighth,
):
    kernels = (kernel_full, kernel_half, kernel_quarter, kernel_eighth)
    volume = laid_out(volume)
    even = lax.axis_index("c") == 0
    first, last = volume[:1], volume[7:]
    one, two = swaps(jnp.where(even, last, first), jnp.where(even, first, last))
    skip3 = jnp.transpose(skip_eighth, (1, 2, 3, 0)).reshape(16, 128)
    skip2 = jnp.transpose(skip_quarter, (1, 2, 3, 0))
    one, two, skip0, skip1, kernels = lax.optimization_barrier(
        (one, two, laid_out(skip_full), laid_out(skip_half), kernels)
    )

    halo_y = swaps(*edge_rows(one, two, volume), "gy")
    dims = ((8, 16, 16), (4, 16, 32), (2, 32, 64), (1, 64, 128))
    w0, w1, w2, w3, t1, t2, t3 = prepare(kernels, dims)
    pre0, act1, shifts0, to_one, to_two = forward_full(
        volume, (one, two), halo_y, w0, skip1, skip3
    )
    halo_z1 = one, two = swaps(to_one, to_two)

    halo_y1 = swaps(*edge_rows_half(one, two, act1, skip1, skip3), "gy")
    pre1, act2, pre2, act3, shifts1 = forward_half(act1, halo_z1, halo_y1, w1, w2)
    columns = lax.axis_size("gy")
    many = (2 * columns,) + act3.shape
    acts = lax.all_to_all(
        lax.optimization_barrier(jnp.broadcast_to(act3[None], many)), ("c", "gy"), 0, 0
    )
    chips = swaps(acts, acts, ("x", "z"))
    dense2, delta2, shifts3, delta3 = deepest(
        columns, acts, chips, skip3, halo_z1, halo_y1, skip2, pre2, w3, t3
    )
    halo_z = one, two = swaps(dense2, dense2)
    block = jnp.concatenate([one, dense2, two], axis=0).reshape(384, 128)
    halo_y = swaps(block, block, "gy")
    grad3 = grad_deepest(shifts3, delta3)
    grad2 = grad_quarter_of(act2, delta2)
    terms = back_rest(
        dense2, halo_z, halo_y, skip1, halo_z1, halo_y1, pre1, skip0, pre0,
        t2, t1, shifts1, shifts0, grad3, grad2,
    )
    outs = unpack(summed(terms))
    return tuple(out.reshape(kernel.shape) for out, kernel in zip(outs, kernels))


def solution(mesh):
    fine = jax.sharding.Mesh(mesh.devices.reshape(4, 8, 2, 8), ("x", "z", "c", "gy"))
    return mapped(fine)


def mapped(fine):
    block = P(None, GZ, "gy", None)
    return jax.shard_map(
        on_device,
        mesh=fine,
        in_specs=(block, P(), P(), P(), P(), block, block, block, block),
        out_specs=(P(), P(), P(), P()),
        check_vma=False,
    )
```

```python
import jax
import jax.numpy as jnp
from jax import lax
from jax.experimental import pallas as pl
from jax.experimental.pallas import tpu as pltpu
from jax.sharding import PartitionSpec as P

F32 = jnp.float32
BF16 = jnp.bfloat16
GZ = ("x", "z", "c")
VMEM_BYTES = 14 * 1024 * 1024
NT = (((1,), (1,)), ((), ()))


def call(body, outs, scratch, flops, *args):
    return pl.pallas_call(
        body,
        out_shape=tuple(jax.ShapeDtypeStruct(shape, dtype) for shape, dtype in outs),
        in_specs=[pl.BlockSpec(memory_space=pltpu.VMEM) for _ in args],
        out_specs=tuple(pl.BlockSpec(memory_space=pltpu.VMEM) for _ in outs),
        scratch_shapes=[pltpu.VMEM(shape, dtype) for shape, dtype in scratch],
        compiler_params=pltpu.CompilerParams(vmem_limit_bytes=VMEM_BYTES),
        cost_estimate=pl.CostEstimate(flops=flops, bytes_accessed=1 << 20, transcendentals=0),
    )(*args)


def place_of():
    depth_at, row_at = lax.axis_index(GZ), lax.axis_index("gy")
    return (
        depth_at > 0,
        depth_at < lax.axis_size(GZ) - 1,
        row_at > 0,
        row_at < lax.axis_size("gy") - 1,
        lax.axis_index("c"),
        row_at,
    )


def row_edges(first, second, start, size):
    rule = lax.axis_index("gy") % 2 == 0
    one, two = (part[start : start + size].astype(F32) for part in (first, second))
    return jnp.where(rule, two, one).astype(BF16), jnp.where(rule, one, two).astype(BF16)


def half_lanes(tile, odd):
    tile = pltpu.roll(tile.astype(F32), 64, 1) if odd else tile.astype(F32)
    return jnp.where(lanes(tile.shape) < 64, tile, 0.0).astype(BF16)


def lanes(shape):
    return lax.broadcasted_iota(jnp.int32, shape, 1)


def at_column(tile, step):
    if step == 0:
        return tile
    moved = pltpu.roll(tile.astype(F32), (-step) % 128, 1)
    edge = 127 if step > 0 else 0
    return jnp.where(lanes(tile.shape) == edge, 0.0, moved).astype(BF16)


def put_shifts(shifts, row, layer, tile):
    for step in range(3):
        shifts[step, row : row + tile.shape[0], layer * 128 : layer * 128 + 128] = at_column(
            tile, step - 1
        )


def convolved(weights, shifts, rows, depth):
    tall = weights.shape[1] // 3
    total = None
    for step in range(3):
        window = shifts[step, rows[0] : rows[1], : (depth + 2) * 128]
        tap = weights[step][:, : rows[1] - rows[0]]
        term = jnp.dot(tap, window, preferred_element_type=F32)
        total = term if total is None else total + term
    value = None
    for down in range(3):
        part = total[down * tall : (down + 1) * tall, down * 128 : (down + depth) * 128]
        value = part if value is None else value + part
    return value


def sigmoid(values):
    return 1.0 / (1.0 + jnp.exp(-values))


def slope(values):
    sig = sigmoid(values)
    return sig * (1.0 + values * (1.0 - sig))


def exact_dot(values, picks):
    high = values.astype(BF16)
    rest = values - high.astype(F32)
    middle = rest.astype(BF16)
    low = (rest - middle.astype(F32)).astype(BF16)
    total = jnp.dot(low, picks, preferred_element_type=F32)
    total = total + jnp.dot(middle, picks, preferred_element_type=F32)
    return total + jnp.dot(high, picks, preferred_element_type=F32)


def pair_columns(down):
    rows = lax.broadcasted_iota(jnp.int32, (128, 128), 0)
    columns = lax.broadcasted_iota(jnp.int32, (128, 128), 1)
    hit = (rows // 2 == columns) if down else (columns // 2 == rows)
    return jnp.where(hit, 0.125, 0.0).astype(BF16)


def pooled(first, second, channels, width):
    both = first + second
    blocks = both.shape[0] // (2 * channels)
    rows = []
    for block in range(blocks):
        start = 2 * block * channels
        rows.append(
            both[start : start + channels] + both[start + channels : start + 2 * channels]
        )
    summed = rows[0] if blocks == 1 else jnp.concatenate(rows, axis=0)
    mean = exact_dot(summed, pair_columns(True))
    return jnp.where(lanes(mean.shape) < width // 2, mean, 0.0)


def silu(values):
    return values * sigmoid(values)


def prepare(kernels, dims):
    def body(*refs):
        ins, outs, wide = refs[:4], refs[4:11], refs[11]
        for level, (rows, chans, feats) in enumerate(dims):
            source, taps = ins[level][...], outs[level]
            picks = (
                lax.broadcasted_iota(jnp.int32, (feats, 128), 0)
                == lax.broadcasted_iota(jnp.int32, (feats, 128), 1) % feats
            )
            spread = jnp.dot(
                source, jnp.where(picks, 1.0, 0.0).astype(BF16), preferred_element_type=F32
            )
            size = taps.shape[2]
            place = lanes((chans, 128)) // feats
            for down in range(3):
                for step in range(3):
                    wide[...] = jnp.zeros_like(wide)
                    for row in range(rows + 2):
                        value = jnp.zeros((chans, 128), F32)
                        for across in range(3):
                            at = ((down * 3 + across) * 3 + step) * chans
                            value = jnp.where(
                                place == row - across, spread[at : at + chans], value
                            )
                        wide[row * chans : (row + 1) * chans, :] = value
                    taps[step, down * 128 : down * 128 + 128, :] = wide[:size, :].T.astype(BF16)
        for level in range(1, 4):
            rows, chans, feats = dims[level]
            if level == 2:
                rows = 4
            source, taps = ins[level][...], outs[3 + level]
            size = (rows + 2) * feats
            picks = (
                lax.broadcasted_iota(jnp.int32, (feats, size), 0)
                == lax.broadcasted_iota(jnp.int32, (feats, size), 1) % feats
            )
            spread = jnp.dot(
                source, jnp.where(picks, 1.0, 0.0).astype(BF16), preferred_element_type=F32
            )
            place = lanes((chans, size)) // feats
            for down in range(3):
                for step in range(3):
                    for row in range(rows):
                        value = jnp.zeros((chans, size), F32)
                        for across in range(3):
                            at = (((2 - down) * 3 + 2 - across) * 3 + 2 - step) * chans
                            value = jnp.where(
                                place == row + across, spread[at : at + chans], value
                            )
                        at = (down * rows + row) * chans
                        taps[step, at : at + chans, :] = value.astype(BF16)

    shapes = [(3, 384, 256), (3, 384, 128), (3, 384, 128), (3, 384, 256)]
    shapes += [(3, 192, 192), (3, 384, 384), (3, 192, 384)]
    flat = [kernel.reshape(-1, kernel.shape[-1]) for kernel in kernels]
    return call(body, [(s, BF16) for s in shapes], [((256, 128), F32)], 1 << 27, *flat)


def forward_full(volume, halo_z, halo_y, weights, skip_half, skip_deep):
    def body(own, one, two, above, below, taps, skip1, skip3, pre, act, shifts, to_one, to_two):
        even = lax.axis_index("c") == 0
        for layer in range(10):
            if 0 < layer < 9:
                high, low = row_edges(above, below, layer * 16, 16)
                middle = own[layer - 1]
            else:
                near, far = (two, one) if layer == 0 else (one, two)
                at = (144, 0) if layer == 0 else (0, 144)
                yes, no = (row_edges(above, below, start, 16) for start in at)
                high, low = (jnp.where(even, yes[part], no[part]) for part in range(2))
                middle = jnp.where(even, near[0], far[0])
            parts = (high, middle, low)
            put_shifts(shifts, 0, layer, parts[0])
            put_shifts(shifts, 16, layer, parts[1])
            put_shifts(shifts, 144, layer, parts[2])
        value = convolved(taps, shifts, (0, 160), 8)
        active = silu(value)
        for layer in range(8):
            pre[layer] = value[:, layer * 128 : layer * 128 + 128]
        for layer in range(4):
            at = layer * 256
            act[layer] = pooled(
                active[:, at : at + 128], active[:, at + 128 : at + 256], 16, 128
            ).astype(BF16)
        for layer in range(3):
            rows = slice(layer * 64, layer * 64 + 64)
            to_one[rows] = jnp.where(even, act[layer + 1], act[layer])
            to_two[rows] = jnp.where(even, act[layer], act[layer + 1])
        to_one[192:320] = jnp.where(even, skip1[3], skip1[0])
        to_two[192:320] = jnp.where(even, skip1[0], skip1[3])
        to_one[320:] = skip3[...]
        to_two[320:] = skip3[...]

    outs = [((8, 128, 128), F32), ((4, 64, 128), BF16), ((3, 160, 1280), BF16)]
    outs += [((336, 128), BF16), ((336, 128), BF16)]
    return call(
        body, outs, [], 1 << 29, volume, *halo_z, *halo_y, weights, skip_half, skip_deep
    )


def forward_half(act, halo_z, halo_y, weights_half, weights_quarter):
    def body(
        own, one, two, above, below, taps, next_taps, pre, act, next_pre, deep, shifts, inner
    ):
        flags = place_of()
        even = flags[4] == 0
        def edge_at(place):
            found = row_edges(above, below, place // 2 * 48, 48)
            return [half_lanes(part, place % 2) for part in found]

        for layer in range(10):
            if 3 <= layer < 7:
                middle = own[layer - 3]
                edges = edge_at(layer)
            else:
                near, far = (two, one) if layer < 3 else (one, two)
                at = layer % 7 * 64
                middle = jnp.where(even, near[at : at + 64], far[at : at + 64])
                at = layer % 7
                yes, no = (edge_at(place) for place in ((7 + at, at) if layer < 3 else (at, 7 + at)))
                edges = [jnp.where(even, yes[part], no[part]) for part in range(2)]
            put_shifts(shifts, 0, layer, edges[0])
            put_shifts(shifts, 48, layer, middle)
            put_shifts(shifts, 112, layer, edges[1])
        for part in range(2):
            value = convolved(taps, shifts, (part * 64, part * 64 + 96), 8)
            for layer in range(8):
                pre[layer, part * 128 : part * 128 + 128, :] = value[
                    :, layer * 128 : layer * 128 + 128
                ]
        row = lax.broadcasted_iota(jnp.int32, (128, 128), 0) // 32
        inside = (row > 0) | (flags[2])
        inside = inside & ((row < 3) | (flags[3]))
        for layer in range(4):
            value = pooled(silu(pre[2 * layer]), silu(pre[2 * layer + 1]), 32, 64)
            keep = inside
            if layer == 0:
                keep = keep & (flags[0])
            if layer == 3:
                keep = keep & (flags[1])
            value = jnp.where(keep, value, 0.0).astype(BF16)
            act[layer] = value
            put_shifts(inner, 0, layer, value)
        value = convolved(next_taps, inner, (0, 128), 2)
        next_pre[0] = value[:, :128]
        next_pre[1] = value[:, 128:]
        coarse = pooled(silu(value[:, :128]), silu(value[:, 128:]), 64, 32)
        dense = coarse[:8].astype(BF16).astype(F32)
        for group in range(1, 8):
            part = coarse[group * 8 : group * 8 + 8].astype(BF16).astype(F32)
            dense = dense + pltpu.roll(part, group * 16, 1)
        deep[...] = dense

    outs = [
        ((8, 256, 128), F32),
        ((4, 128, 128), BF16),
        ((2, 128, 128), F32),
        ((8, 128), F32),
        ((3, 160, 1280), BF16),
    ]
    return call(
        body,
        outs,
        [((3, 128, 512), BF16)],
        1 << 29,
        act,
        *halo_z,
        *halo_y,
        weights_half,
        weights_quarter,
    )


def turned(tile, by):
    return tile if by % 128 == 0 else pltpu.roll(tile, by % 128, 1)


def near_cell(tile, layer_step, step):
    moved = turned(tile, -(16 * layer_step + step))
    column = lanes(tile.shape) % 16
    if step > 0:
        moved = jnp.where(column == 15, 0.0, moved)
    if step < 0:
        moved = jnp.where(column == 0, 0.0, moved)
    return moved.astype(BF16)


def columns_last(tile, start):
    width = tile.shape[0]
    column = lax.broadcasted_iota(jnp.int32, (width, 128), 0)
    picks = jnp.where(lanes((width, 128)) == column + start, 1.0, 0.0).astype(BF16)
    return lax.dot_general(tile, picks, (((0,), (0,)), ((), ())), preferred_element_type=F32)


def opened(dense, layer):
    parts = [turned(dense, 16 * layer - 16 * group) for group in range(8)]
    return jnp.concatenate(parts, axis=0)


def deepest(columns, acts, chips, skip_deep, halo_z, halo_y, skip, pre, weights, weights_back):
    def body(
        acts, chip_one, chip_two, skip_own, skip_one, skip_two, skip_above, skip_below, skip, pre,
        taps, taps_back, dense_out, out, shifts, delta_own, deltas,
    ):
        flags = place_of()
        core, row_at = flags[4], flags[5]
        place = lanes((64, 128)) // 16

        ahead = lax.axis_index("z") % 2 == 0

        def cells(position, row):
            at = position % 2 * columns + row
            if position // 2 == 1:
                return acts[at]
            if position // 2 == 0:
                return jnp.where(ahead, chip_two[at], chip_one[at])
            return jnp.where(ahead, chip_one[at], chip_two[at])

        for near in range(5):
            row = row_at + near - 2
            valid = (row >= 0) & (row < columns)
            row = jnp.clip(row, 0, columns - 1)
            value = jnp.zeros((64, 128), F32)
            for layer in range(5):
                dense = jnp.where(core == 0, cells(layer, row), cells(layer + 1, row))
                value = jnp.where(place == layer, opened(dense, layer), value)
            value = jnp.where(valid, value, 0.0)
            for down in range(3):
                for step in range(3):
                    shifts[down * 3 + step, near * 64 : near * 64 + 64, :] = near_cell(
                        value, down - 1, step - 1
                    )
        place = lanes((128, 128)) // 16
        for near in range(3):
            value = None
            for tap in range(9):
                window = shifts[tap, near * 64 : near * 64 + 192, :]
                weight = taps[tap % 3, tap // 3 * 128 : tap // 3 * 128 + 128, :192]
                term = jnp.dot(weight, window, preferred_element_type=F32)
                value = term if value is None else value + term
            upstream = jnp.zeros((128, 128), F32)
            for layer in range(3):
                if near != 1:
                    yes = row_edges(skip_above, skip_below, 368 - layer * 16, 16)[near // 2]
                    no = row_edges(skip_above, skip_below, 336 + layer * 16, 16)[near // 2]
                    dense = jnp.where(core == 0, yes, no)
                elif layer == 1:
                    dense = skip_own[...]
                else:
                    ends = (skip_two, skip_one) if layer == 0 else (skip_one, skip_two)
                    dense = jnp.where(core == 0, ends[0][320:], ends[1][320:])
                upstream = upstream + columns_last(dense, 16 * layer + 16)
            keep = (place == 2) | ((place == 1) & (flags[0])) | ((place == 3) & (flags[1]))
            if near != 1:
                keep = keep & (flags[2 + near // 2])
            change = jnp.where(keep, upstream * slope(value), 0.0).astype(BF16).astype(F32)
            if near == 1:
                delta_own[...] = jnp.where(place == 2, change, 0.0).astype(BF16)
            deltas[near * 128 : near * 128 + 128, :] = change
        carried = None
        for down in range(3):
            for step in range(3):
                window = near_cell(deltas[...], down - 1, step - 1)
                weight = taps_back[step, down * 64 : down * 64 + 64, :]
                term = jnp.dot(weight, window, preferred_element_type=F32)
                carried = term if carried is None else carried + term
        carried = exact_dot(turned(carried, -32), pair_columns(False))
        carried = jnp.concatenate([carried, carried], axis=0)
        dense = None
        for layer in range(2):
            wide = [columns_last(skip[layer, row], 0) for row in range(2)]
            change = (jnp.concatenate(wide, axis=0) + carried) * slope(pre[layer])
            change = jnp.where(lanes(change.shape) < 32, change, 0.0).astype(BF16)
            out[layer] = change
            change = change.astype(F32)
            dense = change if dense is None else dense + turned(change, 32)
        dense_out[0] = dense.astype(BF16)

    outs = [
        ((1, 128, 128), BF16),
        ((2, 128, 128), BF16),
        ((9, 320, 128), BF16),
        ((128, 128), BF16),
    ]
    scratch = [((384, 128), F32)]
    return call(
        body, outs, scratch, 1 << 28,
        acts, *chips, skip_deep, *halo_z, *halo_y, skip, pre, weights, weights_back,
    )


def grad_deepest(shifts, delta):
    def body(shifts, delta, grad):
        for tap in range(9):
            grad[tap * 192 : tap * 192 + 192, :] = lax.dot_general(
                shifts[tap, 64:256, :], delta[...], NT, preferred_element_type=F32
            )

    return call(body, [((1728, 128), F32)], [], 1 << 27, shifts, delta)[0]


def diagonal(product, rows, chans, feats):
    place = lanes((3 * chans, 128)) // feats
    value = product[: 3 * chans]
    for row in range(1, rows):
        value = jnp.where(place == row, product[row * chans : (row + 3) * chans], value)
    turn = 64
    while turn >= feats:
        value = value + pltpu.roll(value, turn, 1)
        turn //= 2
    return value


def packed(tall, groups):
    size = tall.shape[0] // groups
    place = lanes((size, 128)) // (128 // groups)
    value = tall[:size, :]
    for group in range(1, groups):
        value = jnp.where(place == group, tall[group * size : (group + 1) * size, :], value)
    return value


def put_grads(tall, shifts, rows, offset, depth, delta, dims):
    count, chans, feats = dims
    size = rows[1] - rows[0]
    for down in range(3):
        at = (offset + down) * 128
        window = [shifts[step, rows[0] : rows[1], at : at + depth * 128] for step in range(3)]
        product = lax.dot_general(
            jnp.concatenate(window, axis=0), delta, NT, preferred_element_type=F32
        )
        for step in range(3):
            tap = (down * 3 + step) * 3 * chans
            part = product[step * size : (step + 1) * size]
            tall[tap : tap + 3 * chans, :] = diagonal(part, count, chans, feats)


def grad_quarter_of(act, delta):
    def body(act, delta, grad, shifts, tall):
        for layer in range(4):
            put_shifts(shifts, 0, layer, act[layer])
        both = jnp.concatenate([delta[0], delta[1]], axis=1)
        put_grads(tall, shifts, (0, 128), 0, 2, both, (2, 32, 64))
        grad[...] = packed(tall, 2)

    scratch = [((3, 128, 512), BF16), ((864, 128), F32)]
    return call(body, [((432, 128), F32)], scratch, 1 << 28, act, delta)[0]


def back_rest(
    delta, halo_z, halo_y, skip_half, halo_zs, halo_ys, pre_half, skip_full, pre_full,
    weights_quarter, weights_half, shifts_half, shifts_full, deep_grad, quarter_grad,
):
    def body(
        own, one, two, above, below, skip1, one1, two1, above1, below1, pre1, skip0, pre0,
        taps2, taps1, shifts1, shifts0, grad3, grad2, out, moved2, moved1, delta1, delta0, tall, flat,
    ):
        flags = place_of()
        even = flags[4] == 0
        for layer in range(6):
            block = layer // 2
            high, low = row_edges(above, below, block * 128, 128)
            middle = own[0]
            if block != 1:
                near, far = (two, one) if block == 0 else (one, two)
                middle = jnp.where(even, near[0], far[0])
                other = row_edges(above, below, (2 - block) * 128, 128)
                high, low = jnp.where(even, other[0], high), jnp.where(even, other[1], low)
            tiles = (high, middle, low)
            for part, tile in enumerate(tiles):
                tile = turned(tile.astype(F32), -32 * (layer % 2))
                tile = jnp.where(lanes(tile.shape) < 32, tile, 0.0).astype(BF16)
                put_shifts(moved2, part * 128, layer, tile)
        value = convolved(taps2, moved2, (0, 384), 4)

        def edge_at(place):
            found = row_edges(above1, below1, 240 + place // 2 * 32, 32)
            return [half_lanes(part, place % 2) for part in found]

        picks = pair_columns(False)
        row = lax.broadcasted_iota(jnp.int32, (192, 128), 0) // 32
        inside = lanes((192, 128)) < 64
        inside = inside & ((row > 0) | (flags[2])) & ((row < 5) | (flags[3]))
        for layer in range(6):
            if layer % 2 == 1 or layer == 0:
                at = (layer + 1) // 2 * 128
                carried = exact_dot(value[:, at : at + 128], picks)
                parts = [carried[part * 32 : part * 32 + 32] for part in (0, 1, 1, 2, 2, 3)]
                carried = jnp.concatenate(parts, axis=0)
            if 0 < layer < 5:
                high, low = edge_at(layer)
                middle = skip1[layer - 1]
            else:
                near, far = (two1, one1) if layer == 0 else (one1, two1)
                yes, no = edge_at(5 - layer), edge_at(layer)
                high, low = (jnp.where(even, yes[part], no[part]) for part in range(2))
                middle = jnp.where(even, near[192:320], far[192:320])
            parts = (high, middle, low)
            skip = jnp.concatenate(parts, axis=0).astype(F32)
            change = (skip + carried) * slope(pre1[layer + 1, 32:224])
            keep = inside
            if layer == 0:
                keep = keep & (flags[0])
            if layer == 5:
                keep = keep & (flags[1])
            change = jnp.where(keep, change, 0.0).astype(BF16)
            put_shifts(moved1, 0, layer, change)
            if 0 < layer < 5:
                delta1[:, (layer - 1) * 128 : layer * 128] = change[32:160]
        value = convolved(taps1, moved1, (0, 192), 4)
        for layer in range(8):
            if layer % 2 == 0:
                at = layer // 2 * 128
                carried = exact_dot(value[:, at : at + 128], picks)
                parts = [carried[part // 2 * 16 : part // 2 * 16 + 16] for part in range(8)]
                carried = jnp.concatenate(parts, axis=0)
            change = (skip0[layer].astype(F32) + carried) * slope(pre0[layer])
            delta0[:, layer * 128 : layer * 128 + 128] = change.astype(BF16)
        flat[:1728, :] = grad3[...]
        flat[1728:2160, :] = grad2[...]
        tall[...] = jnp.zeros_like(tall)
        put_grads(tall, shifts1, (32, 128), 2, 4, delta1[...], (4, 16, 32))
        flat[2160:2272, :] = packed(tall, 4)
        put_grads(tall, shifts0, (0, 160), 0, 8, delta0[...], (8, 16, 16))
        flat[2272:2328, :] = packed(tall, 8)
        flat[2328:, :] = jnp.zeros((2560 - 2328, 128), F32)
        for part in range(5):
            at = part * 512
            out[:, part * 128 : part * 128 + 128] = flat[at : at + 512, :].astype(BF16)

    scratch = [
        ((3, 384, 768), BF16),
        ((3, 192, 768), BF16),
        ((128, 512), BF16),
        ((128, 1024), BF16),
        ((448, 128), F32),
        ((2560, 128), F32),
    ]
    return call(
        body, [((512, 640), BF16)], scratch, 1 << 30,
        delta, *halo_z, *halo_y, skip_half, *halo_zs, *halo_ys, pre_half, skip_full, pre_full,
        weights_quarter, weights_half, shifts_half, shifts_full, deep_grad, quarter_grad,
    )[0]


def unpack(sums):
    def body(sums, full, half, quarter, eighth, whole, tall):
        for part in range(5):
            block = sums[:, part * 128 : part * 128 + 128]
            whole[part * 512 : part * 512 + 512, :] = block.astype(F32)

        def spread(out, source, chans):
            for down in range(3):
                for across in range(3):
                    for step in range(3):
                        at = ((down * 3 + across) * 3 + step) * chans
                        start = ((down * 3 + step) * 3 + across) * chans
                        out[at : at + chans, :] = source[
                            start : start + chans, : out.shape[1]
                        ]

        spread(eighth, whole, 64)
        for out, start, size, groups, chans in (
            (quarter, 1728, 432, 2, 32),
            (half, 2160, 112, 4, 16),
            (full, 2272, 56, 8, 16),
        ):
            dense = whole[start : start + size, :]
            for group in range(groups):
                tall[group * size : (group + 1) * size, :] = (
                    dense if group == 0 else pltpu.roll(dense, 128 - group * (128 // groups), 1)
                )
            spread(out, tall, chans)

    outs = [((432, 16), F32), ((432, 32), F32), ((864, 64), F32), ((1728, 128), F32)]
    scratch = [((2560, 128), F32), ((864, 128), F32)]
    return call(body, outs, scratch, 1 << 20, sums)


def pairs(axis):
    size = lax.axis_size(axis)
    between = [(i, i + 1) for i in range(1, size - 1, 2)]
    return [(i, i ^ 1) for i in range(size)], between + [(j, i) for i, j in between]


def swaps(to_one, to_two, axis=GZ):
    first, second = pairs(axis)
    return lax.ppermute(to_one, axis, first), lax.ppermute(to_two, axis, second)


def edge_rows(one, two, volume):
    def body(one, two, own, to_one, to_two):
        even = lax.axis_index("gy") % 2 == 0
        for place in range(10):
            block = one[0] if place == 0 else two[0] if place == 9 else own[place - 1]
            at = place * 16
            to_one[at : at + 16] = jnp.where(even, block[112:], block[:16])
            to_two[at : at + 16] = jnp.where(even, block[:16], block[112:])

    return call(body, [((160, 128), BF16)] * 2, [], 1 << 20, one, two, volume)


def edge_rows_half(one, two, act, skip_half, skip_deep):
    def body(one, two, act, skip1, skip3, to_one, to_two):
        even = lax.axis_index("gy") % 2 == 0

        def put(at, size, blocks):
            low, high = blocks
            packed_rows = []
            for rows in (slice(0, size), slice(low.shape[0] - size, low.shape[0])):
                packed_rows.append(
                    low[rows].astype(F32) + pltpu.roll(high[rows].astype(F32), 64, 1)
                )
            top, bottom = packed_rows
            to_one[at : at + size] = jnp.where(even, bottom, top).astype(BF16)
            to_two[at : at + size] = jnp.where(even, top, bottom).astype(BF16)

        def act_at(place):
            if 3 <= place < 7:
                return act[place - 3]
            at = place % 7 * 64
            return (one if place < 3 else two)[at : at + 64]

        def skip_at(place):
            if 0 < place < 5:
                return skip1[place - 1]
            return (one if place == 0 else two)[192:320]

        for pair in range(5):
            put(pair * 48, 48, (act_at(2 * pair), act_at(2 * pair + 1)))
        for pair in range(3):
            put(240 + pair * 32, 32, (skip_at(2 * pair), skip_at(2 * pair + 1)))
        for place, rows in enumerate((one[320:], skip3[...], two[320:])):
            at = 336 + place * 16
            to_one[at : at + 16] = rows
            to_two[at : at + 16] = rows

    return call(
        body, [((384, 128), BF16)] * 2, [], 1 << 20, one, two, act, skip_half, skip_deep
    )


def laid_out(array):
    chans, depth, height, width = array.shape
    rows = jnp.transpose(array, (1, 2, 0, 3)).reshape(depth, height * chans, width)
    return jnp.pad(rows, ((0, 0), (0, 0), (0, 128 - width)))


def copies(part, count):
    def body(part, out):
        value = part[...].astype(BF16)
        for copy in range(count):
            out[copy] = value

    return call(body, [((count,) + part.shape, BF16)], [], 1 << 20, part)[0]


def summed(terms):
    inner, outer = ("x", "c"), ("z", "gy")
    first, second = lax.axis_size(inner), lax.axis_size(outer)
    rows, width = terms.shape[0] // first, terms.shape[1]
    pieces = lax.all_to_all(terms.reshape(first, rows, width), inner, 0, 0)
    part = jnp.sum(pieces.astype(F32), axis=0)
    pieces = lax.all_to_all(part, outer, 0, 0, tiled=True)
    done = jnp.sum(pieces.reshape(second, -1, width), axis=0)
    spread = jnp.broadcast_to(done[None], (second,) + done.shape).reshape(rows, width)
    part = lax.all_to_all(lax.optimization_barrier(spread), outer, 0, 0, tiled=True)
    return lax.all_to_all(copies(part, first), inner, 0, 0).reshape(terms.shape)


def on_device(
    volume,
    kernel_full,
    kernel_half,
    kernel_quarter,
    kernel_eighth,
    skip_full,
    skip_half,
    skip_quarter,
    skip_eighth,
):
    kernels = (kernel_full, kernel_half, kernel_quarter, kernel_eighth)
    volume = laid_out(volume)
    even = lax.axis_index("c") == 0
    first, last = volume[:1], volume[7:]
    one, two = swaps(jnp.where(even, last, first), jnp.where(even, first, last))
    skip3 = jnp.transpose(skip_eighth, (1, 2, 3, 0)).reshape(16, 128)
    skip2 = jnp.transpose(skip_quarter, (1, 2, 3, 0))
    one, two, skip0, skip1, kernels = lax.optimization_barrier(
        (one, two, laid_out(skip_full), laid_out(skip_half), kernels)
    )

    halo_y = swaps(*edge_rows(one, two, volume), "gy")
    dims = ((8, 16, 16), (4, 16, 32), (2, 32, 64), (1, 64, 128))
    w0, w1, w2, w3, t1, t2, t3 = prepare(kernels, dims)
    pre0, act1, shifts0, to_one, to_two = forward_full(
        volume, (one, two), halo_y, w0, skip1, skip3
    )
    halo_z1 = one, two = swaps(to_one, to_two)

    halo_y1 = swaps(*edge_rows_half(one, two, act1, skip1, skip3), "gy")
    pre1, act2, pre2, act3, shifts1 = forward_half(act1, halo_z1, halo_y1, w1, w2)
    columns = lax.axis_size("gy")
    many = (2 * columns,) + act3.shape
    acts = lax.all_to_all(
        lax.optimization_barrier(jnp.broadcast_to(act3[None], many)), ("c", "gy"), 0, 0
    )
    chips = swaps(acts, acts, ("x", "z"))
    dense2, delta2, shifts3, delta3 = deepest(
        columns, acts, chips, skip3, halo_z1, halo_y1, skip2, pre2, w3, t3
    )
    halo_z = one, two = swaps(dense2, dense2)
    block = jnp.concatenate([one, dense2, two], axis=0).reshape(384, 128)
    halo_y = swaps(block, block, "gy")
    grad3 = grad_deepest(shifts3, delta3)
    grad2 = grad_quarter_of(act2, delta2)
    terms = back_rest(
        dense2, halo_z, halo_y, skip1, halo_z1, halo_y1, pre1, skip0, pre0,
        t2, t1, shifts1, shifts0, grad3, grad2,
    )
    outs = unpack(summed(terms))
    return tuple(out.reshape(kernel.shape) for out, kernel in zip(outs, kernels))


def solution(mesh):
    fine = jax.sharding.Mesh(mesh.devices.reshape(4, 8, 2, 8), ("x", "z", "c", "gy"))
    return mapped(fine)


def mapped(fine):
    block = P(None, GZ, "gy", None)
    return jax.shard_map(
        on_device,
        mesh=fine,
        in_specs=(block, P(), P(), P(), P(), block, block, block, block),
        out_specs=(P(), P(), P(), P()),
        check_vma=False,
    )
```

```python
import jax
import jax.numpy as jnp
from jax import lax
from jax.experimental import pallas as pl
from jax.experimental.pallas import tpu as pltpu
from jax.sharding import PartitionSpec as P

F32 = jnp.float32
BF16 = jnp.bfloat16
GZ = ("x", "z", "c")
VMEM_BYTES = 14 * 1024 * 1024
NT = (((1,), (1,)), ((), ()))


def call(body, outs, scratch, flops, *args):
    return pl.pallas_call(
        body,
        out_shape=tuple(jax.ShapeDtypeStruct(shape, dtype) for shape, dtype in outs),
        in_specs=[pl.BlockSpec(memory_space=pltpu.VMEM) for _ in args],
        out_specs=tuple(pl.BlockSpec(memory_space=pltpu.VMEM) for _ in outs),
        scratch_shapes=[pltpu.VMEM(shape, dtype) for shape, dtype in scratch],
        compiler_params=pltpu.CompilerParams(vmem_limit_bytes=VMEM_BYTES),
        cost_estimate=pl.CostEstimate(flops=flops, bytes_accessed=1 << 20, transcendentals=0),
    )(*args)


def place_of():
    depth_at, row_at = lax.axis_index(GZ), lax.axis_index("gy")
    return (
        depth_at > 0,
        depth_at < lax.axis_size(GZ) - 1,
        row_at > 0,
        row_at < lax.axis_size("gy") - 1,
        lax.axis_index("c"),
        row_at,
    )


def row_edges(first, second, start, size):
    rule = lax.axis_index("gy") % 2 == 0
    one, two = (part[start : start + size].astype(F32) for part in (first, second))
    return jnp.where(rule, two, one).astype(BF16), jnp.where(rule, one, two).astype(BF16)


def half_lanes(tile, odd):
    tile = pltpu.roll(tile.astype(F32), 64, 1) if odd else tile.astype(F32)
    return jnp.where(lanes(tile.shape) < 64, tile, 0.0).astype(BF16)


def lanes(shape):
    return lax.broadcasted_iota(jnp.int32, shape, 1)


def at_column(tile, step):
    if step == 0:
        return tile
    moved = pltpu.roll(tile.astype(F32), (-step) % 128, 1)
    edge = 127 if step > 0 else 0
    return jnp.where(lanes(tile.shape) == edge, 0.0, moved).astype(BF16)


def put_shifts(shifts, row, layer, tile):
    for step in range(3):
        shifts[step, row : row + tile.shape[0], layer * 128 : layer * 128 + 128] = at_column(
            tile, step - 1
        )


def convolved(weights, shifts, rows, depth):
    windows = [
        shifts[step, rows[0] : rows[1], down * 128 : (down + depth) * 128]
        for down in range(3)
        for step in range(3)
    ]
    size = 9 * (rows[1] - rows[0])
    return jnp.dot(
        weights[:, :size], jnp.concatenate(windows, axis=0), preferred_element_type=F32
    )


def sigmoid(values):
    return 1.0 / (1.0 + jnp.exp(-values))


def slope(values):
    sig = sigmoid(values)
    return sig * (1.0 + values * (1.0 - sig))


def exact_dot(values, picks):
    high = values.astype(BF16)
    rest = values - high.astype(F32)
    middle = rest.astype(BF16)
    low = (rest - middle.astype(F32)).astype(BF16)
    total = jnp.dot(low, picks, preferred_element_type=F32)
    total = total + jnp.dot(middle, picks, preferred_element_type=F32)
    return total + jnp.dot(high, picks, preferred_element_type=F32)


def pair_columns(down):
    rows = lax.broadcasted_iota(jnp.int32, (128, 128), 0)
    columns = lax.broadcasted_iota(jnp.int32, (128, 128), 1)
    hit = (rows // 2 == columns) if down else (columns // 2 == rows)
    return jnp.where(hit, 0.125, 0.0).astype(BF16)


def pooled(first, second, channels, width):
    both = first + second
    blocks = both.shape[0] // (2 * channels)
    rows = []
    for block in range(blocks):
        start = 2 * block * channels
        rows.append(
            both[start : start + channels] + both[start + channels : start + 2 * channels]
        )
    summed = rows[0] if blocks == 1 else jnp.concatenate(rows, axis=0)
    mean = exact_dot(summed, pair_columns(True))
    return jnp.where(lanes(mean.shape) < width // 2, mean, 0.0)


def silu(values):
    return values * sigmoid(values)


def prepare(kernels, dims):
    def body(*refs):
        ins, outs, wide = refs[:4], refs[4:11], refs[11]
        for level, (rows, chans, feats) in enumerate(dims):
            source, taps = ins[level][...], outs[level]
            picks = (
                lax.broadcasted_iota(jnp.int32, (feats, 128), 0)
                == lax.broadcasted_iota(jnp.int32, (feats, 128), 1) % feats
            )
            spread = jnp.dot(
                source, jnp.where(picks, 1.0, 0.0).astype(BF16), preferred_element_type=F32
            )
            size = taps.shape[1]
            used = 9 * (rows + 2) * chans
            if used < size:
                wide[used:size, :] = jnp.zeros((size - used, 128), F32)
            place = lanes((chans, 128)) // feats
            for down in range(3):
                for step in range(3):
                    for row in range(rows + 2):
                        value = jnp.zeros((chans, 128), F32)
                        for across in range(3):
                            at = ((down * 3 + across) * 3 + step) * chans
                            value = jnp.where(
                                place == row - across, spread[at : at + chans], value
                            )
                        at = ((down * 3 + step) * (rows + 2) + row) * chans
                        wide[at : at + chans, :] = value
            taps[...] = wide[:size, :].T.astype(BF16)
        for level in range(1, 4):
            rows, chans, feats = dims[level]
            if level == 2:
                rows = 4
            source, taps = ins[level][...], outs[3 + level]
            size = (rows + 2) * feats
            picks = (
                lax.broadcasted_iota(jnp.int32, (feats, size), 0)
                == lax.broadcasted_iota(jnp.int32, (feats, size), 1) % feats
            )
            spread = jnp.dot(
                source, jnp.where(picks, 1.0, 0.0).astype(BF16), preferred_element_type=F32
            )
            place = lanes((chans, size)) // feats
            for down in range(3):
                for step in range(3):
                    for row in range(rows):
                        value = jnp.zeros((chans, size), F32)
                        for across in range(3):
                            at = (((2 - down) * 3 + 2 - across) * 3 + 2 - step) * chans
                            value = jnp.where(
                                place == row + across, spread[at : at + chans], value
                            )
                        at = (down * 3 + step) * size
                        taps[row * chans : (row + 1) * chans, at : at + size] = value.astype(BF16)

    shapes = [(128, 1536), (128, 896), (128, 1152), (128, 1792)]
    shapes += [(64, 1728), (128, 3456), (64, 3456)]
    flat = [kernel.reshape(-1, kernel.shape[-1]) for kernel in kernels]
    return call(body, [(s, BF16) for s in shapes], [((1792, 128), F32)], 1 << 27, *flat)


def forward_full(volume, halo_z, halo_y, weights, skip_half, skip_deep):
    def body(own, one, two, above, below, taps, skip1, skip3, pre, act, shifts, to_one, to_two):
        even = lax.axis_index("c") == 0
        for layer in range(10):
            if 0 < layer < 9:
                high, low = row_edges(above, below, layer * 16, 16)
                middle = own[layer - 1]
            else:
                near, far = (two, one) if layer == 0 else (one, two)
                at = (144, 0) if layer == 0 else (0, 144)
                yes, no = (row_edges(above, below, start, 16) for start in at)
                high, low = (jnp.where(even, yes[part], no[part]) for part in range(2))
                middle = jnp.where(even, near[0], far[0])
            parts = (high, middle, low)
            put_shifts(shifts, 0, layer, parts[0])
            put_shifts(shifts, 16, layer, parts[1])
            put_shifts(shifts, 144, layer, parts[2])
        value = convolved(taps, shifts, (0, 160), 8)
        active = silu(value)
        for layer in range(8):
            pre[layer] = value[:, layer * 128 : layer * 128 + 128]
        for layer in range(4):
            at = layer * 256
            act[layer] = pooled(
                active[:, at : at + 128], active[:, at + 128 : at + 256], 16, 128
            ).astype(BF16)
        for layer in range(3):
            rows = slice(layer * 64, layer * 64 + 64)
            to_one[rows] = jnp.where(even, act[layer + 1], act[layer])
            to_two[rows] = jnp.where(even, act[layer], act[layer + 1])
        to_one[192:320] = jnp.where(even, skip1[3], skip1[0])
        to_two[192:320] = jnp.where(even, skip1[0], skip1[3])
        to_one[320:] = skip3[...]
        to_two[320:] = skip3[...]

    outs = [((8, 128, 128), F32), ((4, 64, 128), BF16), ((3, 160, 1280), BF16)]
    outs += [((336, 128), BF16), ((336, 128), BF16)]
    return call(
        body, outs, [], 1 << 29, volume, *halo_z, *halo_y, weights, skip_half, skip_deep
    )


def forward_half(act, halo_z, halo_y, weights_half, weights_quarter):
    def body(
        own, one, two, above, below, taps, next_taps, pre, act, next_pre, deep, shifts, inner
    ):
        flags = place_of()
        even = flags[4] == 0
        def edge_at(place):
            found = row_edges(above, below, place // 2 * 48, 48)
            return [half_lanes(part, place % 2) for part in found]

        for layer in range(10):
            if 3 <= layer < 7:
                middle = own[layer - 3]
                edges = edge_at(layer)
            else:
                near, far = (two, one) if layer < 3 else (one, two)
                at = layer % 7 * 64
                middle = jnp.where(even, near[at : at + 64], far[at : at + 64])
                at = layer % 7
                yes, no = (edge_at(place) for place in ((7 + at, at) if layer < 3 else (at, 7 + at)))
                edges = [jnp.where(even, yes[part], no[part]) for part in range(2)]
            put_shifts(shifts, 0, layer, edges[0])
            put_shifts(shifts, 48, layer, middle)
            put_shifts(shifts, 112, layer, edges[1])
        for part in range(2):
            value = convolved(taps, shifts, (part * 64, part * 64 + 96), 8)
            for layer in range(8):
                pre[layer, part * 128 : part * 128 + 128, :] = value[
                    :, layer * 128 : layer * 128 + 128
                ]
        row = lax.broadcasted_iota(jnp.int32, (128, 128), 0) // 32
        inside = (row > 0) | (flags[2])
        inside = inside & ((row < 3) | (flags[3]))
        for layer in range(4):
            value = pooled(silu(pre[2 * layer]), silu(pre[2 * layer + 1]), 32, 64)
            keep = inside
            if layer == 0:
                keep = keep & (flags[0])
            if layer == 3:
                keep = keep & (flags[1])
            value = jnp.where(keep, value, 0.0).astype(BF16)
            act[layer] = value
            put_shifts(inner, 0, layer, value)
        value = convolved(next_taps, inner, (0, 128), 2)
        next_pre[0] = value[:, :128]
        next_pre[1] = value[:, 128:]
        coarse = pooled(silu(value[:, :128]), silu(value[:, 128:]), 64, 32)
        dense = coarse[:8].astype(BF16).astype(F32)
        for group in range(1, 8):
            part = coarse[group * 8 : group * 8 + 8].astype(BF16).astype(F32)
            dense = dense + pltpu.roll(part, group * 16, 1)
        deep[...] = dense

    outs = [
        ((8, 256, 128), F32),
        ((4, 128, 128), BF16),
        ((2, 128, 128), F32),
        ((8, 128), F32),
        ((3, 160, 1280), BF16),
    ]
    return call(
        body,
        outs,
        [((3, 128, 512), BF16)],
        1 << 29,
        act,
        *halo_z,
        *halo_y,
        weights_half,
        weights_quarter,
    )


def turned(tile, by):
    return tile if by % 128 == 0 else pltpu.roll(tile, by % 128, 1)


def near_cell(tile, layer_step, step):
    moved = turned(tile, -(16 * layer_step + step))
    column = lanes(tile.shape) % 16
    if step > 0:
        moved = jnp.where(column == 15, 0.0, moved)
    if step < 0:
        moved = jnp.where(column == 0, 0.0, moved)
    return moved.astype(BF16)


def columns_last(tile, start):
    width = tile.shape[0]
    column = lax.broadcasted_iota(jnp.int32, (width, 128), 0)
    picks = jnp.where(lanes((width, 128)) == column + start, 1.0, 0.0).astype(BF16)
    return lax.dot_general(tile, picks, (((0,), (0,)), ((), ())), preferred_element_type=F32)


def opened(dense, layer):
    parts = [turned(dense, 16 * layer - 16 * group) for group in range(8)]
    return jnp.concatenate(parts, axis=0)


def deepest(columns, acts, chips, skip_deep, halo_z, halo_y, skip, pre, weights, weights_back):
    def body(
        acts, chip_one, chip_two, skip_own, skip_one, skip_two, skip_above, skip_below, skip, pre,
        taps, taps_back, dense_out, out, shifts, delta_own, deltas,
    ):
        flags = place_of()
        core, row_at = flags[4], flags[5]
        place = lanes((64, 128)) // 16

        ahead = lax.axis_index("z") % 2 == 0

        def cells(position, row):
            at = position % 2 * columns + row
            if position // 2 == 1:
                return acts[at]
            if position // 2 == 0:
                return jnp.where(ahead, chip_two[at], chip_one[at])
            return jnp.where(ahead, chip_one[at], chip_two[at])

        for near in range(5):
            row = row_at + near - 2
            valid = (row >= 0) & (row < columns)
            row = jnp.clip(row, 0, columns - 1)
            value = jnp.zeros((64, 128), F32)
            for layer in range(5):
                dense = jnp.where(core == 0, cells(layer, row), cells(layer + 1, row))
                value = jnp.where(place == layer, opened(dense, layer), value)
            value = jnp.where(valid, value, 0.0)
            for down in range(3):
                for step in range(3):
                    shifts[down * 3 + step, near * 64 : near * 64 + 64, :] = near_cell(
                        value, down - 1, step - 1
                    )
        place = lanes((128, 128)) // 16
        for near in range(3):
            window = shifts[:, near * 64 : near * 64 + 192, :].reshape(1728, 128)
            value = jnp.dot(taps[:, :1728], window, preferred_element_type=F32)
            upstream = jnp.zeros((128, 128), F32)
            for layer in range(3):
                if near != 1:
                    yes = row_edges(skip_above, skip_below, 368 - layer * 16, 16)[near // 2]
                    no = row_edges(skip_above, skip_below, 336 + layer * 16, 16)[near // 2]
                    dense = jnp.where(core == 0, yes, no)
                elif layer == 1:
                    dense = skip_own[...]
                else:
                    ends = (skip_two, skip_one) if layer == 0 else (skip_one, skip_two)
                    dense = jnp.where(core == 0, ends[0][320:], ends[1][320:])
                upstream = upstream + columns_last(dense, 16 * layer + 16)
            keep = (place == 2) | ((place == 1) & (flags[0])) | ((place == 3) & (flags[1]))
            if near != 1:
                keep = keep & (flags[2 + near // 2])
            change = jnp.where(keep, upstream * slope(value), 0.0).astype(BF16).astype(F32)
            if near == 1:
                delta_own[...] = jnp.where(place == 2, change, 0.0).astype(BF16)
            deltas[near * 128 : near * 128 + 128, :] = change
        windows = [
            near_cell(deltas[...], down - 1, step - 1) for down in range(3) for step in range(3)
        ]
        carried = jnp.dot(
            taps_back[...], jnp.concatenate(windows, axis=0), preferred_element_type=F32
        )
        carried = exact_dot(turned(carried, -32), pair_columns(False))
        carried = jnp.concatenate([carried, carried], axis=0)
        dense = None
        for layer in range(2):
            wide = [columns_last(skip[layer, row], 0) for row in range(2)]
            change = (jnp.concatenate(wide, axis=0) + carried) * slope(pre[layer])
            change = jnp.where(lanes(change.shape) < 32, change, 0.0).astype(BF16)
            out[layer] = change
            change = change.astype(F32)
            dense = change if dense is None else dense + turned(change, 32)
        dense_out[0] = dense.astype(BF16)

    outs = [
        ((1, 128, 128), BF16),
        ((2, 128, 128), BF16),
        ((9, 320, 128), BF16),
        ((128, 128), BF16),
    ]
    scratch = [((384, 128), F32)]
    return call(
        body, outs, scratch, 1 << 28,
        acts, *chips, skip_deep, *halo_z, *halo_y, skip, pre, weights, weights_back,
    )


def grad_deepest(shifts, delta):
    def body(shifts, delta, grad):
        for tap in range(9):
            grad[tap * 192 : tap * 192 + 192, :] = lax.dot_general(
                shifts[tap, 64:256, :], delta[...], NT, preferred_element_type=F32
            )

    return call(body, [((1728, 128), F32)], [], 1 << 27, shifts, delta)[0]


def diagonal(product, rows, chans, feats):
    place = lanes((3 * chans, 128)) // feats
    value = product[: 3 * chans]
    for row in range(1, rows):
        value = jnp.where(place == row, product[row * chans : (row + 3) * chans], value)
    turn = 64
    while turn >= feats:
        value = value + pltpu.roll(value, turn, 1)
        turn //= 2
    return value


def packed(tall, groups):
    size = tall.shape[0] // groups
    place = lanes((size, 128)) // (128 // groups)
    value = tall[:size, :]
    for group in range(1, groups):
        value = jnp.where(place == group, tall[group * size : (group + 1) * size, :], value)
    return value


def put_grads(tall, shifts, rows, offset, depth, delta, dims):
    count, chans, feats = dims
    for down in range(3):
        for step in range(3):
            at = (offset + down) * 128
            product = lax.dot_general(
                shifts[step, rows[0] : rows[1], at : at + depth * 128],
                delta,
                NT,
                preferred_element_type=F32,
            )
            tap = (down * 3 + step) * 3 * chans
            tall[tap : tap + 3 * chans, :] = diagonal(product, count, chans, feats)


def grad_quarter_of(act, delta):
    def body(act, delta, grad, shifts, tall):
        for layer in range(4):
            put_shifts(shifts, 0, layer, act[layer])
        both = jnp.concatenate([delta[0], delta[1]], axis=1)
        put_grads(tall, shifts, (0, 128), 0, 2, both, (2, 32, 64))
        grad[...] = packed(tall, 2)

    scratch = [((3, 128, 512), BF16), ((864, 128), F32)]
    return call(body, [((432, 128), F32)], scratch, 1 << 28, act, delta)[0]


def back_rest(
    delta, halo_z, halo_y, skip_half, halo_zs, halo_ys, pre_half, skip_full, pre_full,
    weights_quarter, weights_half, shifts_half, shifts_full, deep_grad, quarter_grad,
):
    def body(
        own, one, two, above, below, skip1, one1, two1, above1, below1, pre1, skip0, pre0,
        taps2, taps1, shifts1, shifts0, grad3, grad2, out, moved2, moved1, delta1, delta0, tall, flat,
    ):
        flags = place_of()
        even = flags[4] == 0
        for layer in range(6):
            block = layer // 2
            high, low = row_edges(above, below, block * 128, 128)
            middle = own[0]
            if block != 1:
                near, far = (two, one) if block == 0 else (one, two)
                middle = jnp.where(even, near[0], far[0])
                other = row_edges(above, below, (2 - block) * 128, 128)
                high, low = jnp.where(even, other[0], high), jnp.where(even, other[1], low)
            tiles = (high, middle, low)
            for part, tile in enumerate(tiles):
                tile = turned(tile.astype(F32), -32 * (layer % 2))
                tile = jnp.where(lanes(tile.shape) < 32, tile, 0.0).astype(BF16)
                put_shifts(moved2, part * 128, layer, tile)
        value = convolved(taps2, moved2, (0, 384), 4)

        def edge_at(place):
            found = row_edges(above1, below1, 240 + place // 2 * 32, 32)
            return [half_lanes(part, place % 2) for part in found]

        picks = pair_columns(False)
        row = lax.broadcasted_iota(jnp.int32, (192, 128), 0) // 32
        inside = lanes((192, 128)) < 64
        inside = inside & ((row > 0) | (flags[2])) & ((row < 5) | (flags[3]))
        for layer in range(6):
            if layer % 2 == 1 or layer == 0:
                at = (layer + 1) // 2 * 128
                carried = exact_dot(value[:, at : at + 128], picks)
                parts = [carried[part * 32 : part * 32 + 32] for part in (0, 1, 1, 2, 2, 3)]
                carried = jnp.concatenate(parts, axis=0)
            if 0 < layer < 5:
                high, low = edge_at(layer)
                middle = skip1[layer - 1]
            else:
                near, far = (two1, one1) if layer == 0 else (one1, two1)
                yes, no = edge_at(5 - layer), edge_at(layer)
                high, low = (jnp.where(even, yes[part], no[part]) for part in range(2))
                middle = jnp.where(even, near[192:320], far[192:320])
            parts = (high, middle, low)
            skip = jnp.concatenate(parts, axis=0).astype(F32)
            change = (skip + carried) * slope(pre1[layer + 1, 32:224])
            keep = inside
            if layer == 0:
                keep = keep & (flags[0])
            if layer == 5:
                keep = keep & (flags[1])
            change = jnp.where(keep, change, 0.0).astype(BF16)
            put_shifts(moved1, 0, layer, change)
            if 0 < layer < 5:
                delta1[:, (layer - 1) * 128 : layer * 128] = change[32:160]
        value = convolved(taps1, moved1, (0, 192), 4)
        for layer in range(8):
            if layer % 2 == 0:
                at = layer // 2 * 128
                carried = exact_dot(value[:, at : at + 128], picks)
                parts = [carried[part // 2 * 16 : part // 2 * 16 + 16] for part in range(8)]
                carried = jnp.concatenate(parts, axis=0)
            change = (skip0[layer].astype(F32) + carried) * slope(pre0[layer])
            delta0[:, layer * 128 : layer * 128 + 128] = change.astype(BF16)
        flat[:1728, :] = grad3[...]
        flat[1728:2160, :] = grad2[...]
        tall[...] = jnp.zeros_like(tall)
        put_grads(tall, shifts1, (32, 128), 2, 4, delta1[...], (4, 16, 32))
        flat[2160:2272, :] = packed(tall, 4)
        put_grads(tall, shifts0, (0, 160), 0, 8, delta0[...], (8, 16, 16))
        flat[2272:2328, :] = packed(tall, 8)
        flat[2328:, :] = jnp.zeros((2560 - 2328, 128), F32)
        for part in range(5):
            at = part * 512
            out[:, part * 128 : part * 128 + 128] = flat[at : at + 512, :].astype(BF16)

    scratch = [
        ((3, 384, 768), BF16),
        ((3, 192, 768), BF16),
        ((128, 512), BF16),
        ((128, 1024), BF16),
        ((448, 128), F32),
        ((2560, 128), F32),
    ]
    return call(
        body, [((512, 640), BF16)], scratch, 1 << 30,
        delta, *halo_z, *halo_y, skip_half, *halo_zs, *halo_ys, pre_half, skip_full, pre_full,
        weights_quarter, weights_half, shifts_half, shifts_full, deep_grad, quarter_grad,
    )[0]


def unpack(sums):
    def body(sums, full, half, quarter, eighth, whole, tall):
        for part in range(5):
            block = sums[:, part * 128 : part * 128 + 128]
            whole[part * 512 : part * 512 + 512, :] = block.astype(F32)

        def spread(out, source, chans):
            for down in range(3):
                for across in range(3):
                    for step in range(3):
                        at = ((down * 3 + across) * 3 + step) * chans
                        start = ((down * 3 + step) * 3 + across) * chans
                        out[at : at + chans, :] = source[
                            start : start + chans, : out.shape[1]
                        ]

        spread(eighth, whole, 64)
        for out, start, size, groups, chans in (
            (quarter, 1728, 432, 2, 32),
            (half, 2160, 112, 4, 16),
            (full, 2272, 56, 8, 16),
        ):
            dense = whole[start : start + size, :]
            for group in range(groups):
                tall[group * size : (group + 1) * size, :] = (
                    dense if group == 0 else pltpu.roll(dense, 128 - group * (128 // groups), 1)
                )
            spread(out, tall, chans)

    outs = [((432, 16), F32), ((432, 32), F32), ((864, 64), F32), ((1728, 128), F32)]
    scratch = [((2560, 128), F32), ((864, 128), F32)]
    return call(body, outs, scratch, 1 << 20, sums)


def pairs(axis):
    size = lax.axis_size(axis)
    between = [(i, i + 1) for i in range(1, size - 1, 2)]
    return [(i, i ^ 1) for i in range(size)], between + [(j, i) for i, j in between]


def swaps(to_one, to_two, axis=GZ):
    first, second = pairs(axis)
    return lax.ppermute(to_one, axis, first), lax.ppermute(to_two, axis, second)


def edge_rows(one, two, volume):
    def body(one, two, own, to_one, to_two):
        even = lax.axis_index("gy") % 2 == 0
        for place in range(10):
            block = one[0] if place == 0 else two[0] if place == 9 else own[place - 1]
            at = place * 16
            to_one[at : at + 16] = jnp.where(even, block[112:], block[:16])
            to_two[at : at + 16] = jnp.where(even, block[:16], block[112:])

    return call(body, [((160, 128), BF16)] * 2, [], 1 << 20, one, two, volume)


def edge_rows_half(one, two, act, skip_half, skip_deep):
    def body(one, two, act, skip1, skip3, to_one, to_two):
        even = lax.axis_index("gy") % 2 == 0

        def put(at, size, blocks):
            low, high = blocks
            packed_rows = []
            for rows in (slice(0, size), slice(low.shape[0] - size, low.shape[0])):
                packed_rows.append(
                    low[rows].astype(F32) + pltpu.roll(high[rows].astype(F32), 64, 1)
                )
            top, bottom = packed_rows
            to_one[at : at + size] = jnp.where(even, bottom, top).astype(BF16)
            to_two[at : at + size] = jnp.where(even, top, bottom).astype(BF16)

        def act_at(place):
            if 3 <= place < 7:
                return act[place - 3]
            at = place % 7 * 64
            return (one if place < 3 else two)[at : at + 64]

        def skip_at(place):
            if 0 < place < 5:
                return skip1[place - 1]
            return (one if place == 0 else two)[192:320]

        for pair in range(5):
            put(pair * 48, 48, (act_at(2 * pair), act_at(2 * pair + 1)))
        for pair in range(3):
            put(240 + pair * 32, 32, (skip_at(2 * pair), skip_at(2 * pair + 1)))
        for place, rows in enumerate((one[320:], skip3[...], two[320:])):
            at = 336 + place * 16
            to_one[at : at + 16] = rows
            to_two[at : at + 16] = rows

    return call(
        body, [((384, 128), BF16)] * 2, [], 1 << 20, one, two, act, skip_half, skip_deep
    )


def laid_out(array):
    chans, depth, height, width = array.shape
    rows = jnp.transpose(array, (1, 2, 0, 3)).reshape(depth, height * chans, width)
    return jnp.pad(rows, ((0, 0), (0, 0), (0, 128 - width)))


def copies(part, count):
    def body(part, out):
        value = part[...].astype(BF16)
        for copy in range(count):
            out[copy] = value

    return call(body, [((count,) + part.shape, BF16)], [], 1 << 20, part)[0]


def summed(terms):
    inner, outer = ("x", "c"), ("z", "gy")
    first, second = lax.axis_size(inner), lax.axis_size(outer)
    rows, width = terms.shape[0] // first, terms.shape[1]
    pieces = lax.all_to_all(terms.reshape(first, rows, width), inner, 0, 0)
    part = jnp.sum(pieces.astype(F32), axis=0)
    pieces = lax.all_to_all(part, outer, 0, 0, tiled=True)
    done = jnp.sum(pieces.reshape(second, -1, width), axis=0)
    spread = jnp.broadcast_to(done[None], (second,) + done.shape).reshape(rows, width)
    part = lax.all_to_all(lax.optimization_barrier(spread), outer, 0, 0, tiled=True)
    return lax.all_to_all(copies(part, first), inner, 0, 0).reshape(terms.shape)


def on_device(
    volume,
    kernel_full,
    kernel_half,
    kernel_quarter,
    kernel_eighth,
    skip_full,
    skip_half,
    skip_quarter,
    skip_eighth,
):
    kernels = (kernel_full, kernel_half, kernel_quarter, kernel_eighth)
    volume = laid_out(volume)
    even = lax.axis_index("c") == 0
    first, last = volume[:1], volume[7:]
    one, two = swaps(jnp.where(even, last, first), jnp.where(even, first, last))
    skip3 = jnp.transpose(skip_eighth, (1, 2, 3, 0)).reshape(16, 128)
    skip2 = jnp.transpose(skip_quarter, (1, 2, 3, 0))
    one, two, skip_full, skip_half, kernels = lax.optimization_barrier(
        (one, two, skip_full, skip_half, kernels)
    )
    skip0, skip1 = laid_out(skip_full), laid_out(skip_half)

    halo_y = swaps(*edge_rows(one, two, volume), "gy")
    dims = ((8, 16, 16), (4, 16, 32), (2, 32, 64), (1, 64, 128))
    w0, w1, w2, w3, t1, t2, t3 = prepare(kernels, dims)
    pre0, act1, shifts0, to_one, to_two = forward_full(
        volume, (one, two), halo_y, w0, skip1, skip3
    )
    halo_z1 = one, two = swaps(to_one, to_two)

    halo_y1 = swaps(*edge_rows_half(one, two, act1, skip1, skip3), "gy")
    pre1, act2, pre2, act3, shifts1 = forward_half(act1, halo_z1, halo_y1, w1, w2)
    columns = lax.axis_size("gy")
    many = (2 * columns,) + act3.shape
    acts = lax.all_to_all(
        lax.optimization_barrier(jnp.broadcast_to(act3[None], many)), ("c", "gy"), 0, 0
    )
    chips = swaps(acts, acts, ("x", "z"))
    dense2, delta2, shifts3, delta3 = deepest(
        columns, acts, chips, skip3, halo_z1, halo_y1, skip2, pre2, w3, t3
    )
    halo_z = one, two = swaps(dense2, dense2)
    block = jnp.concatenate([one, dense2, two], axis=0).reshape(384, 128)
    halo_y = swaps(block, block, "gy")
    grad3 = grad_deepest(shifts3, delta3)
    grad2 = grad_quarter_of(act2, delta2)
    terms = back_rest(
        dense2, halo_z, halo_y, skip1, halo_z1, halo_y1, pre1, skip0, pre0,
        t2, t1, shifts1, shifts0, grad3, grad2,
    )
    outs = unpack(summed(terms))
    return tuple(out.reshape(kernel.shape) for out, kernel in zip(outs, kernels))


def solution(mesh):
    fine = jax.sharding.Mesh(mesh.devices.reshape(4, 8, 2, 8), ("x", "z", "c", "gy"))
    return mapped(fine)


def mapped(fine):
    block = P(None, GZ, "gy", None)
    return jax.shard_map(
        on_device,
        mesh=fine,
        in_specs=(block, P(), P(), P(), P(), block, block, block, block),
        out_specs=(P(), P(), P(), P()),
        check_vma=False,
    )
```

```python
import jax
import jax.numpy as jnp
from jax import lax
from jax.experimental import pallas as pl
from jax.experimental.pallas import tpu as pltpu
from jax.sharding import PartitionSpec as P

F32 = jnp.float32
BF16 = jnp.bfloat16
GZ = ("x", "z", "c")
VMEM_BYTES = 14 * 1024 * 1024
NT = (((1,), (1,)), ((), ()))


def call(body, outs, scratch, flops, *args):
    return pl.pallas_call(
        body,
        out_shape=tuple(jax.ShapeDtypeStruct(shape, dtype) for shape, dtype in outs),
        in_specs=[pl.BlockSpec(memory_space=pltpu.VMEM) for _ in args],
        out_specs=tuple(pl.BlockSpec(memory_space=pltpu.VMEM) for _ in outs),
        scratch_shapes=[pltpu.VMEM(shape, dtype) for shape, dtype in scratch],
        compiler_params=pltpu.CompilerParams(vmem_limit_bytes=VMEM_BYTES),
        cost_estimate=pl.CostEstimate(flops=flops, bytes_accessed=1 << 20, transcendentals=0),
    )(*args)


def place_of():
    depth_at, row_at = lax.axis_index(GZ), lax.axis_index("gy")
    return (
        depth_at > 0,
        depth_at < lax.axis_size(GZ) - 1,
        row_at > 0,
        row_at < lax.axis_size("gy") - 1,
        lax.axis_index("c"),
        row_at,
    )


def row_edges(first, second, start, size):
    rule = lax.axis_index("gy") % 2 == 0
    one, two = (part[start : start + size].astype(F32) for part in (first, second))
    return jnp.where(rule, two, one).astype(BF16), jnp.where(rule, one, two).astype(BF16)


def half_lanes(tile, odd):
    tile = pltpu.roll(tile.astype(F32), 64, 1) if odd else tile.astype(F32)
    return jnp.where(lanes(tile.shape) < 64, tile, 0.0).astype(BF16)


def lanes(shape):
    return lax.broadcasted_iota(jnp.int32, shape, 1)


def at_column(tile, step):
    if step == 0:
        return tile
    moved = pltpu.roll(tile.astype(F32), (-step) % 128, 1)
    edge = 127 if step > 0 else 0
    return jnp.where(lanes(tile.shape) == edge, 0.0, moved).astype(BF16)


def put_shifts(shifts, row, layer, tile):
    for step in range(3):
        shifts[step, row : row + tile.shape[0], layer * 128 : layer * 128 + 128] = at_column(
            tile, step - 1
        )


def convolved(weights, shifts, rows, depth):
    windows = [
        shifts[step, rows[0] : rows[1], down * 128 : (down + depth) * 128]
        for down in range(3)
        for step in range(3)
    ]
    size = 9 * (rows[1] - rows[0])
    return jnp.dot(
        weights[:, :size], jnp.concatenate(windows, axis=0), preferred_element_type=F32
    )


def sigmoid(values):
    return 1.0 / (1.0 + jnp.exp(-values))


def slope(values):
    sig = sigmoid(values)
    return sig * (1.0 + values * (1.0 - sig))


def exact_dot(values, picks):
    high = values.astype(BF16)
    rest = values - high.astype(F32)
    middle = rest.astype(BF16)
    low = (rest - middle.astype(F32)).astype(BF16)
    total = jnp.dot(low, picks, preferred_element_type=F32)
    total = total + jnp.dot(middle, picks, preferred_element_type=F32)
    return total + jnp.dot(high, picks, preferred_element_type=F32)


def pair_columns(down):
    rows = lax.broadcasted_iota(jnp.int32, (128, 128), 0)
    columns = lax.broadcasted_iota(jnp.int32, (128, 128), 1)
    hit = (rows // 2 == columns) if down else (columns // 2 == rows)
    return jnp.where(hit, 0.125, 0.0).astype(BF16)


def pooled(first, second, channels, width):
    both = first + second
    blocks = both.shape[0] // (2 * channels)
    rows = []
    for block in range(blocks):
        start = 2 * block * channels
        rows.append(
            both[start : start + channels] + both[start + channels : start + 2 * channels]
        )
    summed = rows[0] if blocks == 1 else jnp.concatenate(rows, axis=0)
    mean = exact_dot(summed, pair_columns(True))
    return jnp.where(lanes(mean.shape) < width // 2, mean, 0.0)


def silu(values):
    return values * sigmoid(values)


def prepare(kernels, dims):
    def body(*refs):
        ins, outs, wide = refs[:4], refs[4:11], refs[11]
        for level, (rows, chans, feats) in enumerate(dims):
            source, taps = ins[level][...], outs[level]
            picks = (
                lax.broadcasted_iota(jnp.int32, (feats, 128), 0)
                == lax.broadcasted_iota(jnp.int32, (feats, 128), 1) % feats
            )
            spread = jnp.dot(
                source, jnp.where(picks, 1.0, 0.0).astype(BF16), preferred_element_type=F32
            )
            size = taps.shape[1]
            used = 9 * (rows + 2) * chans
            if used < size:
                wide[used:size, :] = jnp.zeros((size - used, 128), F32)
            place = lanes((chans, 128)) // feats
            for down in range(3):
                for step in range(3):
                    for row in range(rows + 2):
                        value = jnp.zeros((chans, 128), F32)
                        for across in range(3):
                            at = ((down * 3 + across) * 3 + step) * chans
                            value = jnp.where(
                                place == row - across, spread[at : at + chans], value
                            )
                        at = ((down * 3 + step) * (rows + 2) + row) * chans
                        wide[at : at + chans, :] = value
            taps[...] = wide[:size, :].T.astype(BF16)
        for level in range(1, 4):
            rows, chans, feats = dims[level]
            if level == 2:
                rows = 4
            source, taps = ins[level][...], outs[3 + level]
            size = (rows + 2) * feats
            picks = (
                lax.broadcasted_iota(jnp.int32, (feats, size), 0)
                == lax.broadcasted_iota(jnp.int32, (feats, size), 1) % feats
            )
            spread = jnp.dot(
                source, jnp.where(picks, 1.0, 0.0).astype(BF16), preferred_element_type=F32
            )
            place = lanes((chans, size)) // feats
            for down in range(3):
                for step in range(3):
                    for row in range(rows):
                        value = jnp.zeros((chans, size), F32)
                        for across in range(3):
                            at = (((2 - down) * 3 + 2 - across) * 3 + 2 - step) * chans
                            value = jnp.where(
                                place == row + across, spread[at : at + chans], value
                            )
                        at = (down * 3 + step) * size
                        taps[row * chans : (row + 1) * chans, at : at + size] = value.astype(BF16)

    shapes = [(128, 1536), (128, 896), (128, 1152), (128, 1792)]
    shapes += [(64, 1728), (128, 3456), (64, 3456)]
    flat = [kernel.reshape(-1, kernel.shape[-1]) for kernel in kernels]
    return call(body, [(s, BF16) for s in shapes], [((1792, 128), F32)], 1 << 27, *flat)


def forward_full(volume, halo_z, halo_y, weights, skip_half, skip_deep):
    def body(own, one, two, above, below, taps, skip1, skip3, pre, act, shifts, to_one, to_two):
        even = lax.axis_index("c") == 0
        for layer in range(10):
            if 0 < layer < 9:
                high, low = row_edges(above, below, layer * 16, 16)
                middle = own[layer - 1]
            else:
                near, far = (two, one) if layer == 0 else (one, two)
                at = (144, 0) if layer == 0 else (0, 144)
                yes, no = (row_edges(above, below, start, 16) for start in at)
                high, low = (jnp.where(even, yes[part], no[part]) for part in range(2))
                middle = jnp.where(even, near[0], far[0])
            parts = (high, middle, low)
            put_shifts(shifts, 0, layer, parts[0])
            put_shifts(shifts, 16, layer, parts[1])
            put_shifts(shifts, 144, layer, parts[2])
        value = convolved(taps, shifts, (0, 160), 8)
        active = silu(value)
        for layer in range(8):
            pre[layer] = value[:, layer * 128 : layer * 128 + 128]
        for layer in range(4):
            at = layer * 256
            act[layer] = pooled(
                active[:, at : at + 128], active[:, at + 128 : at + 256], 16, 128
            ).astype(BF16)
        for layer in range(3):
            rows = slice(layer * 64, layer * 64 + 64)
            to_one[rows] = jnp.where(even, act[layer + 1], act[layer])
            to_two[rows] = jnp.where(even, act[layer], act[layer + 1])
        to_one[192:320] = jnp.where(even, skip1[3], skip1[0])
        to_two[192:320] = jnp.where(even, skip1[0], skip1[3])
        to_one[320:] = skip3[...]
        to_two[320:] = skip3[...]

    outs = [((8, 128, 128), F32), ((4, 64, 128), BF16), ((3, 160, 1280), BF16)]
    outs += [((336, 128), BF16), ((336, 128), BF16)]
    return call(
        body, outs, [], 1 << 29, volume, *halo_z, *halo_y, weights, skip_half, skip_deep
    )


def forward_half(act, halo_z, halo_y, weights_half, weights_quarter):
    def body(
        own, one, two, above, below, taps, next_taps, pre, act, next_pre, deep, shifts, inner
    ):
        flags = place_of()
        even = flags[4] == 0
        def edge_at(place):
            found = row_edges(above, below, place // 2 * 48, 48)
            return [half_lanes(part, place % 2) for part in found]

        for layer in range(10):
            if 3 <= layer < 7:
                middle = own[layer - 3]
                edges = edge_at(layer)
            else:
                near, far = (two, one) if layer < 3 else (one, two)
                at = layer % 7 * 64
                middle = jnp.where(even, near[at : at + 64], far[at : at + 64])
                at = layer % 7
                yes, no = (edge_at(place) for place in ((7 + at, at) if layer < 3 else (at, 7 + at)))
                edges = [jnp.where(even, yes[part], no[part]) for part in range(2)]
            put_shifts(shifts, 0, layer, edges[0])
            put_shifts(shifts, 48, layer, middle)
            put_shifts(shifts, 112, layer, edges[1])
        for part in range(2):
            value = convolved(taps, shifts, (part * 64, part * 64 + 96), 8)
            for layer in range(8):
                pre[layer, part * 128 : part * 128 + 128, :] = value[
                    :, layer * 128 : layer * 128 + 128
                ]
        row = lax.broadcasted_iota(jnp.int32, (128, 128), 0) // 32
        inside = (row > 0) | (flags[2])
        inside = inside & ((row < 3) | (flags[3]))
        for layer in range(4):
            value = pooled(silu(pre[2 * layer]), silu(pre[2 * layer + 1]), 32, 64)
            keep = inside
            if layer == 0:
                keep = keep & (flags[0])
            if layer == 3:
                keep = keep & (flags[1])
            value = jnp.where(keep, value, 0.0).astype(BF16)
            act[layer] = value
            put_shifts(inner, 0, layer, value)
        value = convolved(next_taps, inner, (0, 128), 2)
        next_pre[0] = value[:, :128]
        next_pre[1] = value[:, 128:]
        coarse = pooled(silu(value[:, :128]), silu(value[:, 128:]), 64, 32)
        dense = coarse[:8].astype(BF16).astype(F32)
        for group in range(1, 8):
            part = coarse[group * 8 : group * 8 + 8].astype(BF16).astype(F32)
            dense = dense + pltpu.roll(part, group * 16, 1)
        deep[...] = dense

    outs = [
        ((8, 256, 128), F32),
        ((4, 128, 128), BF16),
        ((2, 128, 128), F32),
        ((8, 128), F32),
        ((3, 160, 1280), BF16),
    ]
    return call(
        body,
        outs,
        [((3, 128, 512), BF16)],
        1 << 29,
        act,
        *halo_z,
        *halo_y,
        weights_half,
        weights_quarter,
    )


def turned(tile, by):
    return tile if by % 128 == 0 else pltpu.roll(tile, by % 128, 1)


def near_cell(tile, layer_step, step):
    moved = turned(tile, -(16 * layer_step + step))
    column = lanes(tile.shape) % 16
    if step > 0:
        moved = jnp.where(column == 15, 0.0, moved)
    if step < 0:
        moved = jnp.where(column == 0, 0.0, moved)
    return moved.astype(BF16)


def columns_last(tile, start):
    width = tile.shape[0]
    column = lax.broadcasted_iota(jnp.int32, (width, 128), 0)
    picks = jnp.where(lanes((width, 128)) == column + start, 1.0, 0.0).astype(BF16)
    return lax.dot_general(tile, picks, (((0,), (0,)), ((), ())), preferred_element_type=F32)


def opened(dense, layer):
    parts = [turned(dense, 16 * layer - 16 * group) for group in range(8)]
    return jnp.concatenate(parts, axis=0)


def deepest(columns, acts, chips, skip_deep, halo_z, halo_y, skip, pre, weights, weights_back):
    def body(
        acts, chip_one, chip_two, skip_own, skip_one, skip_two, skip_above, skip_below, skip, pre,
        taps, taps_back, dense_out, out, shifts, delta_own, deltas,
    ):
        flags = place_of()
        core, row_at = flags[4], flags[5]
        place = lanes((64, 128)) // 16

        ahead = lax.axis_index("z") % 2 == 0

        def cells(position, row):
            at = position % 2 * columns + row
            if position // 2 == 1:
                return acts[at]
            if position // 2 == 0:
                return jnp.where(ahead, chip_two[at], chip_one[at])
            return jnp.where(ahead, chip_one[at], chip_two[at])

        for near in range(5):
            row = row_at + near - 2
            valid = (row >= 0) & (row < columns)
            row = jnp.clip(row, 0, columns - 1)
            value = jnp.zeros((64, 128), F32)
            for layer in range(5):
                dense = jnp.where(core == 0, cells(layer, row), cells(layer + 1, row))
                value = jnp.where(place == layer, opened(dense, layer), value)
            value = jnp.where(valid, value, 0.0)
            for down in range(3):
                for step in range(3):
                    shifts[down * 3 + step, near * 64 : near * 64 + 64, :] = near_cell(
                        value, down - 1, step - 1
                    )
        place = lanes((128, 128)) // 16
        for near in range(3):
            window = shifts[:, near * 64 : near * 64 + 192, :].reshape(1728, 128)
            value = jnp.dot(taps[:, :1728], window, preferred_element_type=F32)
            upstream = jnp.zeros((128, 128), F32)
            for layer in range(3):
                if near != 1:
                    yes = row_edges(skip_above, skip_below, 368 - layer * 16, 16)[near // 2]
                    no = row_edges(skip_above, skip_below, 336 + layer * 16, 16)[near // 2]
                    dense = jnp.where(core == 0, yes, no)
                elif layer == 1:
                    dense = skip_own[...]
                else:
                    ends = (skip_two, skip_one) if layer == 0 else (skip_one, skip_two)
                    dense = jnp.where(core == 0, ends[0][320:], ends[1][320:])
                upstream = upstream + columns_last(dense, 16 * layer + 16)
            keep = (place == 2) | ((place == 1) & (flags[0])) | ((place == 3) & (flags[1]))
            if near != 1:
                keep = keep & (flags[2 + near // 2])
            change = jnp.where(keep, upstream * slope(value), 0.0).astype(BF16).astype(F32)
            if near == 1:
                delta_own[...] = jnp.where(place == 2, change, 0.0).astype(BF16)
            deltas[near * 128 : near * 128 + 128, :] = change
        windows = [
            near_cell(deltas[...], down - 1, step - 1) for down in range(3) for step in range(3)
        ]
        carried = jnp.dot(
            taps_back[...], jnp.concatenate(windows, axis=0), preferred_element_type=F32
        )
        carried = exact_dot(turned(carried, -32), pair_columns(False))
        carried = jnp.concatenate([carried, carried], axis=0)
        dense = None
        for layer in range(2):
            wide = [columns_last(skip[layer, row], 0) for row in range(2)]
            change = (jnp.concatenate(wide, axis=0) + carried) * slope(pre[layer])
            change = jnp.where(lanes(change.shape) < 32, change, 0.0).astype(BF16)
            out[layer] = change
            change = change.astype(F32)
            dense = change if dense is None else dense + turned(change, 32)
        dense_out[0] = dense.astype(BF16)

    outs = [
        ((1, 128, 128), BF16),
        ((2, 128, 128), BF16),
        ((9, 320, 128), BF16),
        ((128, 128), BF16),
    ]
    scratch = [((384, 128), F32)]
    return call(
        body, outs, scratch, 1 << 28,
        acts, *chips, skip_deep, *halo_z, *halo_y, skip, pre, weights, weights_back,
    )


def grad_deepest(shifts, delta):
    def body(shifts, delta, grad):
        for tap in range(9):
            grad[tap * 192 : tap * 192 + 192, :] = lax.dot_general(
                shifts[tap, 64:256, :], delta[...], NT, preferred_element_type=F32
            )

    return call(body, [((1728, 128), F32)], [], 1 << 27, shifts, delta)[0]


def diagonal(product, rows, chans, feats):
    place = lanes((3 * chans, 128)) // feats
    value = product[: 3 * chans]
    for row in range(1, rows):
        value = jnp.where(place == row, product[row * chans : (row + 3) * chans], value)
    turn = 64
    while turn >= feats:
        value = value + pltpu.roll(value, turn, 1)
        turn //= 2
    return value


def packed(tall, groups):
    size = tall.shape[0] // groups
    place = lanes((size, 128)) // (128 // groups)
    value = tall[:size, :]
    for group in range(1, groups):
        value = jnp.where(place == group, tall[group * size : (group + 1) * size, :], value)
    return value


def put_grads(tall, shifts, rows, offset, depth, delta, dims):
    count, chans, feats = dims
    for down in range(3):
        for step in range(3):
            at = (offset + down) * 128
            product = lax.dot_general(
                shifts[step, rows[0] : rows[1], at : at + depth * 128],
                delta,
                NT,
                preferred_element_type=F32,
            )
            tap = (down * 3 + step) * 3 * chans
            tall[tap : tap + 3 * chans, :] = diagonal(product, count, chans, feats)


def grad_quarter_of(act, delta):
    def body(act, delta, grad, shifts, tall):
        for layer in range(4):
            put_shifts(shifts, 0, layer, act[layer])
        both = jnp.concatenate([delta[0], delta[1]], axis=1)
        put_grads(tall, shifts, (0, 128), 0, 2, both, (2, 32, 64))
        grad[...] = packed(tall, 2)

    scratch = [((3, 128, 512), BF16), ((864, 128), F32)]
    return call(body, [((432, 128), F32)], scratch, 1 << 28, act, delta)[0]


def back_rest(
    delta, halo_z, halo_y, skip_half, halo_zs, halo_ys, pre_half, skip_full, pre_full,
    weights_quarter, weights_half, shifts_half, shifts_full, deep_grad, quarter_grad,
):
    def body(
        own, one, two, above, below, skip1, one1, two1, above1, below1, pre1, skip0, pre0,
        taps2, taps1, shifts1, shifts0, grad3, grad2, out, moved2, moved1, delta1, delta0, tall, flat,
    ):
        flags = place_of()
        even = flags[4] == 0
        for layer in range(6):
            block = layer // 2
            high, low = row_edges(above, below, block * 128, 128)
            middle = own[0]
            if block != 1:
                near, far = (two, one) if block == 0 else (one, two)
                middle = jnp.where(even, near[0], far[0])
                other = row_edges(above, below, (2 - block) * 128, 128)
                high, low = jnp.where(even, other[0], high), jnp.where(even, other[1], low)
            tiles = (high, middle, low)
            for part, tile in enumerate(tiles):
                tile = turned(tile.astype(F32), -32 * (layer % 2))
                tile = jnp.where(lanes(tile.shape) < 32, tile, 0.0).astype(BF16)
                put_shifts(moved2, part * 128, layer, tile)
        value = convolved(taps2, moved2, (0, 384), 4)

        def edge_at(place):
            found = row_edges(above1, below1, 240 + place // 2 * 32, 32)
            return [half_lanes(part, place % 2) for part in found]

        picks = pair_columns(False)
        row = lax.broadcasted_iota(jnp.int32, (192, 128), 0) // 32
        inside = lanes((192, 128)) < 64
        inside = inside & ((row > 0) | (flags[2])) & ((row < 5) | (flags[3]))
        for layer in range(6):
            if layer % 2 == 1 or layer == 0:
                at = (layer + 1) // 2 * 128
                carried = exact_dot(value[:, at : at + 128], picks)
                parts = [carried[part * 32 : part * 32 + 32] for part in (0, 1, 1, 2, 2, 3)]
                carried = jnp.concatenate(parts, axis=0)
            if 0 < layer < 5:
                high, low = edge_at(layer)
                middle = skip1[layer - 1]
            else:
                near, far = (two1, one1) if layer == 0 else (one1, two1)
                yes, no = edge_at(5 - layer), edge_at(layer)
                high, low = (jnp.where(even, yes[part], no[part]) for part in range(2))
                middle = jnp.where(even, near[192:320], far[192:320])
            parts = (high, middle, low)
            skip = jnp.concatenate(parts, axis=0).astype(F32)
            change = (skip + carried) * slope(pre1[layer + 1, 32:224])
            keep = inside
            if layer == 0:
                keep = keep & (flags[0])
            if layer == 5:
                keep = keep & (flags[1])
            change = jnp.where(keep, change, 0.0).astype(BF16)
            put_shifts(moved1, 0, layer, change)
            if 0 < layer < 5:
                delta1[:, (layer - 1) * 128 : layer * 128] = change[32:160]
        value = convolved(taps1, moved1, (0, 192), 4)
        for layer in range(8):
            if layer % 2 == 0:
                at = layer // 2 * 128
                carried = exact_dot(value[:, at : at + 128], picks)
                parts = [carried[part // 2 * 16 : part // 2 * 16 + 16] for part in range(8)]
                carried = jnp.concatenate(parts, axis=0)
            change = (skip0[layer].astype(F32) + carried) * slope(pre0[layer])
            delta0[:, layer * 128 : layer * 128 + 128] = change.astype(BF16)
        flat[:1728, :] = grad3[...]
        flat[1728:2160, :] = grad2[...]
        tall[...] = jnp.zeros_like(tall)
        put_grads(tall, shifts1, (32, 128), 2, 4, delta1[...], (4, 16, 32))
        flat[2160:2272, :] = packed(tall, 4)
        put_grads(tall, shifts0, (0, 160), 0, 8, delta0[...], (8, 16, 16))
        flat[2272:2328, :] = packed(tall, 8)
        flat[2328:, :] = jnp.zeros((2560 - 2328, 128), F32)
        for part in range(5):
            at = part * 512
            out[:, part * 128 : part * 128 + 128] = flat[at : at + 512, :].astype(BF16)

    scratch = [
        ((3, 384, 768), BF16),
        ((3, 192, 768), BF16),
        ((128, 512), BF16),
        ((128, 1024), BF16),
        ((448, 128), F32),
        ((2560, 128), F32),
    ]
    return call(
        body, [((512, 640), BF16)], scratch, 1 << 30,
        delta, *halo_z, *halo_y, skip_half, *halo_zs, *halo_ys, pre_half, skip_full, pre_full,
        weights_quarter, weights_half, shifts_half, shifts_full, deep_grad, quarter_grad,
    )[0]


def unpack(mine, other):
    def body(mine, other, full, half, quarter, eighth, whole, tall):
        even = lax.axis_index("c") == 0
        count, size = mine.shape[0], mine.shape[1]
        for at in range(count):
            own, partner = mine[at].astype(F32), other[at].astype(F32)
            for core in range(2):
                chunk = jnp.where(even, *((own, partner) if core == 0 else (partner, own)))
                for part in range(5):
                    row = part * 512 + (2 * at + core) * size
                    whole[row : row + size, :] = chunk[:, part * 128 : part * 128 + 128]

        def spread(out, source, chans):
            for down in range(3):
                for across in range(3):
                    for step in range(3):
                        at = ((down * 3 + across) * 3 + step) * chans
                        start = ((down * 3 + step) * 3 + across) * chans
                        out[at : at + chans, :] = source[
                            start : start + chans, : out.shape[1]
                        ]

        spread(eighth, whole, 64)
        for out, start, size, groups, chans in (
            (quarter, 1728, 432, 2, 32),
            (half, 2160, 112, 4, 16),
            (full, 2272, 56, 8, 16),
        ):
            dense = whole[start : start + size, :]
            for group in range(groups):
                tall[group * size : (group + 1) * size, :] = (
                    dense if group == 0 else pltpu.roll(dense, 128 - group * (128 // groups), 1)
                )
            spread(out, tall, chans)

    outs = [((432, 16), F32), ((432, 32), F32), ((864, 64), F32), ((1728, 128), F32)]
    scratch = [((2560, 128), F32), ((864, 128), F32)]
    return call(body, outs, scratch, 1 << 20, mine, other)


def pairs(axis):
    size = lax.axis_size(axis)
    between = [(i, i + 1) for i in range(1, size - 1, 2)]
    return [(i, i ^ 1) for i in range(size)], between + [(j, i) for i, j in between]


def swaps(to_one, to_two, axis=GZ):
    first, second = pairs(axis)
    return lax.ppermute(to_one, axis, first), lax.ppermute(to_two, axis, second)


def edge_rows(one, two, volume):
    def body(one, two, own, to_one, to_two):
        even = lax.axis_index("gy") % 2 == 0
        for place in range(10):
            block = one[0] if place == 0 else two[0] if place == 9 else own[place - 1]
            at = place * 16
            to_one[at : at + 16] = jnp.where(even, block[112:], block[:16])
            to_two[at : at + 16] = jnp.where(even, block[:16], block[112:])

    return call(body, [((160, 128), BF16)] * 2, [], 1 << 20, one, two, volume)


def edge_rows_half(one, two, act, skip_half, skip_deep):
    def body(one, two, act, skip1, skip3, to_one, to_two):
        even = lax.axis_index("gy") % 2 == 0

        def put(at, size, blocks):
            low, high = blocks
            packed_rows = []
            for rows in (slice(0, size), slice(low.shape[0] - size, low.shape[0])):
                packed_rows.append(
                    low[rows].astype(F32) + pltpu.roll(high[rows].astype(F32), 64, 1)
                )
            top, bottom = packed_rows
            to_one[at : at + size] = jnp.where(even, bottom, top).astype(BF16)
            to_two[at : at + size] = jnp.where(even, top, bottom).astype(BF16)

        def act_at(place):
            if 3 <= place < 7:
                return act[place - 3]
            at = place % 7 * 64
            return (one if place < 3 else two)[at : at + 64]

        def skip_at(place):
            if 0 < place < 5:
                return skip1[place - 1]
            return (one if place == 0 else two)[192:320]

        for pair in range(5):
            put(pair * 48, 48, (act_at(2 * pair), act_at(2 * pair + 1)))
        for pair in range(3):
            put(240 + pair * 32, 32, (skip_at(2 * pair), skip_at(2 * pair + 1)))
        for place, rows in enumerate((one[320:], skip3[...], two[320:])):
            at = 336 + place * 16
            to_one[at : at + 16] = rows
            to_two[at : at + 16] = rows

    return call(
        body, [((384, 128), BF16)] * 2, [], 1 << 20, one, two, act, skip_half, skip_deep
    )


def laid_out(array):
    chans, depth, height, width = array.shape
    rows = jnp.transpose(array, (1, 2, 0, 3)).reshape(depth, height * chans, width)
    return jnp.pad(rows, ((0, 0), (0, 0), (0, 128 - width)))


def copies(part, count):
    def body(part, out):
        value = part[...].astype(BF16)
        for copy in range(count):
            out[copy] = value

    return call(body, [((count,) + part.shape, BF16)], [], 1 << 20, part)[0]


def summed(terms):
    inner, outer = ("x", "c"), ("z", "gy")
    first, second = lax.axis_size(inner), lax.axis_size(outer)
    rows, width = terms.shape[0] // first, terms.shape[1]
    pieces = lax.all_to_all(terms.reshape(first, rows, width), inner, 0, 0)
    part = jnp.sum(pieces.astype(F32), axis=0)
    pieces = lax.all_to_all(part, outer, 0, 0, tiled=True)
    done = jnp.sum(pieces.reshape(second, -1, width), axis=0)
    spread = jnp.broadcast_to(done[None], (second,) + done.shape).reshape(rows, width)
    part = lax.all_to_all(lax.optimization_barrier(spread), outer, 0, 0, tiled=True)
    mine = lax.all_to_all(copies(part, lax.axis_size("x")), "x", 0, 0)
    return mine, lax.ppermute(mine, "c", [(0, 1), (1, 0)])


def on_device(
    volume,
    kernel_full,
    kernel_half,
    kernel_quarter,
    kernel_eighth,
    skip_full,
    skip_half,
    skip_quarter,
    skip_eighth,
):
    kernels = (kernel_full, kernel_half, kernel_quarter, kernel_eighth)
    volume = laid_out(volume)
    even = lax.axis_index("c") == 0
    first, last = volume[:1], volume[7:]
    one, two = swaps(jnp.where(even, last, first), jnp.where(even, first, last))
    skip3 = jnp.transpose(skip_eighth, (1, 2, 3, 0)).reshape(16, 128)
    skip2 = jnp.transpose(skip_quarter, (1, 2, 3, 0))
    one, two, skip_full, skip_half, kernels = lax.optimization_barrier(
        (one, two, skip_full, skip_half, kernels)
    )
    skip0, skip1 = laid_out(skip_full), laid_out(skip_half)

    halo_y = swaps(*edge_rows(one, two, volume), "gy")
    dims = ((8, 16, 16), (4, 16, 32), (2, 32, 64), (1, 64, 128))
    w0, w1, w2, w3, t1, t2, t3 = prepare(kernels, dims)
    pre0, act1, shifts0, to_one, to_two = forward_full(
        volume, (one, two), halo_y, w0, skip1, skip3
    )
    halo_z1 = one, two = swaps(to_one, to_two)

    halo_y1 = swaps(*edge_rows_half(one, two, act1, skip1, skip3), "gy")
    pre1, act2, pre2, act3, shifts1 = forward_half(act1, halo_z1, halo_y1, w1, w2)
    columns = lax.axis_size("gy")
    many = (2 * columns,) + act3.shape
    acts = lax.all_to_all(
        lax.optimization_barrier(jnp.broadcast_to(act3[None], many)), ("c", "gy"), 0, 0
    )
    chips = swaps(acts, acts, ("x", "z"))
    dense2, delta2, shifts3, delta3 = deepest(
        columns, acts, chips, skip3, halo_z1, halo_y1, skip2, pre2, w3, t3
    )
    halo_z = one, two = swaps(dense2, dense2)
    block = jnp.concatenate([one, dense2, two], axis=0).reshape(384, 128)
    halo_y = swaps(block, block, "gy")
    grad3 = grad_deepest(shifts3, delta3)
    grad2 = grad_quarter_of(act2, delta2)
    terms = back_rest(
        dense2, halo_z, halo_y, skip1, halo_z1, halo_y1, pre1, skip0, pre0,
        t2, t1, shifts1, shifts0, grad3, grad2,
    )
    outs = unpack(*summed(terms))
    return tuple(out.reshape(kernel.shape) for out, kernel in zip(outs, kernels))


def solution(mesh):
    fine = jax.sharding.Mesh(mesh.devices.reshape(4, 8, 2, 8), ("x", "z", "c", "gy"))
    return mapped(fine)


def mapped(fine):
    block = P(None, GZ, "gy", None)
    return jax.shard_map(
        on_device,
        mesh=fine,
        in_specs=(block, P(), P(), P(), P(), block, block, block, block),
        out_specs=(P(), P(), P(), P()),
        check_vma=False,
    )
```

```python
import jax
import jax.numpy as jnp
from jax import lax
from jax.experimental import pallas as pl
from jax.experimental.pallas import tpu as pltpu
from jax.sharding import PartitionSpec as P

F32 = jnp.float32
BF16 = jnp.bfloat16
GZ = ("x", "z", "c")
VMEM_BYTES = 14 * 1024 * 1024
NT = (((1,), (1,)), ((), ()))


def call(body, outs, scratch, flops, *args):
    return pl.pallas_call(
        body,
        out_shape=tuple(jax.ShapeDtypeStruct(shape, dtype) for shape, dtype in outs),
        in_specs=[pl.BlockSpec(memory_space=pltpu.VMEM) for _ in args],
        out_specs=tuple(pl.BlockSpec(memory_space=pltpu.VMEM) for _ in outs),
        scratch_shapes=[pltpu.VMEM(shape, dtype) for shape, dtype in scratch],
        compiler_params=pltpu.CompilerParams(vmem_limit_bytes=VMEM_BYTES),
        cost_estimate=pl.CostEstimate(flops=flops, bytes_accessed=1 << 20, transcendentals=0),
    )(*args)


def place_of():
    depth_at, row_at = lax.axis_index(GZ), lax.axis_index("gy")
    return (
        depth_at > 0,
        depth_at < lax.axis_size(GZ) - 1,
        row_at > 0,
        row_at < lax.axis_size("gy") - 1,
        lax.axis_index("c"),
        row_at,
    )


def row_edges(first, second, start, size):
    rule = lax.axis_index("gy") % 2 == 0
    one, two = (part[start : start + size].astype(F32) for part in (first, second))
    return jnp.where(rule, two, one).astype(BF16), jnp.where(rule, one, two).astype(BF16)


def half_lanes(tile, odd):
    tile = pltpu.roll(tile.astype(F32), 64, 1) if odd else tile.astype(F32)
    return jnp.where(lanes(tile.shape) < 64, tile, 0.0).astype(BF16)


def lanes(shape):
    return lax.broadcasted_iota(jnp.int32, shape, 1)


def at_column(tile, step):
    if step == 0:
        return tile
    moved = pltpu.roll(tile.astype(F32), (-step) % 128, 1)
    edge = 127 if step > 0 else 0
    return jnp.where(lanes(tile.shape) == edge, 0.0, moved).astype(BF16)


def put_shifts(shifts, row, layer, tile):
    for step in range(3):
        shifts[step, row : row + tile.shape[0], layer * 128 : layer * 128 + 128] = at_column(
            tile, step - 1
        )


def convolved(weights, shifts, rows, depth):
    windows = [
        shifts[step, rows[0] : rows[1], down * 128 : (down + depth) * 128]
        for down in range(3)
        for step in range(3)
    ]
    size = 9 * (rows[1] - rows[0])
    return jnp.dot(
        weights[:, :size], jnp.concatenate(windows, axis=0), preferred_element_type=F32
    )


def sigmoid(values):
    return 1.0 / (1.0 + jnp.exp(-values))


def slope(values):
    sig = sigmoid(values)
    return sig * (1.0 + values * (1.0 - sig))


def exact_dot(values, picks):
    high = values.astype(BF16)
    rest = values - high.astype(F32)
    middle = rest.astype(BF16)
    low = (rest - middle.astype(F32)).astype(BF16)
    total = jnp.dot(low, picks, preferred_element_type=F32)
    total = total + jnp.dot(middle, picks, preferred_element_type=F32)
    return total + jnp.dot(high, picks, preferred_element_type=F32)


def pair_columns(down):
    rows = lax.broadcasted_iota(jnp.int32, (128, 128), 0)
    columns = lax.broadcasted_iota(jnp.int32, (128, 128), 1)
    hit = (rows // 2 == columns) if down else (columns // 2 == rows)
    return jnp.where(hit, 0.125, 0.0).astype(BF16)


def pooled(first, second, channels, width):
    both = first + second
    blocks = both.shape[0] // (2 * channels)
    rows = []
    for block in range(blocks):
        start = 2 * block * channels
        rows.append(
            both[start : start + channels] + both[start + channels : start + 2 * channels]
        )
    summed = rows[0] if blocks == 1 else jnp.concatenate(rows, axis=0)
    mean = exact_dot(summed, pair_columns(True))
    return jnp.where(lanes(mean.shape) < width // 2, mean, 0.0)


def silu(values):
    return values * sigmoid(values)


def prepare(kernels, dims):
    def body(*refs):
        ins, outs, wide = refs[:4], refs[4:11], refs[11]
        for level, (rows, chans, feats) in enumerate(dims):
            source, taps = ins[level][...], outs[level]
            picks = (
                lax.broadcasted_iota(jnp.int32, (feats, 128), 0)
                == lax.broadcasted_iota(jnp.int32, (feats, 128), 1) % feats
            )
            spread = jnp.dot(
                source, jnp.where(picks, 1.0, 0.0).astype(BF16), preferred_element_type=F32
            )
            size = taps.shape[1]
            used = 9 * (rows + 2) * chans
            if used < size:
                wide[used:size, :] = jnp.zeros((size - used, 128), F32)
            place = lanes((chans, 128)) // feats
            for down in range(3):
                for step in range(3):
                    for row in range(rows + 2):
                        value = jnp.zeros((chans, 128), F32)
                        for across in range(3):
                            at = ((down * 3 + across) * 3 + step) * chans
                            value = jnp.where(
                                place == row - across, spread[at : at + chans], value
                            )
                        at = ((down * 3 + step) * (rows + 2) + row) * chans
                        wide[at : at + chans, :] = value
            taps[...] = wide[:size, :].T.astype(BF16)
        for level in range(1, 4):
            rows, chans, feats = dims[level]
            if level == 2:
                rows = 4
            source, taps = ins[level][...], outs[3 + level]
            size = (rows + 2) * feats
            picks = (
                lax.broadcasted_iota(jnp.int32, (feats, size), 0)
                == lax.broadcasted_iota(jnp.int32, (feats, size), 1) % feats
            )
            spread = jnp.dot(
                source, jnp.where(picks, 1.0, 0.0).astype(BF16), preferred_element_type=F32
            )
            place = lanes((chans, size)) // feats
            for down in range(3):
                for step in range(3):
                    for row in range(rows):
                        value = jnp.zeros((chans, size), F32)
                        for across in range(3):
                            at = (((2 - down) * 3 + 2 - across) * 3 + 2 - step) * chans
                            value = jnp.where(
                                place == row + across, spread[at : at + chans], value
                            )
                        at = (down * 3 + step) * size
                        taps[row * chans : (row + 1) * chans, at : at + size] = value.astype(BF16)

    shapes = [(128, 1536), (128, 896), (128, 1152), (128, 1792)]
    shapes += [(64, 1728), (128, 3456), (64, 3456)]
    flat = [kernel.reshape(-1, kernel.shape[-1]) for kernel in kernels]
    return call(body, [(s, BF16) for s in shapes], [((1792, 128), F32)], 1 << 27, *flat)


def forward_full(volume, halo_z, halo_y, weights, skip_half, skip_deep):
    def body(own, one, two, above, below, taps, skip1, skip3, pre, act, shifts, to_one, to_two):
        even = lax.axis_index("c") == 0
        for layer in range(10):
            if 0 < layer < 9:
                high, low = row_edges(above, below, layer * 16, 16)
                middle = own[layer - 1]
            else:
                near, far = (two, one) if layer == 0 else (one, two)
                at = (144, 0) if layer == 0 else (0, 144)
                yes, no = (row_edges(above, below, start, 16) for start in at)
                high, low = (jnp.where(even, yes[part], no[part]) for part in range(2))
                middle = jnp.where(even, near[0], far[0])
            parts = (high, middle, low)
            put_shifts(shifts, 0, layer, parts[0])
            put_shifts(shifts, 16, layer, parts[1])
            put_shifts(shifts, 144, layer, parts[2])
        value = convolved(taps, shifts, (0, 160), 8)
        active = silu(value)
        for layer in range(8):
            pre[layer] = value[:, layer * 128 : layer * 128 + 128]
        for layer in range(4):
            at = layer * 256
            act[layer] = pooled(
                active[:, at : at + 128], active[:, at + 128 : at + 256], 16, 128
            ).astype(BF16)
        for layer in range(3):
            rows = slice(layer * 64, layer * 64 + 64)
            to_one[rows] = jnp.where(even, act[layer + 1], act[layer])
            to_two[rows] = jnp.where(even, act[layer], act[layer + 1])
        to_one[192:320] = jnp.where(even, skip1[3], skip1[0])
        to_two[192:320] = jnp.where(even, skip1[0], skip1[3])
        to_one[320:] = skip3[...]
        to_two[320:] = skip3[...]

    outs = [((8, 128, 128), F32), ((4, 64, 128), BF16), ((3, 160, 1280), BF16)]
    outs += [((336, 128), BF16), ((336, 128), BF16)]
    return call(
        body, outs, [], 1 << 29, volume, *halo_z, *halo_y, weights, skip_half, skip_deep
    )


def forward_half(act, halo_z, halo_y, weights_half, weights_quarter):
    def body(
        own, one, two, above, below, taps, next_taps, pre, act, next_pre, deep, shifts, inner
    ):
        flags = place_of()
        even = flags[4] == 0
        def edge_at(place):
            found = row_edges(above, below, place // 2 * 48, 48)
            return [half_lanes(part, place % 2) for part in found]

        for layer in range(10):
            if 3 <= layer < 7:
                middle = own[layer - 3]
                edges = edge_at(layer)
            else:
                near, far = (two, one) if layer < 3 else (one, two)
                at = layer % 7 * 64
                middle = jnp.where(even, near[at : at + 64], far[at : at + 64])
                at = layer % 7
                yes, no = (edge_at(place) for place in ((7 + at, at) if layer < 3 else (at, 7 + at)))
                edges = [jnp.where(even, yes[part], no[part]) for part in range(2)]
            put_shifts(shifts, 0, layer, edges[0])
            put_shifts(shifts, 48, layer, middle)
            put_shifts(shifts, 112, layer, edges[1])
        for part in range(2):
            value = convolved(taps, shifts, (part * 64, part * 64 + 96), 8)
            for layer in range(8):
                pre[layer, part * 128 : part * 128 + 128, :] = value[
                    :, layer * 128 : layer * 128 + 128
                ]
        row = lax.broadcasted_iota(jnp.int32, (128, 128), 0) // 32
        inside = (row > 0) | (flags[2])
        inside = inside & ((row < 3) | (flags[3]))
        for layer in range(4):
            value = pooled(silu(pre[2 * layer]), silu(pre[2 * layer + 1]), 32, 64)
            keep = inside
            if layer == 0:
                keep = keep & (flags[0])
            if layer == 3:
                keep = keep & (flags[1])
            value = jnp.where(keep, value, 0.0).astype(BF16)
            act[layer] = value
            put_shifts(inner, 0, layer, value)
        value = convolved(next_taps, inner, (0, 128), 2)
        next_pre[0] = value[:, :128]
        next_pre[1] = value[:, 128:]
        coarse = pooled(silu(value[:, :128]), silu(value[:, 128:]), 64, 32)
        dense = coarse[:8].astype(BF16).astype(F32)
        for group in range(1, 8):
            part = coarse[group * 8 : group * 8 + 8].astype(BF16).astype(F32)
            dense = dense + pltpu.roll(part, group * 16, 1)
        deep[...] = dense

    outs = [
        ((8, 256, 128), F32),
        ((4, 128, 128), BF16),
        ((2, 128, 128), F32),
        ((8, 128), F32),
        ((3, 160, 1280), BF16),
    ]
    return call(
        body,
        outs,
        [((3, 128, 512), BF16)],
        1 << 29,
        act,
        *halo_z,
        *halo_y,
        weights_half,
        weights_quarter,
    )


def turned(tile, by):
    return tile if by % 128 == 0 else pltpu.roll(tile, by % 128, 1)


def near_cell(tile, layer_step, step):
    moved = turned(tile, -(16 * layer_step + step))
    column = lanes(tile.shape) % 16
    if step > 0:
        moved = jnp.where(column == 15, 0.0, moved)
    if step < 0:
        moved = jnp.where(column == 0, 0.0, moved)
    return moved.astype(BF16)


def columns_last(tile, start):
    width = tile.shape[0]
    column = lax.broadcasted_iota(jnp.int32, (width, 128), 0)
    picks = jnp.where(lanes((width, 128)) == column + start, 1.0, 0.0).astype(BF16)
    return lax.dot_general(tile, picks, (((0,), (0,)), ((), ())), preferred_element_type=F32)


def opened(dense, layer):
    parts = [turned(dense, 16 * layer - 16 * group) for group in range(8)]
    return jnp.concatenate(parts, axis=0)


def deepest(columns, acts, chips, skip_deep, halo_z, halo_y, skip, pre, weights, weights_back):
    def body(
        acts, chip_one, chip_two, skip_own, skip_one, skip_two, skip_above, skip_below, skip, pre,
        taps, taps_back, dense_out, out, shifts, delta_own, deltas,
    ):
        flags = place_of()
        core, row_at = flags[4], flags[5]
        place = lanes((64, 128)) // 16

        ahead = lax.axis_index("z") % 2 == 0

        def cells(position, row):
            at = position % 2 * columns + row
            if position // 2 == 1:
                return acts[at]
            if position // 2 == 0:
                return jnp.where(ahead, chip_two[at], chip_one[at])
            return jnp.where(ahead, chip_one[at], chip_two[at])

        for near in range(5):
            row = row_at + near - 2
            valid = (row >= 0) & (row < columns)
            row = jnp.clip(row, 0, columns - 1)
            value = jnp.zeros((64, 128), F32)
            for layer in range(5):
                dense = jnp.where(core == 0, cells(layer, row), cells(layer + 1, row))
                value = jnp.where(place == layer, opened(dense, layer), value)
            value = jnp.where(valid, value, 0.0)
            for down in range(3):
                for step in range(3):
                    shifts[down * 3 + step, near * 64 : near * 64 + 64, :] = near_cell(
                        value, down - 1, step - 1
                    )
        place = lanes((128, 128)) // 16
        for near in range(3):
            window = shifts[:, near * 64 : near * 64 + 192, :].reshape(1728, 128)
            value = jnp.dot(taps[:, :1728], window, preferred_element_type=F32)
            upstream = jnp.zeros((128, 128), F32)
            for layer in range(3):
                if near != 1:
                    yes = row_edges(skip_above, skip_below, 368 - layer * 16, 16)[near // 2]
                    no = row_edges(skip_above, skip_below, 336 + layer * 16, 16)[near // 2]
                    dense = jnp.where(core == 0, yes, no)
                elif layer == 1:
                    dense = skip_own[...]
                else:
                    ends = (skip_two, skip_one) if layer == 0 else (skip_one, skip_two)
                    dense = jnp.where(core == 0, ends[0][320:], ends[1][320:])
                upstream = upstream + columns_last(dense, 16 * layer + 16)
            keep = (place == 2) | ((place == 1) & (flags[0])) | ((place == 3) & (flags[1]))
            if near != 1:
                keep = keep & (flags[2 + near // 2])
            change = jnp.where(keep, upstream * slope(value), 0.0).astype(BF16).astype(F32)
            if near == 1:
                delta_own[...] = jnp.where(place == 2, change, 0.0).astype(BF16)
            deltas[near * 128 : near * 128 + 128, :] = change
        windows = [
            near_cell(deltas[...], down - 1, step - 1) for down in range(3) for step in range(3)
        ]
        carried = jnp.dot(
            taps_back[...], jnp.concatenate(windows, axis=0), preferred_element_type=F32
        )
        carried = exact_dot(turned(carried, -32), pair_columns(False))
        carried = jnp.concatenate([carried, carried], axis=0)
        dense = None
        for layer in range(2):
            wide = [columns_last(skip[layer, row], 0) for row in range(2)]
            change = (jnp.concatenate(wide, axis=0) + carried) * slope(pre[layer])
            change = jnp.where(lanes(change.shape) < 32, change, 0.0).astype(BF16)
            out[layer] = change
            change = change.astype(F32)
            dense = change if dense is None else dense + turned(change, 32)
        dense_out[0] = dense.astype(BF16)

    outs = [
        ((1, 128, 128), BF16),
        ((2, 128, 128), BF16),
        ((9, 320, 128), BF16),
        ((128, 128), BF16),
    ]
    scratch = [((384, 128), F32)]
    return call(
        body, outs, scratch, 1 << 28,
        acts, *chips, skip_deep, *halo_z, *halo_y, skip, pre, weights, weights_back,
    )


def grad_deepest(shifts, delta):
    def body(shifts, delta, grad):
        for tap in range(9):
            grad[tap * 192 : tap * 192 + 192, :] = lax.dot_general(
                shifts[tap, 64:256, :], delta[...], NT, preferred_element_type=F32
            )

    return call(body, [((1728, 128), F32)], [], 1 << 27, shifts, delta)[0]


def diagonal(product, rows, chans, feats):
    place = lanes((3 * chans, 128)) // feats
    value = product[: 3 * chans]
    for row in range(1, rows):
        value = jnp.where(place == row, product[row * chans : (row + 3) * chans], value)
    turn = 64
    while turn >= feats:
        value = value + pltpu.roll(value, turn, 1)
        turn //= 2
    return value


def packed(tall, groups):
    size = tall.shape[0] // groups
    place = lanes((size, 128)) // (128 // groups)
    value = tall[:size, :]
    for group in range(1, groups):
        value = jnp.where(place == group, tall[group * size : (group + 1) * size, :], value)
    return value


def put_grads(tall, shifts, rows, offset, depth, delta, dims):
    count, chans, feats = dims
    for down in range(3):
        for step in range(3):
            at = (offset + down) * 128
            product = lax.dot_general(
                shifts[step, rows[0] : rows[1], at : at + depth * 128],
                delta,
                NT,
                preferred_element_type=F32,
            )
            tap = (down * 3 + step) * 3 * chans
            tall[tap : tap + 3 * chans, :] = diagonal(product, count, chans, feats)


def grad_quarter_of(act, delta):
    def body(act, delta, grad, shifts, tall):
        for layer in range(4):
            put_shifts(shifts, 0, layer, act[layer])
        both = jnp.concatenate([delta[0], delta[1]], axis=1)
        put_grads(tall, shifts, (0, 128), 0, 2, both, (2, 32, 64))
        grad[...] = packed(tall, 2)

    scratch = [((3, 128, 512), BF16), ((864, 128), F32)]
    return call(body, [((432, 128), F32)], scratch, 1 << 28, act, delta)[0]


def back_rest(
    delta, halo_z, halo_y, skip_half, halo_zs, halo_ys, pre_half, skip_full, pre_full,
    weights_quarter, weights_half, shifts_half, shifts_full, deep_grad, quarter_grad,
):
    def body(
        own, one, two, above, below, skip1, one1, two1, above1, below1, pre1, skip0, pre0,
        taps2, taps1, shifts1, shifts0, grad3, grad2, out, moved2, moved1, delta1, delta0, tall, flat,
    ):
        flags = place_of()
        even = flags[4] == 0
        for layer in range(6):
            block = layer // 2
            high, low = row_edges(above, below, block // 2 * 128, 128)
            middle = own[0]
            if block != 1:
                near, far = (two, one) if block == 0 else (one, two)
                middle = jnp.where(even, near[0], far[0])
                other = row_edges(above, below, (2 - block) // 2 * 128, 128)
                high, low = jnp.where(even, other[0], high), jnp.where(even, other[1], low)
            tiles = (high, middle, low)
            for part, tile in enumerate(tiles):
                start = 64 if block == 1 and part != 1 else 0
                tile = turned(tile.astype(F32), -start - 32 * (layer % 2))
                tile = jnp.where(lanes(tile.shape) < 32, tile, 0.0).astype(BF16)
                put_shifts(moved2, part * 128, layer, tile)
        value = convolved(taps2, moved2, (0, 384), 4)

        def edge_at(place):
            found = row_edges(above1, below1, 240 + place // 2 * 32, 32)
            return [half_lanes(part, place % 2) for part in found]

        picks = pair_columns(False)
        row = lax.broadcasted_iota(jnp.int32, (192, 128), 0) // 32
        inside = lanes((192, 128)) < 64
        inside = inside & ((row > 0) | (flags[2])) & ((row < 5) | (flags[3]))
        for layer in range(6):
            if layer % 2 == 1 or layer == 0:
                at = (layer + 1) // 2 * 128
                carried = exact_dot(value[:, at : at + 128], picks)
                parts = [carried[part * 32 : part * 32 + 32] for part in (0, 1, 1, 2, 2, 3)]
                carried = jnp.concatenate(parts, axis=0)
            if 0 < layer < 5:
                high, low = edge_at(layer)
                middle = skip1[layer - 1]
            else:
                near, far = (two1, one1) if layer == 0 else (one1, two1)
                yes, no = edge_at(5 - layer), edge_at(layer)
                high, low = (jnp.where(even, yes[part], no[part]) for part in range(2))
                middle = jnp.where(even, near[192:320], far[192:320])
            parts = (high, middle, low)
            skip = jnp.concatenate(parts, axis=0).astype(F32)
            change = (skip + carried) * slope(pre1[layer + 1, 32:224])
            keep = inside
            if layer == 0:
                keep = keep & (flags[0])
            if layer == 5:
                keep = keep & (flags[1])
            change = jnp.where(keep, change, 0.0).astype(BF16)
            put_shifts(moved1, 0, layer, change)
            if 0 < layer < 5:
                delta1[:, (layer - 1) * 128 : layer * 128] = change[32:160]
        value = convolved(taps1, moved1, (0, 192), 4)
        for layer in range(8):
            if layer % 2 == 0:
                at = layer // 2 * 128
                carried = exact_dot(value[:, at : at + 128], picks)
                parts = [carried[part // 2 * 16 : part // 2 * 16 + 16] for part in range(8)]
                carried = jnp.concatenate(parts, axis=0)
            change = (skip0[layer].astype(F32) + carried) * slope(pre0[layer])
            delta0[:, layer * 128 : layer * 128 + 128] = change.astype(BF16)
        flat[:1728, :] = grad3[...]
        flat[1728:2160, :] = grad2[...]
        tall[...] = jnp.zeros_like(tall)
        put_grads(tall, shifts1, (32, 128), 2, 4, delta1[...], (4, 16, 32))
        flat[2160:2272, :] = packed(tall, 4)
        put_grads(tall, shifts0, (0, 160), 0, 8, delta0[...], (8, 16, 16))
        flat[2272:2328, :] = packed(tall, 8)
        flat[2328:, :] = jnp.zeros((2560 - 2328, 128), F32)
        for part in range(5):
            at = part * 512
            out[:, part * 128 : part * 128 + 128] = flat[at : at + 512, :].astype(BF16)

    scratch = [
        ((3, 384, 768), BF16),
        ((3, 192, 768), BF16),
        ((128, 512), BF16),
        ((128, 1024), BF16),
        ((448, 128), F32),
        ((2560, 128), F32),
    ]
    return call(
        body, [((512, 640), BF16)], scratch, 1 << 30,
        delta, *halo_z, *halo_y, skip_half, *halo_zs, *halo_ys, pre_half, skip_full, pre_full,
        weights_quarter, weights_half, shifts_half, shifts_full, deep_grad, quarter_grad,
    )[0]


def unpack(mine, other):
    def body(mine, other, full, half, quarter, eighth, whole, tall):
        even = lax.axis_index("c") == 0
        count, size = mine.shape[0], mine.shape[1]
        for at in range(count):
            own, partner = mine[at].astype(F32), other[at].astype(F32)
            for core in range(2):
                chunk = jnp.where(even, *((own, partner) if core == 0 else (partner, own)))
                for part in range(5):
                    row = part * 512 + (2 * at + core) * size
                    whole[row : row + size, :] = chunk[:, part * 128 : part * 128 + 128]

        def spread(out, source, chans):
            for down in range(3):
                for across in range(3):
                    for step in range(3):
                        at = ((down * 3 + across) * 3 + step) * chans
                        start = ((down * 3 + step) * 3 + across) * chans
                        out[at : at + chans, :] = source[
                            start : start + chans, : out.shape[1]
                        ]

        spread(eighth, whole, 64)
        for out, start, size, groups, chans in (
            (quarter, 1728, 432, 2, 32),
            (half, 2160, 112, 4, 16),
            (full, 2272, 56, 8, 16),
        ):
            dense = whole[start : start + size, :]
            for group in range(groups):
                tall[group * size : (group + 1) * size, :] = (
                    dense if group == 0 else pltpu.roll(dense, 128 - group * (128 // groups), 1)
                )
            spread(out, tall, chans)

    outs = [((432, 16), F32), ((432, 32), F32), ((864, 64), F32), ((1728, 128), F32)]
    scratch = [((2560, 128), F32), ((864, 128), F32)]
    return call(body, outs, scratch, 1 << 20, mine, other)


def pairs(axis):
    size = lax.axis_size(axis)
    between = [(i, i + 1) for i in range(1, size - 1, 2)]
    return [(i, i ^ 1) for i in range(size)], between + [(j, i) for i, j in between]


def swaps(to_one, to_two, axis=GZ):
    first, second = pairs(axis)
    return lax.ppermute(to_one, axis, first), lax.ppermute(to_two, axis, second)


def edge_rows(one, two, volume):
    def body(one, two, own, to_one, to_two):
        even = lax.axis_index("gy") % 2 == 0
        for place in range(10):
            block = one[0] if place == 0 else two[0] if place == 9 else own[place - 1]
            at = place * 16
            to_one[at : at + 16] = jnp.where(even, block[112:], block[:16])
            to_two[at : at + 16] = jnp.where(even, block[:16], block[112:])

    return call(body, [((160, 128), BF16)] * 2, [], 1 << 20, one, two, volume)


def edge_rows_half(one, two, act, skip_half, skip_deep):
    def body(one, two, act, skip1, skip3, to_one, to_two):
        even = lax.axis_index("gy") % 2 == 0

        def put(at, size, blocks):
            low, high = blocks
            packed_rows = []
            for rows in (slice(0, size), slice(low.shape[0] - size, low.shape[0])):
                packed_rows.append(
                    low[rows].astype(F32) + pltpu.roll(high[rows].astype(F32), 64, 1)
                )
            top, bottom = packed_rows
            to_one[at : at + size] = jnp.where(even, bottom, top).astype(BF16)
            to_two[at : at + size] = jnp.where(even, top, bottom).astype(BF16)

        def act_at(place):
            if 3 <= place < 7:
                return act[place - 3]
            at = place % 7 * 64
            return (one if place < 3 else two)[at : at + 64]

        def skip_at(place):
            if 0 < place < 5:
                return skip1[place - 1]
            return (one if place == 0 else two)[192:320]

        for pair in range(5):
            put(pair * 48, 48, (act_at(2 * pair), act_at(2 * pair + 1)))
        for pair in range(3):
            put(240 + pair * 32, 32, (skip_at(2 * pair), skip_at(2 * pair + 1)))
        for place, rows in enumerate((one[320:], skip3[...], two[320:])):
            at = 336 + place * 16
            to_one[at : at + 16] = rows
            to_two[at : at + 16] = rows

    return call(
        body, [((384, 128), BF16)] * 2, [], 1 << 20, one, two, act, skip_half, skip_deep
    )


def side_by_side(one, own, two):
    def body(one, own, two, out):
        moved = pltpu.roll(own[0].astype(F32), 64, 1)
        out[:128] = (one[0].astype(F32) + moved).astype(BF16)
        out[128:] = two[0]

    return call(body, [((256, 128), BF16)], [], 1 << 20, one, own, two)[0]


def laid_out(array):
    chans, depth, height, width = array.shape
    rows = jnp.transpose(array, (1, 2, 0, 3)).reshape(depth, height * chans, width)
    return jnp.pad(rows, ((0, 0), (0, 0), (0, 128 - width)))


def copies(part, count):
    def body(part, out):
        value = part[...].astype(BF16)
        for copy in range(count):
            out[copy] = value

    return call(body, [((count,) + part.shape, BF16)], [], 1 << 20, part)[0]


def summed(terms):
    inner, outer = ("x", "c"), ("z", "gy")
    first, second = lax.axis_size(inner), lax.axis_size(outer)
    rows, width = terms.shape[0] // first, terms.shape[1]
    pieces = lax.all_to_all(terms.reshape(first, rows, width), inner, 0, 0)
    part = jnp.sum(pieces.astype(F32), axis=0)
    pieces = lax.all_to_all(part, outer, 0, 0, tiled=True)
    done = jnp.sum(pieces.reshape(second, -1, width), axis=0)
    spread = jnp.broadcast_to(done[None], (second,) + done.shape).reshape(rows, width)
    part = lax.all_to_all(lax.optimization_barrier(spread), outer, 0, 0, tiled=True)
    mine = lax.all_to_all(copies(part, lax.axis_size("x")), "x", 0, 0)
    return mine, lax.ppermute(mine, "c", [(0, 1), (1, 0)])


def on_device(
    volume,
    kernel_full,
    kernel_half,
    kernel_quarter,
    kernel_eighth,
    skip_full,
    skip_half,
    skip_quarter,
    skip_eighth,
):
    kernels = (kernel_full, kernel_half, kernel_quarter, kernel_eighth)
    volume = laid_out(volume)
    even = lax.axis_index("c") == 0
    first, last = volume[:1], volume[7:]
    one, two = swaps(jnp.where(even, last, first), jnp.where(even, first, last))
    skip3 = jnp.transpose(skip_eighth, (1, 2, 3, 0)).reshape(16, 128)
    skip2 = jnp.transpose(skip_quarter, (1, 2, 3, 0))
    one, two, skip_full, skip_half, kernels = lax.optimization_barrier(
        (one, two, skip_full, skip_half, kernels)
    )
    skip0, skip1 = laid_out(skip_full), laid_out(skip_half)

    halo_y = swaps(*edge_rows(one, two, volume), "gy")
    dims = ((8, 16, 16), (4, 16, 32), (2, 32, 64), (1, 64, 128))
    w0, w1, w2, w3, t1, t2, t3 = prepare(kernels, dims)
    pre0, act1, shifts0, to_one, to_two = forward_full(
        volume, (one, two), halo_y, w0, skip1, skip3
    )
    halo_z1 = one, two = swaps(to_one, to_two)

    halo_y1 = swaps(*edge_rows_half(one, two, act1, skip1, skip3), "gy")
    pre1, act2, pre2, act3, shifts1 = forward_half(act1, halo_z1, halo_y1, w1, w2)
    columns = lax.axis_size("gy")
    many = (2 * columns,) + act3.shape
    acts = lax.all_to_all(
        lax.optimization_barrier(jnp.broadcast_to(act3[None], many)), ("c", "gy"), 0, 0
    )
    chips = swaps(acts, acts, ("x", "z"))
    dense2, delta2, shifts3, delta3 = deepest(
        columns, acts, chips, skip3, halo_z1, halo_y1, skip2, pre2, w3, t3
    )
    halo_z = one, two = swaps(dense2, dense2)
    block = side_by_side(one, dense2, two)
    halo_y = swaps(block, block, "gy")
    grad3 = grad_deepest(shifts3, delta3)
    grad2 = grad_quarter_of(act2, delta2)
    terms = back_rest(
        dense2, halo_z, halo_y, skip1, halo_z1, halo_y1, pre1, skip0, pre0,
        t2, t1, shifts1, shifts0, grad3, grad2,
    )
    outs = unpack(*summed(terms))
    return tuple(out.reshape(kernel.shape) for out, kernel in zip(outs, kernels))


def solution(mesh):
    fine = jax.sharding.Mesh(mesh.devices.reshape(4, 8, 2, 8), ("x", "z", "c", "gy"))
    return mapped(fine)


def mapped(fine):
    block = P(None, GZ, "gy", None)
    return jax.shard_map(
        on_device,
        mesh=fine,
        in_specs=(block, P(), P(), P(), P(), block, block, block, block),
        out_specs=(P(), P(), P(), P()),
        check_vma=False,
    )
```
